32 devices in a mesh: dp: 8 (over z, x), tensor: 4 (over y, core).
Axes of the slice: x: 2, y: 2, z: 4, core: 2. Of those that a mesh axis runs over, the one named last changes fastest.
Arguments:
- inputs: bfloat16 [32768, 768], P(('dp', 'tensor')), may hold values from -5.6 to 5.6
- lengths: int32 [32], P('dp'), may hold values from 256 to 1024, as said below
- groups: int32 [32, 32], replicated, may hold values from 0 to 1, as said below
- qkv_weight: float32 [3, 768, 768], P(None, 'dp', 'tensor'), may hold values from -0.21875 to 0.21875
- out_weight: float32 [768, 768], P('tensor', 'dp'), may hold values from -0.21875 to 0.21875
- up_weight: float32 [768, 3072], P('dp', 'tensor'), may hold values from -0.21875 to 0.21875
- down_weight: float32 [3072, 768], P('tensor', 'dp'), may hold values from -0.109375 to 0.109375
- col_bias: float32 [4, 1152], P('tensor', 'dp'), may hold values from -0.4 to 0.4
- row_params: float32 [6, 768], P(None, 'dp'), may hold values from -0.4 to 1.4
- qkv_first: float32 [3, 768, 768], P(None, 'dp', 'tensor'), may hold values from -0.56568545 to 0.56568545
- out_first: float32 [768, 768], P('tensor', 'dp'), may hold values from -0.56568545 to 0.56568545
- up_first: float32 [768, 3072], P('dp', 'tensor'), may hold values from -0.56568545 to 0.56568545
- down_first: float32 [3072, 768], P('tensor', 'dp'), may hold values from -0.56568545 to 0.56568545
- col_first: float32 [4, 1152], P('tensor', 'dp'), may hold values from -0.56568545 to 0.56568545
- row_first: float32 [6, 768], P(None, 'dp'), may hold values from -3.6769552 to 3.6769552
- qkv_second: float32 [3, 768, 768], P(None, 'dp', 'tensor'), may hold values from 0.0128 to 0.0512
- out_second: float32 [768, 768], P('tensor', 'dp'), may hold values from 0.0128 to 0.0512
- up_second: float32 [768, 3072], P('dp', 'tensor'), may hold values from 0.0128 to 0.0512
- down_second: float32 [3072, 768], P('tensor', 'dp'), may hold values from 0.0128 to 0.0512
- col_second: float32 [4, 1152], P('tensor', 'dp'), may hold values from 0.0128 to 0.0512
- row_second: float32 [6, 768], P(None, 'dp'), may hold values from 0.64 to 2.56
- qkv_ema: float32 [3, 768, 768], P(None, 'dp', 'tensor'), may hold values from -0.21875 to 0.21875
- out_ema: float32 [768, 768], P('tensor', 'dp'), may hold values from -0.21875 to 0.21875
- up_ema: float32 [768, 3072], P('dp', 'tensor'), may hold values from -0.21875 to 0.21875
- down_ema: float32 [3072, 768], P('tensor', 'dp'), may hold values from -0.109375 to 0.109375
- col_ema: float32 [4, 1152], P('tensor', 'dp'), may hold values from -0.4 to 0.4
- row_ema: float32 [6, 768], P(None, 'dp'), may hold values from -0.4 to 1.4
Outputs:
- outputs: bfloat16 [32768, 768], P(('dp', 'tensor'))
- input_grad: float32 [32768, 768], P(('dp', 'tensor'))
- qkv_first_new: float32 [3, 768, 768], P(None, 'dp', 'tensor')
- qkv_second_new: float32 [3, 768, 768], P(None, 'dp', 'tensor')
- qkv_weight_new: float32 [3, 768, 768], P(None, 'dp', 'tensor')
- qkv_ema_new: float32 [3, 768, 768], P(None, 'dp', 'tensor')
- out_first_new: float32 [768, 768], P('tensor', 'dp')
- out_second_new: float32 [768, 768], P('tensor', 'dp')
- out_weight_new: float32 [768, 768], P('tensor', 'dp')
- out_ema_new: float32 [768, 768], P('tensor', 'dp')
- up_first_new: float32 [768, 3072], P('dp', 'tensor')
- up_second_new: float32 [768, 3072], P('dp', 'tensor')
- up_weight_new: float32 [768, 3072], P('dp', 'tensor')
- up_ema_new: float32 [768, 3072], P('dp', 'tensor')
- down_first_new: float32 [3072, 768], P('tensor', 'dp')
- down_second_new: float32 [3072, 768], P('tensor', 'dp')
- down_weight_new: float32 [3072, 768], P('tensor', 'dp')
- down_ema_new: float32 [3072, 768], P('tensor', 'dp')
- col_first_new: float32 [4, 1152], P('tensor', 'dp')
- col_second_new: float32 [4, 1152], P('tensor', 'dp')
- col_bias_new: float32 [4, 1152], P('tensor', 'dp')
- col_ema_new: float32 [4, 1152], P('tensor', 'dp')
- row_first_new: float32 [6, 768], P(None, 'dp')
- row_second_new: float32 [6, 768], P(None, 'dp')
- row_params_new: float32 [6, 768], P(None, 'dp')
- row_ema_new: float32 [6, 768], P(None, 'dp')
The draws below stay inside these ranges and needn't reach their ends.
Inputs may be any that keep to these rules, and one draw needn't show every extreme that they name: The last 1024 - lengths[s] rows of sequence s are padding; some sequence has none. `groups`: each row has 1 to 6 ones, none on the diagonal; some row has 6.
All inputs are finite; a program needn't handle non-finite values.
Results may differ from the reference program's by a relative error of at most 0.0055.
The reference program's roundings to bfloat16 on the way count: a program that leaves them out, or rounds other values in their place, can miss the bound.
Values may be sent and summed in bfloat16 or wider, within the bound.
A program may use at most 192 MiB of HBM per device.

```python
import math
import jax
import jax.numpy as jnp
from jax import lax

D = 768
H = 12
HD = 64
FF = 3072
LEN = 1024
STEP = 5
NSEQ = 32
TOKENS = 32768
CB = 1152
N_TENSOR = 4


def draw_inputs(key, part):
    key = jax.random.fold_in(key, 11)
    base_key, jitter_key = jax.random.split(key)
    offsets = 0.8 * jax.random.truncated_normal(base_key, -4.0, 4.0, (NSEQ, 1, LEN * 0 + D), jnp.float32)
    jitter = 0.6 * jax.random.truncated_normal(jitter_key, -4.0, 4.0, (NSEQ, LEN, D), jnp.float32)
    return (offsets + jitter).reshape(TOKENS, D).astype(jnp.bfloat16)


def draw_lengths(key, part):
    key = jax.random.fold_in(key, 12)
    first_key, second_key = jax.random.split(key)
    sampled = jax.random.randint(first_key, (NSEQ,), LEN // 4, LEN + 1)
    longest = jax.random.randint(second_key, (), 0, NSEQ)
    return jnp.where(jnp.arange(NSEQ) == longest, LEN, sampled).astype(jnp.int32)


def draw_groups(key, part):
    key = jax.random.fold_in(key, 13)
    count_key, order_key, full_key = jax.random.split(key, 3)
    counts = jax.random.randint(count_key, (NSEQ,), 1, 7)
    fullest = jax.random.randint(full_key, (), 0, NSEQ)
    counts = jnp.where(jnp.arange(NSEQ) == fullest, 6, counts)
    row_keys = jax.random.split(order_key, NSEQ)
    offsets = jax.vmap(lambda row_key: jax.random.permutation(row_key, NSEQ - 1)[:6] + 1)(row_keys)
    rows_index = jnp.arange(NSEQ)
    partners = (rows_index[:, None] + offsets) % NSEQ
    chosen = (jnp.arange(6)[None, :] < counts[:, None]).astype(jnp.int32)
    members = jnp.zeros((NSEQ, NSEQ), jnp.int32)
    return members.at[rows_index[:, None], partners].add(chosen)


def row_values(key):
    gain_key, shift_key = jax.random.split(key)
    gains = 1.0 + 0.1 * jax.random.truncated_normal(gain_key, -4.0, 4.0, (6, D), jnp.float32)
    shifts = 0.1 * jax.random.truncated_normal(shift_key, -4.0, 4.0, (6, D), jnp.float32)
    is_gain = ((jnp.arange(6) == 1) | (jnp.arange(6) == 4))[:, None]
    return jnp.where(is_gain, gains, shifts)


def draw_row_params(key, part):
    key = jax.random.fold_in(key, 14)
    return row_values(key)


def draw_row_ema(key, part):
    key = jax.random.fold_in(key, 15)
    return row_values(key)


def levels(rng, extent, cuts, low, largest):
    def one(position, parts):
        draws = jax.random.uniform(jax.random.fold_in(jax.random.fold_in(rng, 6), position), (parts,), jnp.float32, low / len(cuts), largest / len(cuts))
        return jnp.repeat(jnp.exp(draws), extent[position] // parts).reshape((-1,) + (1,) * (len(extent) - position - 1))

    factor_of = one(*cuts[0])
    for cut in cuts[1:]:
        factor_of = factor_of * one(*cut)
    return factor_of


def gaussian(key, extent, scale, reach, cuts=(), kind=jnp.bfloat16):
    entries = jax.random.normal(key, extent, jnp.float32) * scale
    if len(cuts) > 0:
        entries = levels(key, extent, cuts, -0.22, 0.18) * entries
    return jnp.clip(entries, min=-reach, max=reach).astype(kind)


def setup_inputs(seed: int = 0) -> dict:
    key_of = jax.random.split(jax.random.key(seed), 28)
    inputs = draw_inputs(jax.random.fold_in(key_of[27], 71), 0)
    lengths = draw_lengths(jax.random.fold_in(key_of[27], 71), 0)
    groups = draw_groups(jax.random.fold_in(key_of[27], 71), 0)
    qkv_weight = gaussian(key_of[3], (3, D, D), D ** -0.5, 0.21875, ((1, 8), (2, 4)), jnp.float32)
    out_weight = gaussian(key_of[4], (D, D), D ** -0.5, 0.21875, ((0, 4), (1, 8)), jnp.float32)
    up_weight = gaussian(key_of[5], (D, FF), D ** -0.5, 0.21875, ((0, 8), (1, 4)), jnp.float32)
    down_weight = gaussian(key_of[6], (FF, D), FF ** -0.5, 0.109375, ((0, 4), (1, 8)), jnp.float32)
    col_bias = gaussian(key_of[7], (N_TENSOR, CB), 0.1, 0.4, ((0, 4), (1, 8)), jnp.float32)
    row_params = draw_row_params(jax.random.fold_in(key_of[27], 71), 0)
    qkv_first = gaussian(key_of[9], (3, D, D), (0.02 * NSEQ ** 0.5), 0.56568545, ((1, 8), (2, 4)), jnp.float32)
    out_first = gaussian(key_of[10], (D, D), (0.02 * NSEQ ** 0.5), 0.56568545, ((0, 4), (1, 8)), jnp.float32)
    up_first = gaussian(key_of[11], (D, FF), (0.02 * NSEQ ** 0.5), 0.56568545, ((0, 8), (1, 4)), jnp.float32)
    down_first = gaussian(key_of[12], (FF, D), (0.02 * NSEQ ** 0.5), 0.56568545, ((0, 4), (1, 8)), jnp.float32)
    col_first = gaussian(key_of[13], (N_TENSOR, CB), (0.02 * NSEQ ** 0.5), 0.56568545, ((0, 4), (1, 8)), jnp.float32)
    row_first = gaussian(key_of[14], (6, D), (0.13 * NSEQ ** 0.5), 3.6769552, ((1, 8),), jnp.float32)
    qkv_second = jnp.clip(jnp.exp(math.log(0.0512) - 1.3862944 * jax.random.uniform(key_of[15], (3, D, D), jnp.float32) ** levels(key_of[15], (3, D, D), ((1, 8), (2, 4)), -0.2, 0.2)), 0.0128, 0.0512)
    out_second = jnp.clip(jnp.exp(math.log(0.0512) - 1.3862944 * jax.random.uniform(key_of[16], (D, D), jnp.float32) ** levels(key_of[16], (D, D), ((0, 4), (1, 8)), -0.2, 0.2)), 0.0128, 0.0512)
    up_second = jnp.clip(jnp.exp(math.log(0.0512) - 1.3862944 * jax.random.uniform(key_of[17], (D, FF), jnp.float32) ** levels(key_of[17], (D, FF), ((0, 8), (1, 4)), -0.2, 0.2)), 0.0128, 0.0512)
    down_second = jnp.clip(jnp.exp(math.log(0.0512) - 1.3862944 * jax.random.uniform(key_of[18], (FF, D), jnp.float32) ** levels(key_of[18], (FF, D), ((0, 4), (1, 8)), -0.2, 0.2)), 0.0128, 0.0512)
    col_second = jnp.clip(jnp.exp(math.log(0.0512) - 1.3862944 * jax.random.uniform(key_of[19], (N_TENSOR, CB), jnp.float32) ** levels(key_of[19], (N_TENSOR, CB), ((0, 4), (1, 8)), -0.2, 0.2)), 0.0128, 0.0512)
    row_second = jnp.clip(jnp.exp(math.log(2.56) - 1.3862944 * jax.random.uniform(key_of[20], (6, D), jnp.float32) ** levels(key_of[20], (6, D), ((1, 8),), -0.2, 0.2)), 0.64, 2.56)
    qkv_ema = gaussian(key_of[21], (3, D, D), D ** -0.5, 0.21875, ((1, 8), (2, 4)), jnp.float32)
    out_ema = gaussian(key_of[22], (D, D), D ** -0.5, 0.21875, ((0, 4), (1, 8)), jnp.float32)
    up_ema = gaussian(key_of[23], (D, FF), D ** -0.5, 0.21875, ((0, 8), (1, 4)), jnp.float32)
    down_ema = gaussian(key_of[24], (FF, D), FF ** -0.5, 0.109375, ((0, 4), (1, 8)), jnp.float32)
    col_ema = gaussian(key_of[25], (N_TENSOR, CB), 0.1, 0.4, ((0, 4), (1, 8)), jnp.float32)
    row_ema = draw_row_ema(jax.random.fold_in(key_of[27], 71), 0)
    return dict(inputs=inputs, lengths=lengths, groups=groups, qkv_weight=qkv_weight, out_weight=out_weight, up_weight=up_weight, down_weight=down_weight, col_bias=col_bias, row_params=row_params, qkv_first=qkv_first, out_first=out_first, up_first=up_first, down_first=down_first, col_first=col_first, row_first=row_first, qkv_second=qkv_second, out_second=out_second, up_second=up_second, down_second=down_second, col_second=col_second, row_second=row_second, qkv_ema=qkv_ema, out_ema=out_ema, up_ema=up_ema, down_ema=down_ema, col_ema=col_ema, row_ema=row_ema)


@jax.custom_vjp
def low(v):
    return lax.optimization_barrier(v.astype(jnp.bfloat16)).astype(jnp.float32)

@jax.custom_vjp
def low_back(v):
    return v

def low_keep(v):
    return (low(v), None)

def low_pass(kept, grad):
    return (grad,)

def back_keep(v):
    return (v, None)

def back_low(kept, grad):
    return (low(grad),)
low.defvjp(low_keep, low_pass)
low_back.defvjp(back_keep, back_low)
highest = lax.Precision.HIGHEST
eps_norm = 1e-05
temper = 40.0
masked = -1000000000.0
beta_one = 0.5
beta_two = 0.5
adam_eps = 1e-08
decay_rate = 0.01
ema_keep = 0.9

def matmul(left, right):
    return jnp.dot(left, right, precision=highest, preferred_element_type=jnp.float32)

def round_both(values):
    return low(low_back(values))

def layer_norm(seq_rows, gain_row, shift_row):
    row_mean = lax.optimization_barrier(jnp.mean(seq_rows, axis=-1, keepdims=True))
    centred = seq_rows - row_mean
    variance = lax.optimization_barrier(jnp.mean(centred * centred, axis=-1, keepdims=True))
    return centred * lax.rsqrt(variance + eps_norm) * gain_row + shift_row

def contrast_loss(pooled, groups):
    inverse_norm = lax.rsqrt(lax.optimization_barrier(jnp.sum(pooled * pooled, axis=1, keepdims=True)) + eps_norm)
    unit_rows = pooled * inverse_norm
    similar = temper * jnp.dot(unit_rows, unit_rows.T, precision=highest)
    diagonal = jnp.eye(NSEQ, dtype=bool)
    others = jnp.where(diagonal, masked, similar)
    spread = jax.nn.logsumexp(others, axis=1)
    members = groups.astype(jnp.float32)
    positive = lax.optimization_barrier(jnp.sum(members * similar, axis=1)) / lax.optimization_barrier(jnp.sum(members, axis=1))
    return jnp.sum(spread - positive)

def one_sequence(seq_rows, length, params):
    wq, wk, wv, wo, w_up, w_down, query_bias, value_bias, hidden_bias, row_vals = params
    queries = round_both(matmul(seq_rows, wq) + query_bias)
    keys_all = round_both(matmul(seq_rows, wk))
    values = round_both(matmul(seq_rows, wv) + value_bias)
    heads_q = queries.reshape(LEN, H, HD)
    heads_k = keys_all.reshape(LEN, H, HD)
    heads_v = values.reshape(LEN, H, HD)
    raw_scores = jnp.einsum('qhd,khd->hqk', heads_q, heads_k, precision=highest) * HD ** (-0.5)
    positions = jnp.arange(LEN)
    key_bias = jnp.where(positions < length, 0.0, masked)
    soft_probs = jax.nn.softmax(low_back(raw_scores) + key_bias[None, None, :], axis=-1)
    context = jnp.einsum('hqk,khd->qhd', low(soft_probs), heads_v, precision=highest)
    context = round_both(context.reshape(LEN, D))
    branch = low_back(matmul(context, wo) + row_vals[0])
    first = layer_norm(seq_rows + branch, row_vals[1], row_vals[2])
    hidden = low_back(matmul(low(first), w_up) + hidden_bias)
    active = low(jax.nn.gelu(hidden, approximate=False))
    second = low_back(matmul(active, w_down) + row_vals[3])
    output = layer_norm(first + second, row_vals[4], row_vals[5])
    token_weights = (positions < length).astype(jnp.float32)
    pooled = lax.optimization_barrier(jnp.sum(output * token_weights[:, None], axis=0)) / length.astype(jnp.float32)
    return (output, pooled)

def adam_update(weight, first_old, second, ema_old, gradient, step_rate):
    first_new = beta_one * first_old + (1 - beta_one) * gradient
    second_new = beta_two * second + (1 - beta_two) * gradient * gradient
    first_hat = first_new / (1 - beta_one ** STEP)
    second_hat = second_new / (1 - beta_two ** STEP)
    weight_new = weight - step_rate * (first_hat / (jnp.sqrt(second_hat) + adam_eps) + decay_rate * weight)
    ema_new = ema_keep * ema_old + (1 - ema_keep) * weight_new
    return (first_new, second_new, weight_new, ema_new)

def reference(inputs, lengths, groups, qkv_weight, out_weight, up_weight, down_weight, col_bias, row_params, qkv_first, out_first, up_first, down_first, col_first, row_first, qkv_second, out_second, up_second, down_second, col_second, row_second, qkv_ema, out_ema, up_ema, down_ema, col_ema, row_ema):
    head_cols = D // N_TENSOR

    def full_forward(rows_all, qkv_w, out_w, up_w, down_w, col_w, row_w):
        col_values = low(col_w)
        params = (low(qkv_w[0]), low(qkv_w[1]), low(qkv_w[2]), low(out_w), low(up_w), low(down_w), col_values[:, :head_cols].reshape(D), col_values[:, head_cols:2 * head_cols].reshape(D), col_values[:, 2 * head_cols:].reshape(FF), low(row_w))
        step_fn = jax.checkpoint(lambda pair: one_sequence(pair[0], pair[1], params))
        outputs, pooled = lax.map(step_fn, (rows_all.reshape(NSEQ, LEN, D), lengths))
        return (contrast_loss(pooled, groups), outputs.reshape(TOKENS, D))
    loss_value, pull_back, outputs = jax.vjp(full_forward, inputs.astype(jnp.float32), qkv_weight, out_weight, up_weight, down_weight, col_bias, row_params, has_aux=True)
    gradients = pull_back(jnp.ones_like(loss_value))
    input_grad = gradients[0]
    qkv_new = adam_update(qkv_weight, qkv_first, qkv_second, qkv_ema, gradients[1], D ** (-0.5))
    out_new = adam_update(out_weight, out_first, out_second, out_ema, gradients[2], D ** (-0.5))
    up_new = adam_update(up_weight, up_first, up_second, up_ema, gradients[3], D ** (-0.5))
    down_new = adam_update(down_weight, down_first, down_second, down_ema, gradients[4], FF ** (-0.5))
    col_new = adam_update(col_bias, col_first, col_second, col_ema, gradients[5], 0.1)
    row_new = adam_update(row_params, row_first, row_second, row_ema, gradients[6], 0.15)
    return (outputs.astype(jnp.bfloat16), input_grad, qkv_new[0], qkv_new[1], qkv_new[2], qkv_new[3], out_new[0], out_new[1], out_new[2], out_new[3], up_new[0], up_new[1], up_new[2], up_new[3], down_new[0], down_new[1], down_new[2], down_new[3], col_new[0], col_new[1], col_new[2], col_new[3], row_new[0], row_new[1], row_new[2], row_new[3])
```

```python
import functools

import jax
import jax.numpy as jnp
from jax import lax
from jax.experimental import pallas as pl
from jax.experimental.pallas import tpu as pltpu
from jax.sharding import PartitionSpec as P

D = 768
H = 12
HD = 64
FF = 3072
LEN = 1024
STEP = 5
NT = 4
HC = D // NT
AUG = 80

MESH = pl.DeviceIdType.MESH
f32 = jnp.float32
bf16 = jnp.bfloat16
highest = lax.Precision.HIGHEST
eps_norm = 1e-05
temper = 40.0
masked = -1000000000.0
beta_one = 0.5
beta_two = 0.5
adam_eps = 1e-08
decay_rate = 0.01
ema_keep = 0.9
VMEM_CAP = 60 << 20


def nn(a, b):
    return jnp.dot(a, b, preferred_element_type=f32)


def nt(a, b):
    return lax.dot_general(a, b, (((1,), (1,)), ((), ())), preferred_element_type=f32)


def tn(a, b):
    return lax.dot_general(a, b, (((0,), (0,)), ((), ())), preferred_element_type=f32)


def contrast_loss(pooled, groups):
    inverse_norm = lax.rsqrt(jnp.sum(pooled * pooled, axis=1, keepdims=True) + eps_norm)
    unit_rows = pooled * inverse_norm
    similar = temper * jnp.dot(unit_rows, unit_rows.T, precision=highest)
    diagonal = jnp.eye(pooled.shape[0], dtype=bool)
    others = jnp.where(diagonal, masked, similar)
    spread = jax.nn.logsumexp(others, axis=1)
    members = groups.astype(jnp.float32)
    positive = jnp.sum(members * similar, axis=1) / jnp.sum(members, axis=1)
    return jnp.sum(spread - positive)


def adam_update(weight, first_old, second, ema_old, gradient, step_rate):
    first_new = beta_one * first_old + (1 - beta_one) * gradient
    second_new = beta_two * second + (1 - beta_two) * gradient * gradient
    first_hat = first_new / (1 - beta_one**STEP)
    second_hat = second_new / (1 - beta_two**STEP)
    weight_new = weight - step_rate * (
        first_hat / (jnp.sqrt(second_hat) + adam_eps) + decay_rate * weight
    )
    ema_new = ema_keep * ema_old + (1 - ema_keep) * weight_new
    return (first_new, second_new, weight_new, ema_new)


class Place:
    def __init__(self, depth):
        dp = lax.axis_index("dp")
        t = lax.axis_index("tensor")
        self.depth = depth
        self.z, self.x, self.y, self.c = dp // 2, dp % 2, t // 2, t % 2
        self.me = (self.z, self.x, self.y, self.c)
        self.over_x = (self.z, 1 - self.x, self.y, self.c)
        self.over_y = (self.z, self.x, 1 - self.y, self.c)
        self.over_xy = (self.z, 1 - self.x, 1 - self.y, self.c)
        self.over_c = (self.z, self.x, self.y, 1 - self.c)

    def along_z(self, k):
        return ((self.z + k) % self.depth, self.x, self.y, self.c)


def device(place):
    z, x, y, c = place
    return (z * 2 + x, y * 2 + c)


def enter(p):
    bar = pltpu.get_barrier_semaphore()
    to = [p.over_x, p.over_y, p.over_c] + [p.along_z(k) for k in range(1, p.depth)]
    for place in to:
        pl.semaphore_signal(bar, inc=1, device_id=device(place), device_id_type=MESH)
    pl.semaphore_wait(bar, len(to))


def remote(src, dst, send, recv, to):
    return pltpu.make_async_remote_copy(
        src_ref=src, dst_ref=dst, send_sem=send, recv_sem=recv, device_id=device(to), device_id_type=MESH
    )


class Gather:
    def __init__(self, p, part, own, full, sems):
        self.p, self.part, self.rows, self.own, self.full = p, part, own.shape[0], own, full
        self.recv, self.sz, self.sx, self.sy, self.sc = sems
        self.sent = []

    def spot(self, place, half=None):
        z, x, y, c = place
        r = self.rows
        step = 32 // self.full.dtype.itemsize
        start = (z * 2 + x) * r
        if half is not None:
            start, r = start + half * (r // 2), r // 2
        return self.full.at[y * 2 + c, pl.ds(pl.multiple_of(start, step), r), :]

    def copy(self, src, place, half, to, send):
        z, x, y, c = place
        dst = self.spot(place, half)
        recv = self.recv.at[self.part, (z * 2 + x) * 4 + y * 2 + c, half or 0]
        return remote(dst if src is None else src, dst, send, recv, to)

    def send(self, src, place, half, to, send):
        def make():
            return self.copy(src, place(), half, to(), send())

        make().start()
        self.sent.append(make)

    def arrived(self, place, half=None):
        self.copy(None, place, half, self.p.over_c, self.sc.at[self.part, 0]).wait_recv()

    def line_place(self, k, base=None):
        z, x, y, c = base or self.p.me
        return ((self.p.z + k) % self.p.depth, x, y, c)

    def start(self):
        p, q = self.p, self.part
        for k in range(1, p.depth):
            self.send(self.own, lambda: p.me, None, lambda k=k: p.along_z(k), lambda k=k: self.sz.at[q, k])
        self.send(self.own, lambda: p.me, None, lambda: p.over_x, lambda: self.sx.at[q, 0, 0])
        self.send(self.own, lambda: p.me, None, lambda: p.over_y, lambda: self.sy.at[q, 0, 0])
        self.send(self.own, lambda: p.me, None, lambda: p.over_c, lambda: self.sc.at[q, 0])

    def local(self, sem):
        return pltpu.make_async_copy(self.own, self.spot(self.p.me), sem.at[self.part])

    def line(self, k):
        p, q = self.p, self.part
        place = functools.partial(self.line_place, k)
        self.arrived(place())
        self.send(None, place, None, lambda: p.over_x, lambda: self.sx.at[q, 0, k])
        self.send(None, place, None, lambda: p.over_y, lambda: self.sy.at[q, 0, k])
        self.send(None, place, None, lambda: p.over_c, lambda: self.sc.at[q, k])

    def cross(self, k):
        p, q, n = self.p, self.part, self.p.depth
        for way, (base, to, sem) in enumerate(((p.over_x, p.over_y, self.sy), (p.over_y, p.over_x, self.sx))):
            place = functools.partial(self.line_place, k, base)
            self.arrived(place())
            self.send(None, place, way, lambda to=to: to, lambda sem=sem: sem.at[q, 1, k])
            self.send(None, place, None, lambda: p.over_c, lambda way=way: self.sc.at[q, (1 + way) * n + k])

    def corner(self, k):
        p, q, n = self.p, self.part, self.p.depth
        place = functools.partial(self.line_place, k, p.over_xy)
        self.arrived(place(), 0)
        self.arrived(place(), 1)
        self.send(None, place, None, lambda: p.over_c, lambda: self.sc.at[q, 3 * n + k])

    def other_core(self):
        p = self.p
        for k in range(p.depth):
            for x in range(2):
                for y in range(2):
                    self.arrived(((p.z + k) % p.depth, x, y, 1 - p.c))

    def flow(self):
        n = self.p.depth
        steps = [functools.partial(self.cross, 0)]
        for k in ([1, n - 1] + list(range(2, n - 1))) if n > 2 else range(1, n):
            steps.append(functools.partial(self.line, k))
            steps.append(functools.partial(self.cross, k))
        steps += [functools.partial(self.corner, k) for k in range(n)]
        steps.append(self.other_core)
        return steps

    def finish(self):
        for make in self.sent:
            make().wait_send()


def gather_sems(parts, n):
    dma = pltpu.SemaphoreType.DMA
    return [dma((parts, 8 * n, 2)), dma((parts, n)), dma((parts, 2, n)), dma((parts, 2, n)), dma((parts, 4 * n))]


def gather_kernel(n, *refs):
    own, full = refs[0], refs[1]
    sems, local = refs[2:7], refs[7]
    p = Place(n)
    enter(p)
    g = Gather(p, 0, own, full, sems)
    g.start()
    g.local(local).start()
    for step in g.flow():
        step()
    g.finish()
    g.local(local).wait()


def gather_one(own, n, ident):
    return pl.pallas_call(
        functools.partial(gather_kernel, n),
        out_shape=jax.ShapeDtypeStruct((4, 2 * n * own.shape[0], own.shape[1]), own.dtype),
        in_specs=[pl.BlockSpec(memory_space=pl.ANY)],
        out_specs=pl.BlockSpec(memory_space=pl.ANY),
        scratch_shapes=gather_sems(1, n) + [pltpu.SemaphoreType.DMA((1,))],
        compiler_params=pltpu.CompilerParams(collective_id=ident, has_side_effects=True),
    )(own)


class Scatter:
    def __init__(self, p, part, rows, source, slab, out, bufs, sems):
        self.p, self.part, self.rows, self.source, self.slab, self.out = p, part, rows, source, slab, out
        self.b_core, self.b_corner, self.b_cross, self.b_line = bufs
        self.ss, self.rs, self.sc, self.rc, self.sx, self.rx, self.sl, self.rl = sems
        self.sent = []

    def span(self, z, x, half=None):
        r = self.rows
        start = (z * 2 + x) * r
        if half is not None:
            start, r = start + half * (r // 2), r // 2
        return pl.ds(pl.multiple_of(start, 16), r)

    def go(self, make, *args):
        make(*args).start()
        self.sent.append(functools.partial(make, *args))

    def core_copy(self, y):
        p, q = self.p, self.part
        return remote(self.source(y * 2 + 1 - p.c), self.b_core.at[y], self.ss.at[q, y], self.rs.at[q, y], p.over_c)

    def core(self):
        for y in range(2):
            self.go(self.core_copy, y)

    def corner_copy(self, z, half):
        p, q = self.p, self.part
        src = self.slab(1 - p.y).at[self.span(z, 1 - p.x, half), :]
        to = p.over_x if half else p.over_y
        return remote(src, self.b_corner.at[half, z], self.sc.at[q, half, z], self.rc.at[q, half, z], to)

    def corner(self):
        r = self.rows
        for y in range(2):
            self.core_copy(y).wait_recv()
            slab = self.slab(y)

            def add(i, _, y=y, slab=slab):
                s = pl.ds(pl.multiple_of(i * r, 16), r)
                slab[s, :] = (slab[s, :].astype(f32) + self.b_core[y, s, :].astype(f32)).astype(bf16)
                return 0

            lax.fori_loop(0, 2 * self.p.depth, add, 0)
        for z in range(self.p.depth):
            for half in range(2):
                self.go(self.corner_copy, z, half)

    def cross_copy(self, z, way):
        p, q = self.p, self.part
        src = self.slab(1 - p.y).at[self.span(z, p.x), :] if way else self.slab(p.y).at[self.span(z, 1 - p.x), :]
        to = p.over_y if way else p.over_x
        return remote(src, self.b_cross.at[way, z], self.sx.at[q, way, z], self.rx.at[q, way, z], to)

    def cross(self):
        p = self.p
        for z in range(p.depth):
            for way in range(2):
                self.corner_copy(z, way).wait_recv()
                slab, s = (self.slab(1 - p.y), self.span(z, p.x, 1)) if way else (self.slab(p.y), self.span(z, 1 - p.x, 0))
                slab[s, :] = (slab[s, :].astype(f32) + self.b_corner[way, z].astype(f32)).astype(bf16)
                self.go(self.cross_copy, z, way)

    def line_copy(self, k):
        p, q = self.p, self.part
        z = (p.z + k) % p.depth
        return remote(self.slab(p.y).at[self.span(z, p.x), :], self.b_line.at[k], self.sl.at[q, k], self.rl.at[q, k], p.along_z(k))

    def column(self, z):
        p = self.p
        for way in range(2):
            self.cross_copy(z, way).wait_recv()
        return self.slab(p.y)[self.span(z, p.x), :].astype(f32) + self.b_cross[0, z].astype(f32) + self.b_cross[1, z].astype(f32)

    def line(self):
        p = self.p
        for k in range(1, p.depth):
            z = (p.z + k) % p.depth
            self.slab(p.y)[self.span(z, p.x), :] = self.column(z).astype(bf16)
            self.go(self.line_copy, k)

    def last(self):
        p = self.p
        total = self.column(p.z)
        for k in range(1, p.depth):
            self.line_copy(k).wait_recv()
            total = total + self.b_line[k].astype(f32)
        self.out[...] = total

    def finish(self):
        for make in self.sent:
            make().wait_send()


def scatter_bufs(n, rows, width):
    return [
        pltpu.VMEM((2, 2 * n * rows, width), bf16), pltpu.VMEM((2, n, rows // 2, width), bf16),
        pltpu.VMEM((2, n, rows, width), bf16), pltpu.VMEM((n, rows, width), bf16),
    ]


def scatter_sems(parts, n):
    dma = pltpu.SemaphoreType.DMA
    return [dma((parts, 2))] * 2 + [dma((parts, 2, n))] * 4 + [dma((parts, n))] * 2


def split3(row):
    hi = row.astype(bf16).astype(f32)
    mid = (row - hi).astype(bf16).astype(f32)
    return hi, mid, row - hi - mid


def aug_rows(*rows):
    width = rows[0].shape[1]
    at = lax.broadcasted_iota(jnp.int32, (16, width), 0)
    out = jnp.zeros((16, width), f32)
    for i, row in enumerate(rows):
        out = jnp.where(at == i, row, out)
    return out.astype(bf16)


def norm(r):
    cent = r - jnp.mean(r, axis=1, keepdims=True)
    rstd = lax.rsqrt(jnp.mean(cent * cent, axis=1, keepdims=True) + eps_norm)
    return cent * rstd, rstd


def any_spec(n):
    return [pl.BlockSpec(memory_space=pl.ANY)] * n


def vmem_spec(n):
    return [pl.BlockSpec(memory_space=pltpu.VMEM)] * n


def run(steps):
    for step in steps:
        step()


def at_step(index, hooks):
    for k, steps in hooks.items():
        pl.when(index == k)(functools.partial(run, steps))


NJ = HC // HD
ROWS = 256
CHUNKS = LEN // ROWS
PARTS = 7


def forward_kernel(n, cb, comm, *refs):
    dp = 2 * n
    r = D // dp
    (len_ref, x_ref, own_a, own_b, own_1, own_2,
     out_ref, h1_ref, xhat1_ref, rstd1_ref, g_ref, xhat2_ref, rstd2_ref, gain_ref, row_ref, hb_ref, ct_ref, every_ref, xt,
     gp_out, q_out, k_out, v_out, wa_out, w1_out, w2_out,
     wa, w1, w2, table, bcol, col, qt, kt, vt, c_nat, wo, r2, stage, pool_own, every,
     local, q_sem, stage_sem, w_sem, *sems) = refs
    length = len_ref[0]
    gathers = {}
    if comm:
        p = Place(n)
        enter(p)
        pairs = [(own_a.at[j], wa.at[j]) for j in range(NJ)] + [(own_b, table), (own_1, w1), (own_2, w2), (pool_own, every)]
        a0, a1, a2, bias, up, down, pools = [Gather(p, i, own, full, sems) for i, (own, full) in enumerate(pairs)]

        def begin(g):
            g.start()
            g.local(local).start()

        def end(g):
            g.flow()[-1]()
            g.local(local).wait()

        def piece(g, first, last):
            return [functools.partial(run, g.flow()[first:last])]

        begin(a0)
        begin(bias)
        for one, two in zip(a0.flow()[:-1], bias.flow()[:-1]):
            one()
            two()
            if one is None:
                break
        begin(a1)
        begin(a2)
        xt[...] = x_ref[...].T
        end(a0)
        end(bias)
        begin(up)
        begin(down)
        hooks = {
            0: piece(a1, 0, 3), 1: piece(a1, 3, 7), 2: piece(a1, 7, 11) + piece(a2, 0, 3),
            3: [functools.partial(end, a1)] + piece(a2, 3, 7), 4: piece(a2, 7, 11) + piece(up, 0, 1),
            5: piece(up, 1, 3), 6: piece(up, 3, 5) + piece(down, 0, 1), 7: [functools.partial(end, a2)] + piece(up, 5, 7),
            8: piece(down, 1, 3), 9: piece(down, 3, 5), 10: piece(up, 7, 11), 11: piece(down, 5, 7),
        }
    else:
        loads = [
            pltpu.make_async_copy(src, dst, local.at[i])
            for i, (src, dst) in enumerate(((own_a, wa), (own_b, table), (own_1, w1), (own_2, w2)))
        ]
        for cp in loads:
            cp.start()
        xt[...] = x_ref[...].T
        for cp in loads:
            cp.wait()
        hooks = {}

    col_rows = -(-cb // r)
    for i in range(dp):
        rows = slice(i * 32, i * 32 + 16)
        row_ref[:, i * r : i * r + r] = table[0, rows, 0:r].astype(f32)
        for t in range(NT):
            tile = table[t, rows, :].astype(f32)
            for k in range(col_rows):
                wide = min(r, cb - k * r)
                col[t, :, i * cb + k * r : i * cb + k * r + wide] = jnp.broadcast_to(tile[6 + k : 7 + k, 0:wide], (8, wide))
    for t in range(NT):
        bcol[t] = jnp.transpose(col[t, :, 0 : 2 * HC])[:, 0:1]
        hb_ref[t] = col[t, 0:1, 2 * HC : 2 * HC + D]

    ones = jnp.ones((1, LEN), f32)
    where = lax.broadcasted_iota(jnp.int32, (1, LEN), 1)
    key_bias = jnp.where(where < length, 0.0, masked).astype(f32)
    kept = ((qt, q_out), (kt, k_out), (vt, v_out))

    def head(h, _):
        j, t = h // NT, h % NT
        qkv = tn(wa[j, t, :, 0 : 3 * HD], xt[...])
        qt[h, 0:HD, :] = ((qkv[0:HD] + bcol[t, pl.ds(pl.multiple_of(j * HD, HD), HD), :]) * HD**-0.5).astype(bf16)
        kt[h, 0:HD, :] = qkv[HD : 2 * HD].astype(bf16)
        vt[h] = (qkv[2 * HD : 3 * HD] + bcol[t, pl.ds(pl.multiple_of(HC + j * HD, HD), HD), :]).astype(bf16)
        qt[h, HD:AUG, :] = aug_rows(ones)
        kt[h, HD:AUG, :] = aug_rows(key_bias, ones, ones, ones)
        s = tn(kt[h], qt[h])
        top = jnp.max(s, axis=0, keepdims=True)
        e = jnp.exp(s - top)
        total = jnp.sum(e, axis=0, keepdims=True)
        prob = (e * (1.0 / total)).astype(bf16)
        ct_ref[pl.ds(pl.multiple_of(h * HD, HD), HD), :] = nn(vt[h], prob).astype(bf16)
        hi, mid, lo = split3(-(top + jnp.log(total)))
        qt[h, HD:AUG, :] = aug_rows(ones, hi, mid, lo)
        for i, (src, dst) in enumerate(kept):
            pltpu.make_async_copy(src.at[h], dst.at[h], q_sem.at[i, h]).start()
        at_step(h, hooks)
        return 0

    lax.fori_loop(0, H, head, 0)

    if comm:
        run(piece(down, 7, 9))
    c_nat[...] = ct_ref[...].T
    for j in range(NJ):
        for t in range(NT):
            h = j * NT + t
            wo[:, h * HD : h * HD + HD] = wa[j, t, :, 3 * HD : 4 * HD]
    weights = ((wa, wa_out), (w1, w1_out), (w2, w2_out))

    def first(i, _):
        s = pl.ds(pl.multiple_of(i * ROWS, ROWS), ROWS)
        r1 = x_ref[s, :].astype(f32) + (nt(c_nat[s, :], wo[...]) + row_ref[0:1])
        xhat, rstd = norm(r1)
        xhat1_ref[s, :] = xhat
        rstd1_ref[s, :] = rstd
        h1_ref[s, :] = (xhat * row_ref[1:2] + row_ref[2:3]).astype(bf16)
        return 0

    lax.fori_loop(0, CHUNKS, first, 0)
    if comm:
        end(up)

    def staged(step):
        t, i = step // CHUNKS, step % CHUNKS
        s = pl.ds(pl.multiple_of(i * ROWS, ROWS), ROWS)
        return pltpu.make_async_copy(stage.at[step % 2], gp_out.at[t, s, :], stage_sem.at[step % 2])

    def hidden(step, _):
        t, i = step // CHUNKS, step % CHUNKS
        s = pl.ds(pl.multiple_of(i * ROWS, ROWS), ROWS)
        z = nn(h1_ref[s, :], w1[t]) + hb_ref[t]
        cdf = 0.5 + 0.5 * lax.erf(z * 0.5**0.5)
        g_ref[t, s, :] = (z * cdf).astype(bf16)

        @pl.when(step >= 2)
        def _():
            staged(step - 2).wait()

        stage[step % 2] = cdf + z * (jnp.exp(-0.5 * z * z) * 0.3989422804014327)
        staged(step).start()
        if comm:
            at_step(step, {8: piece(down, 9, 11)})
        return 0

    lax.fori_loop(0, NT * CHUNKS, hidden, 0)
    staged(NT * CHUNKS - 2).wait()
    staged(NT * CHUNKS - 1).wait()
    if comm:
        end(down)
    for i, (src, dst) in enumerate(weights):
        pltpu.make_async_copy(src, dst, w_sem.at[i]).start()
    pool = jnp.zeros((1, D), f32)
    gain_ref[...] = jnp.zeros_like(gain_ref)
    r2[0:1, :] = pool

    def second(i, _):
        s = pl.ds(pl.multiple_of(i * ROWS, ROWS), ROWS)
        res = xhat1_ref[s, :] * row_ref[1:2] + row_ref[2:3] + row_ref[3:4]
        for t in range(NT):
            res = res + nt(g_ref[t, s, :], w2[t])
        xhat, rstd = norm(res)
        xhat2_ref[s, :] = xhat
        rstd2_ref[s, :] = rstd
        y = xhat * row_ref[4:5] + row_ref[5:6]
        out_ref[s, :] = y.astype(bf16)
        here = i * ROWS + lax.broadcasted_iota(jnp.int32, (ROWS, 1), 0) < length
        r2[0:1, :] += jnp.sum(jnp.where(here, y, 0.0), axis=0, keepdims=True)
        gain_ref[...] += jnp.sum(jnp.where(here, xhat, 0.0), axis=0, keepdims=True)
        return 0

    lax.fori_loop(0, CHUNKS, second, 0)
    mean = r2[0:1, :] * (1.0 / jnp.full((1, 1), length).astype(f32))
    pool_own[...] = jnp.zeros_like(pool_own)
    for i in range(D // 128):
        pool_own[i : i + 1, :] = mean[:, i * 128 : i * 128 + 128]
    if comm:
        begin(pools)
        run(pools.flow()[:-1])
        end(pools)
        every_ref[...] = every[...]
        for g in (a0, a1, a2, bias, up, down, pools):
            g.finish()
    else:
        every_ref[...] = pool_own[...]
    for h in range(H):
        for i, (src, dst) in enumerate(kept):
            pltpu.make_async_copy(src.at[h], dst.at[h], q_sem.at[i, h]).wait()
    for i, (src, dst) in enumerate(weights):
        pltpu.make_async_copy(src, dst, w_sem.at[i]).wait()


def forward(length, x, own_a, own_b, own_1, own_2, n, cb, comm):
    s = jax.ShapeDtypeStruct
    dp = 2 * n
    dma = pltpu.SemaphoreType.DMA
    shapes = [
        s((LEN, D), bf16), s((LEN, D), bf16), s((LEN, D), f32), s((LEN, 1), f32), s((NT, LEN, D), bf16), s((LEN, D), f32),
        s((LEN, 1), f32), s((1, D), f32), s((16, D), f32), s((NT, 1, D), f32), s((D, LEN), bf16),
        s((NT, dp * 16, 128) if comm else (16, 128), f32), s((D, LEN), bf16),
    ]
    kept = [
        s((NT, LEN, D), f32), s((H, AUG, LEN), bf16), s((H, AUG, LEN), bf16), s((H, HD, LEN), bf16),
        s((NJ, NT, D, 4 * HD), bf16), s((NT, D, D), bf16), s((NT, D, D), bf16),
    ]
    scratch = [
        pltpu.VMEM((NJ, NT, D, 4 * HD), bf16), pltpu.VMEM((NT, D, D), bf16), pltpu.VMEM((NT, D, D), bf16),
        pltpu.VMEM((NT, dp * 32, 128), bf16), pltpu.VMEM((NT, 2 * HC, 1), f32), pltpu.VMEM((NT, 8, dp * cb), f32),
        pltpu.VMEM((H, AUG, LEN), bf16), pltpu.VMEM((H, AUG, LEN), bf16), pltpu.VMEM((H, HD, LEN), bf16),
        pltpu.VMEM((LEN, D), bf16), pltpu.VMEM((D, D), bf16), pltpu.VMEM((8, D), f32), pltpu.VMEM((2, ROWS, D), f32),
        pltpu.VMEM((16, 128), f32), pltpu.VMEM((NT, dp * 16, 128), f32),
        dma((PARTS,)), dma((3, H)), dma((2,)), dma((3,)),
    ]
    if comm:
        scratch += gather_sems(PARTS, n)
        params = pltpu.CompilerParams(collective_id=0, has_side_effects=True, vmem_limit_bytes=VMEM_CAP)
    else:
        params = pltpu.CompilerParams(vmem_limit_bytes=VMEM_CAP)
    return pl.pallas_call(
        functools.partial(forward_kernel, n, cb, comm),
        out_shape=shapes + kept,
        in_specs=[pl.BlockSpec(memory_space=pltpu.SMEM)] + vmem_spec(1) + any_spec(4),
        out_specs=vmem_spec(len(shapes)) + any_spec(len(kept)),
        scratch_shapes=scratch,
        compiler_params=params,
    )(length, x, own_a, own_b, own_1, own_2)


def feed_back_kernel(
    len_ref, u_ref, gain_ref, xhat2_ref, rstd2_ref, row_ref, w1_ref, w2_ref, g_ref, gp_ref, h1_ref,
    gw1_ref, gw2_ref, dh_ref, ghb_ref, grow_ref,
    df_ref, dft_ref, h1t_ref, dz_ref,
):
    @pl.when(pl.program_id(0) == 0)
    def _():
        length = len_ref[0]
        u = u_ref[...]
        du = u * row_ref[4:5]
        mean_du = jnp.mean(du, axis=1, keepdims=True)
        h1t_ref[...] = h1_ref[...].T
        grow_ref[...] = jnp.zeros_like(grow_ref)

        def rows(i, _):
            s = pl.ds(pl.multiple_of(i * ROWS, ROWS), ROWS)
            here = i * ROWS + lax.broadcasted_iota(jnp.int32, (ROWS, 1), 0) < length
            xhat = xhat2_ref[s, :]
            dot = jnp.mean(xhat * du, axis=1, keepdims=True)
            dr = jnp.where(here, rstd2_ref[s, :] * (du - mean_du - xhat * dot), 0.0)
            dh_ref[s, :] = dr
            low = dr.astype(bf16)
            df_ref[s, :] = low
            grow_ref[3:4] += jnp.sum(low.astype(f32), axis=0, keepdims=True)
            return 0

        lax.fori_loop(0, CHUNKS, rows, 0)
        grow_ref[4:5] = u * gain_ref[...]
        grow_ref[5:6] = u * jnp.full((1, 1), length).astype(f32)
        dft_ref[...] = df_ref[...].T

    hb = jnp.zeros((1, D), f32)
    for i in range(CHUNKS):
        s = pl.ds(i * ROWS, ROWS)
        dz = (nn(df_ref[s, :], w2_ref[0]) * gp_ref[0, s, :]).astype(bf16)
        dz_ref[s, :] = dz
        hb = hb + jnp.sum(dz.astype(f32), axis=0, keepdims=True)
        dh_ref[s, :] += nt(dz, w1_ref[0])
    ghb_ref[0] = hb
    gw1_ref[0] = nn(h1t_ref[...], dz_ref[...]).astype(bf16)
    gw2_ref[0] = nn(dft_ref[...], g_ref[0]).astype(bf16)


def feed_back(length, u, gain, xhat2, rstd2, row, w1, w2, g, gp, h1):
    s = jax.ShapeDtypeStruct

    def part(rows):
        return pl.BlockSpec((1, rows, D), lambda t: (t, 0, 0))

    def all_of(*shape):
        return pl.BlockSpec(shape, lambda t: (0,) * len(shape))

    return pl.pallas_call(
        feed_back_kernel,
        grid=(NT,),
        out_shape=[s((NT, D, D), bf16), s((NT, D, D), bf16), s((LEN, D), f32), s((NT, 1, D), f32), s((16, D), f32)],
        in_specs=[pl.BlockSpec(memory_space=pltpu.SMEM), all_of(1, D), all_of(1, D), all_of(LEN, D), all_of(LEN, 1), all_of(16, D),
                  part(D), part(D), part(LEN), part(LEN), all_of(LEN, D)],
        out_specs=[part(D), part(D), all_of(LEN, D), part(1), all_of(16, D)],
        scratch_shapes=[pltpu.VMEM((LEN, D), bf16), pltpu.VMEM((D, LEN), bf16), pltpu.VMEM((D, LEN), bf16), pltpu.VMEM((LEN, D), bf16)],
        compiler_params=pltpu.CompilerParams(vmem_limit_bytes=VMEM_CAP),
    )(length, u, gain, xhat2, rstd2, row, w1, w2, g, gp, h1)


def backward_kernel(n, cb, comm, *refs):
    dp = 2 * n
    r = D // dp
    (row_ref, rstd_ref, ghb_ref, grow_in, ct_ref, xt, dh_in, xhat_in, wa_in, q_in, k_in, v_in, gw1_in, gw2_in,
     dx_ref, *rest) = refs
    outs, rest = rest[: NJ + 3], rest[NJ + 3 :]
    (wa, qkv, dat, dct, dqkv, wcat, dxt, s_ref, d_ref, p_ref, ds_ref, grow, gcol, gbias, load, q_sem, *rest) = rest
    hooks = {}
    grads = [wa.at[j] for j in range(NJ)]
    if comm:
        own1, own2, *rest = rest
        bufs, sems = rest[:-8], rest[-8:]
        p = Place(n)
        enter(p)
        parts = []
        for i, (rows, src, slab) in enumerate(
            [(r, lambda t: gw1_in.at[t], lambda y: own1.at[y]), (r, lambda t: gw2_in.at[t], lambda y: own2.at[y])]
            + [(r, lambda t, g=g: g.at[t], lambda y, g=g: g.at[y * 2 + p.c]) for g in grads]
            + [(32, lambda t: gbias.at[t], lambda y: gbias.at[y * 2 + p.c])]
        ):
            parts.append(Scatter(p, i, rows, src, slab, outs[i], bufs[4 * i : 4 * i + 4], sems))
        up, down, a0, a1, a2, bias = parts
        up.core()
        down.core()
        owns = [
            pltpu.make_async_copy(src.at[y * 2 + p.c], dst.at[y], load.at[3 + 2 * i + y])
            for i, (src, dst) in enumerate(((gw1_in, own1), (gw2_in, own2))) for y in range(2)
        ]
        hooks = {
            0: [down.corner], 2: [up.cross], 3: [a0.core], 4: [down.cross], 5: [a0.corner], 6: [up.line], 7: [a1.core],
            8: [a0.cross], 9: [down.line, up.last, a1.corner], 10: [a0.line], 11: [a1.cross, a2.core],
        }
    else:
        owns = []
    loads = [
        pltpu.make_async_copy(dh_in, s_ref.at[:, 0:D], load.at[0]), pltpu.make_async_copy(xhat_in, d_ref.at[:, 0:D], load.at[1]),
        pltpu.make_async_copy(wa_in, wa, load.at[2]),
    ]
    for cp in loads + owns:
        cp.start()

    def fetch(h, slot):
        return [
            pltpu.make_async_copy(src.at[h], qkv.at[slot, i, 0 : src.shape[1], :], q_sem.at[slot, i])
            for i, src in enumerate((q_in, k_in, v_in))
        ]

    for cp in fetch(0, 0):
        cp.start()
    dxt[...] = jnp.zeros_like(dxt)
    grow[...] = grow_in[...]
    loads[0].wait()
    loads[1].wait()

    def first(i, _):
        s = pl.ds(pl.multiple_of(i * ROWS, ROWS), ROWS)
        dh = s_ref[s, 0:D]
        xhat = d_ref[s, 0:D]
        grow[1:2] += jnp.sum(dh * xhat, axis=0, keepdims=True)
        grow[2:3] += jnp.sum(dh, axis=0, keepdims=True)
        dn = dh * row_ref[1:2]
        dr = rstd_ref[s, :] * (dn - jnp.mean(dn, axis=1, keepdims=True) - xhat * jnp.mean(dn * xhat, axis=1, keepdims=True))
        dx_ref[s, :] = dr
        low = dr.astype(bf16)
        grow[0:1] += jnp.sum(low.astype(f32), axis=0, keepdims=True)
        dat[:, s] = low.T
        return 0

    for i in range(CHUNKS):
        first(i, 0)
    loads[2].wait()
    for cp in owns:
        cp.wait()
    for j in range(NJ):
        for t in range(NT):
            h = j * NT + t
            wcat[:, h * HD : h * HD + HD] = wa[j, t, :, 3 * HD : 4 * HD]
    for i in range(D // ROWS):
        s = slice(i * ROWS, (i + 1) * ROWS)
        dct[s, :] = tn(wcat[:, s], dat[...]).astype(bf16)
        gwo = nt(dat[s, :], ct_ref[...]).astype(bf16)
        for j in range(NJ):
            for t in range(NT):
                h = j * NT + t
                wa[j, t, s, 3 * HD : 4 * HD] = gwo[:, h * HD : h * HD + HD]
    if comm:
        up.corner()

    def head(h, _):
        j, t = h // NT, h % NT
        slot = h % 2
        for cp in fetch(h, slot):
            cp.wait()

        @pl.when(h + 1 < H)
        def _():
            for cp in fetch(h + 1, 1 - slot):
                cp.start()

        own = pl.ds(pl.multiple_of(h * HD, HD), HD)
        prob = jnp.exp(tn(qkv[slot, 1], qkv[slot, 0]))
        s_ref[...] = prob
        d_ref[...] = tn(qkv[slot, 2, 0:HD, :], dct[own, :])
        p_ref[...] = prob.astype(bf16)
        inner = jnp.sum(s_ref[...] * d_ref[...], axis=0, keepdims=True)
        ds_ref[...] = (s_ref[...] * (d_ref[...] - inner)).astype(bf16)
        at = pl.multiple_of(t * 3 * HD, HD)
        dqkv[pl.ds(at, HD), :] = (nn(qkv[slot, 1, 0:HD, :], ds_ref[...]) * HD**-0.5).astype(bf16)
        dqkv[pl.ds(at + HD, HD), :] = nt(qkv[slot, 0, 0:HD, :], ds_ref[...]).astype(bf16)
        dqkv[pl.ds(at + 2 * HD, HD), :] = nt(dct[own, :], p_ref[...]).astype(bf16)

        @pl.when(t == NT - 1)
        def _():
            for k in range(NT):
                wcat[:, k * 3 * HD : (k + 1) * 3 * HD] = wa[j, k, :, 0 : 3 * HD]
            sums = nt(jnp.ones((16, LEN), bf16), dqkv[...])
            for k in range(NT):
                gcol[j, k] = sums[0:8, k * 3 * HD : (k + 1) * 3 * HD]
            for i in range(D // ROWS):
                s = slice(i * ROWS, (i + 1) * ROWS)
                dxt[s, :] += nn(wcat[s, :], dqkv[...])
                g = nt(xt[s, :], dqkv[...]).astype(bf16)
                for k in range(NT):
                    wa[j, k, s, 0 : 3 * HD] = g[:, k * 3 * HD : (k + 1) * 3 * HD]

        at_step(h, hooks)
        return 0

    lax.fori_loop(0, H, head, 0)

    col_rows = -(-cb // r)
    cols = []
    for t in range(NT):
        pieces = [gcol[j, t, 0:1, 0:HD] for j in range(NJ)] + [gcol[j, t, 0:1, 2 * HD : 3 * HD] for j in range(NJ)]
        cols.append(jnp.concatenate(pieces + [ghb_ref[t]], axis=1))
    at = lax.broadcasted_iota(jnp.int32, (32, 128), 0)
    for i in range(dp):
        rows = jnp.pad(grow[0:8, i * r : i * r + r], ((0, 24), (0, 128 - r)))
        for t in range(NT):
            block = jnp.where(at < 6, rows, 0.0)
            for k in range(col_rows):
                wide = min(r, cb - k * r)
                piece = cols[t][:, i * cb + k * r : i * cb + k * r + wide]
                block = jnp.where(at == 6 + k, jnp.pad(piece, ((0, 0), (0, 128 - wide))), block)
            gbias[t, i * 32 : i * 32 + 32, :] = block.astype(bf16)
    if comm:
        bias.core()
    for i in range(CHUNKS):
        s = pl.ds(i * ROWS, ROWS)
        dx_ref[s, :] += dxt[:, s].T
    if comm:
        a2.corner()
        bias.corner()
        down.last()
        a0.last()
        a1.line()
        a2.cross()
        bias.cross()
        a1.last()
        a2.line()
        bias.line()
        a2.last()
        bias.last()
        for part in parts:
            part.finish()
    else:
        copies = [pltpu.make_async_copy(src, dst, load.at[i]) for i, (src, dst) in enumerate(zip(grads + [gbias], outs))]
        for cp in copies:
            cp.start()
        for cp in copies:
            cp.wait()


def backward(row, rstd1, ghb, grow, ct, xt, dh, xhat1, wa, qt, kt, vt, gw1, gw2, n, cb, comm):
    s = jax.ShapeDtypeStruct
    dp = 2 * n
    r = D // dp
    dma = pltpu.SemaphoreType.DMA
    if comm:
        widths = [(r, D), (r, D)] + [(r, 4 * HD)] * NJ + [(32, 128)]
        sums = [s(shape, f32) for shape in widths]
        sum_specs = vmem_spec(len(sums))
    else:
        widths = []
        sums = [s((NT, D, 4 * HD), bf16)] * NJ + [s((NT, dp * 32, 128), bf16)] + [s((8, 128), f32)] * 2
        sum_specs = any_spec(len(sums))
    scratch = [
        pltpu.VMEM((NJ, NT, D, 4 * HD), bf16), pltpu.VMEM((2, 3, AUG, LEN), bf16), pltpu.VMEM((D, LEN), bf16), pltpu.VMEM((D, LEN), bf16),
        pltpu.VMEM((D, LEN), bf16), pltpu.VMEM((D, D), bf16), pltpu.VMEM((D, LEN), f32),
        pltpu.VMEM((LEN, LEN), f32), pltpu.VMEM((LEN, LEN), f32), pltpu.VMEM((LEN, LEN), bf16), pltpu.VMEM((LEN, LEN), bf16),
        pltpu.VMEM((16, D), f32), pltpu.VMEM((NJ, NT, 8, 3 * HD), f32), pltpu.VMEM((NT, dp * 32, 128), bf16),
        dma((7,)), dma((2, 3)),
    ]
    if comm:
        scratch += [pltpu.VMEM((2, D, D), bf16)] * 2
        for rows, wide in widths:
            scratch += scatter_bufs(n, rows, wide)
        scratch += scatter_sems(len(widths), n)
        params = pltpu.CompilerParams(collective_id=1, has_side_effects=True, vmem_limit_bytes=VMEM_CAP)
    else:
        params = pltpu.CompilerParams(vmem_limit_bytes=VMEM_CAP)
    return pl.pallas_call(
        functools.partial(backward_kernel, n, cb, comm),
        out_shape=[s((LEN, D), f32)] + sums,
        in_specs=vmem_spec(6) + any_spec(8),
        out_specs=vmem_spec(1) + sum_specs,
        scratch_shapes=scratch,
        compiler_params=params,
    )(row, rstd1, ghb, grow, ct, xt, dh, xhat1, wa, qt, kt, vt, gw1, gw2)


def gather_plain(own):
    return lax.all_gather(lax.all_gather(own, "dp", axis=0, tiled=True), "tensor", axis=0)


def scatter_plain(full):
    own = lax.psum_scatter(full.astype(f32), "tensor", scatter_dimension=0, tiled=False)
    return lax.psum_scatter(own, "dp", scatter_dimension=0, tiled=True)


def by_head(wide):
    return jnp.moveaxis(wide.reshape(*wide.shape[:-1], NJ, HD), -2, 0)


def on_device(
    inputs, lengths, groups, qkv_weight, out_weight, up_weight, down_weight, col_bias, row_params,
    qkv_first, out_first, up_first, down_first, col_first, row_first,
    qkv_second, out_second, up_second, down_second, col_second, row_second,
    qkv_ema, out_ema, up_ema, down_ema, col_ema, row_ema,
):
    dp = lax.axis_size("dp")
    n = dp // 2
    r = D // dp
    cb = col_bias.shape[1]
    index = lax.axis_index(("dp", "tensor"))
    length = lax.dynamic_slice_in_dim(lengths, lax.axis_index("tensor"), 1)
    comm = r % 32 == 0

    own_a = jnp.concatenate([by_head(qkv_weight[i]) for i in range(3)] + [by_head(out_weight.T)], axis=-1).astype(bf16)
    own_1 = up_weight.astype(bf16)
    own_2 = down_weight.T.astype(bf16)
    col_rows = -(-cb // r)
    col_pad = jnp.pad(col_bias[0], (0, col_rows * r - cb)).reshape(col_rows, r)
    own_b = jnp.pad(jnp.concatenate([row_params, col_pad], axis=0), ((0, 26 - col_rows), (0, 128 - r))).astype(bf16)
    if not comm:
        own_a = jnp.stack([gather_plain(own_a[j]) for j in range(NJ)])
        own_b, own_1, own_2 = gather_plain(own_b), gather_plain(own_1), gather_plain(own_2)
    (outputs, h1, xhat1, rstd1, g, xhat2, rstd2, gain, row, hb, ct, every, xt, gp, qt, kt, vt, wa, w1, w2) = forward(
        length, inputs, own_a, own_b, own_1, own_2, n, cb, comm
    )
    if not comm:
        every = gather_plain(every)
    every = every.reshape(NT, dp, 16, 128)[:, :, : D // 128].transpose(1, 0, 2, 3).reshape(dp * NT, D)
    grad_pooled = jax.grad(lambda v: contrast_loss(v, groups))(every)
    u = lax.dynamic_slice_in_dim(grad_pooled, index, 1, 0) / length[0].astype(f32)

    gw1, gw2, dh, ghb, grow = feed_back(length, u, gain, xhat2, rstd2, row, w1, w2, g, gp, h1)
    input_grad, *sums = backward(row, rstd1, ghb, grow, ct, xt, dh, xhat1, wa, qt, kt, vt, gw1, gw2, n, cb, comm)
    if comm:
        gw1, gw2, *ga, gbias = sums
    else:
        *ga, gbias = [scatter_plain(v) for v in sums[: NJ + 1]]
        gw1, gw2 = scatter_plain(gw1), scatter_plain(gw2)

    ga = jnp.stack(ga, axis=1).reshape(r, NJ, 4, HD).transpose(2, 0, 1, 3).reshape(4, r, HC)
    grad_row = gbias[0:6, :r]
    grad_col = gbias[6 : 6 + col_rows, :r].reshape(1, col_rows * r)[:, :cb]
    qkv_new = adam_update(qkv_weight, qkv_first, qkv_second, qkv_ema, ga[0:3], D ** (-0.5))
    out_new = adam_update(out_weight, out_first, out_second, out_ema, ga[3].T, D ** (-0.5))
    up_new = adam_update(up_weight, up_first, up_second, up_ema, gw1, D ** (-0.5))
    down_new = adam_update(down_weight, down_first, down_second, down_ema, gw2.T, FF ** (-0.5))
    col_new = adam_update(col_bias, col_first, col_second, col_ema, grad_col, 0.1)
    row_new = adam_update(row_params, row_first, row_second, row_ema, grad_row, 0.15)
    return (outputs, input_grad, *qkv_new, *out_new, *up_new, *down_new, *col_new, *row_new)


def solution(mesh):
    tokens = P(("dp", "tensor"), None)
    placed = (P(None, "dp", "tensor"), P("tensor", "dp"), P("dp", "tensor"), P("tensor", "dp"), P("tensor", "dp"), P(None, "dp"))
    new = tuple(spec for spec in placed for _ in range(4))
    return jax.shard_map(
        on_device,
        mesh=mesh,
        in_specs=(tokens, P("dp"), P()) + placed * 4,
        out_specs=(tokens, tokens) + new,
        check_vma=False,
    )
```

```python
import functools

import jax
import jax.numpy as jnp
from jax import lax
from jax.experimental import pallas as pl
from jax.experimental.pallas import tpu as pltpu
from jax.sharding import PartitionSpec as P

D = 768
H = 12
HD = 64
FF = 3072
LEN = 1024
STEP = 5
NT = 4
HC = D // NT
AUG = 80

MESH = pl.DeviceIdType.MESH
f32 = jnp.float32
bf16 = jnp.bfloat16
highest = lax.Precision.HIGHEST
eps_norm = 1e-05
temper = 40.0
masked = -1000000000.0
beta_one = 0.5
beta_two = 0.5
adam_eps = 1e-08
decay_rate = 0.01
ema_keep = 0.9
VMEM_CAP = 60 << 20


def nn(a, b):
    return jnp.dot(a, b, preferred_element_type=f32)


def nt(a, b):
    return lax.dot_general(a, b, (((1,), (1,)), ((), ())), preferred_element_type=f32)


def tn(a, b):
    return lax.dot_general(a, b, (((0,), (0,)), ((), ())), preferred_element_type=f32)


def adam_update(weight, first_old, second, ema_old, gradient, step_rate):
    first_new = beta_one * first_old + (1 - beta_one) * gradient
    second_new = beta_two * second + (1 - beta_two) * gradient * gradient
    first_hat = first_new / (1 - beta_one**STEP)
    second_hat = second_new / (1 - beta_two**STEP)
    weight_new = weight - step_rate * (
        first_hat / (jnp.sqrt(second_hat) + adam_eps) + decay_rate * weight
    )
    ema_new = ema_keep * ema_old + (1 - ema_keep) * weight_new
    return (first_new, second_new, weight_new, ema_new)


class Place:
    def __init__(self, depth):
        dp = lax.axis_index("dp")
        t = lax.axis_index("tensor")
        self.depth = depth
        self.z, self.x, self.y, self.c = dp // 2, dp % 2, t // 2, t % 2
        self.me = (self.z, self.x, self.y, self.c)
        self.over_x = (self.z, 1 - self.x, self.y, self.c)
        self.over_y = (self.z, self.x, 1 - self.y, self.c)
        self.over_xy = (self.z, 1 - self.x, 1 - self.y, self.c)
        self.over_c = (self.z, self.x, self.y, 1 - self.c)

    def along_z(self, k):
        return ((self.z + k) % self.depth, self.x, self.y, self.c)


def device(place):
    z, x, y, c = place
    return (z * 2 + x, y * 2 + c)


def enter(p):
    bar = pltpu.get_barrier_semaphore()
    to = [p.over_x, p.over_y, p.over_c] + [p.along_z(k) for k in range(1, p.depth)]
    for place in to:
        pl.semaphore_signal(bar, inc=1, device_id=device(place), device_id_type=MESH)
    pl.semaphore_wait(bar, len(to))


def remote(src, dst, send, recv, to):
    return pltpu.make_async_remote_copy(
        src_ref=src, dst_ref=dst, send_sem=send, recv_sem=recv, device_id=device(to), device_id_type=MESH
    )


class Gather:
    def __init__(self, p, part, own, full, sems, straight=False):
        self.p, self.part, self.rows, self.own, self.full, self.straight = p, part, own.shape[0], own, full, straight
        self.recv, self.sz, self.sx, self.sy, self.sc = sems
        self.sent = []

    def spot(self, place, half=None):
        z, x, y, c = place
        r = self.rows
        step = 32 // self.full.dtype.itemsize
        start = (z * 2 + x) * r
        if half is not None:
            start, r = start + half * (r // 2), r // 2
        return self.full.at[y * 2 + c, pl.ds(pl.multiple_of(start, step), r), :]

    def copy(self, src, place, half, to, send):
        z, x, y, c = place
        dst = self.spot(place, half)
        recv = self.recv.at[self.part, (z * 2 + x) * 4 + y * 2 + c, half or 0]
        return remote(dst if src is None else src, dst, send, recv, to)

    def send(self, place, half, to, send, when=None, src=None):
        def make():
            return self.copy(src, place(), half, to(), send())

        if when is not None:
            pl.when(when())(lambda: make().start())
        else:
            make().start()
        self.sent.append((make, when))

    def arrived(self, place, half=None):
        self.copy(None, place, half, self.p.over_c, self.sc.at[self.part, 0]).wait_recv()

    def local(self, sem):
        return pltpu.make_async_copy(self.own, self.spot(self.p.me), sem.at[self.part])

    def spread(self, place, slot, when=None, src=None):
        p, q = self.p, self.part
        self.send(place, None, lambda: p.over_x, lambda: self.sx.at[q, 0, slot], when, src)
        self.send(place, None, lambda: p.over_y, lambda: self.sy.at[q, 0, slot], when, src)
        self.send(place, None, lambda: p.over_c, lambda: self.sc.at[q, slot], when, src)

    def start(self):
        p, q, n = self.p, self.part, self.p.depth
        if self.straight:
            for k in range(1, n):
                self.send(lambda: p.me, None, lambda k=k: p.along_z(k), lambda k=k: self.sz.at[q, k], None, self.own)
        else:
            self.send(lambda: p.me, None, lambda: p.along_z(1), lambda: self.sz.at[q, 0], lambda: p.z + 1 < n, self.own)
            self.send(lambda: p.me, None, lambda: p.along_z(-1), lambda: self.sz.at[q, n], lambda: p.z > 0, self.own)
        self.spread(lambda: p.me, 0, None, self.own)

    def sides(self, k):
        p, n = self.p, self.p.depth
        if k == 0:
            return [(0, 0, None)]
        if self.straight:
            return [(1, k, None)]
        return [(-1, k, lambda: p.z >= k), (1, n + k, lambda: p.z + k < n)]

    def line_place(self, k, base):
        z, x, y, c = base
        return ((self.p.z + k) % self.p.depth, x, y, c)

    def wait_for(self, places, when):
        def wait():
            for place, half in places:
                self.arrived(place(), half)

        if when is not None:
            pl.when(when())(wait)
        else:
            wait()

    def line(self, k):
        p, q, n = self.p, self.part, self.p.depth
        for sign, slot, when in self.sides(k):
            place = functools.partial(self.line_place, sign * k, p.me)
            self.wait_for([(place, None)], when)
            if not self.straight:
                more = (lambda: jnp.logical_and(p.z >= k, p.z + 1 < n)) if sign < 0 else (lambda: jnp.logical_and(p.z + k < n, p.z > 0))
                self.send(place, None, lambda sign=sign: p.along_z(-sign), lambda slot=slot: self.sz.at[q, slot], more)
            self.spread(place, slot, when)

    def cross(self, k):
        p, q, n = self.p, self.part, self.p.depth
        for sign, slot, when in self.sides(k):
            for way, (base, to, sem) in enumerate(((p.over_x, p.over_y, self.sy), (p.over_y, p.over_x, self.sx))):
                place = functools.partial(self.line_place, sign * k, base)
                self.wait_for([(place, None)], when)
                self.send(place, way, lambda to=to: to, lambda sem=sem, slot=slot: sem.at[q, 1, slot], when)
                at = (1 + way) * 2 * n + slot
                self.send(place, None, lambda: p.over_c, lambda at=at: self.sc.at[q, at], when)

    def corner(self, k):
        p, q, n = self.p, self.part, self.p.depth
        for sign, slot, when in self.sides(k):
            place = functools.partial(self.line_place, sign * k, p.over_xy)
            self.wait_for([(place, 0), (place, 1)], when)
            self.send(place, None, lambda: p.over_c, lambda slot=slot: self.sc.at[q, 6 * n + slot], when)

    def other_core(self):
        p = self.p
        for z in range(p.depth):
            for x in range(2):
                for y in range(2):
                    self.arrived((z, x, y, 1 - p.c))

    def flow(self):
        n = self.p.depth
        steps = [functools.partial(self.cross, 0)]
        order = [1, n - 1] + list(range(2, n - 1)) if self.straight and n > 2 else list(range(1, n))
        for k in order:
            steps += [functools.partial(self.line, k), functools.partial(self.cross, k)]
        steps += [functools.partial(self.corner, k) for k in range(n)]
        steps.append(self.other_core)
        return steps

    def finish(self):
        for make, when in self.sent:
            if when is not None:
                pl.when(when())(lambda make=make: make().wait_send())
            else:
                make().wait_send()


def gather_sems(parts, n):
    dma = pltpu.SemaphoreType.DMA
    return [dma((parts, 8 * n, 2)), dma((parts, 2 * n)), dma((parts, 2, 2 * n)), dma((parts, 2, 2 * n)), dma((parts, 8 * n))]


class Scatter:
    def __init__(self, p, part, rows, source, slab, out, bufs, sems):
        self.p, self.part, self.rows, self.source, self.slab, self.out = p, part, rows, source, slab, out
        self.b_core, self.b_corner, self.b_cross, self.b_line = bufs
        self.ss, self.rs, self.sc, self.rc, self.sx, self.rx, self.sl, self.rl = sems
        self.sent = []

    def span(self, z, x, half=None):
        r = self.rows
        start = (z * 2 + x) * r
        if half is not None:
            start, r = start + half * (r // 2), r // 2
        return pl.ds(pl.multiple_of(start, 16), r)

    def go(self, make, *args):
        make(*args).start()
        self.sent.append(functools.partial(make, *args))

    def core_copy(self, y):
        p, q = self.p, self.part
        return remote(self.source(y * 2 + 1 - p.c), self.b_core.at[y], self.ss.at[q, y], self.rs.at[q, y], p.over_c)

    def core(self):
        for y in range(2):
            self.go(self.core_copy, y)

    def corner_copy(self, z, half):
        p, q = self.p, self.part
        src = self.slab(1 - p.y).at[self.span(z, 1 - p.x, half), :]
        to = p.over_x if half else p.over_y
        return remote(src, self.b_corner.at[half, z], self.sc.at[q, half, z], self.rc.at[q, half, z], to)

    def corner(self):
        r = self.rows
        for y in range(2):
            self.core_copy(y).wait_recv()
            slab = self.slab(y)

            def add(i, _, y=y, slab=slab):
                s = pl.ds(pl.multiple_of(i * r, 16), r)
                slab[s, :] = (slab[s, :].astype(f32) + self.b_core[y, s, :].astype(f32)).astype(bf16)
                return 0

            lax.fori_loop(0, 2 * self.p.depth, add, 0)
        for z in range(self.p.depth):
            for half in range(2):
                self.go(self.corner_copy, z, half)

    def cross_copy(self, z, way):
        p, q = self.p, self.part
        src = self.slab(1 - p.y).at[self.span(z, p.x), :] if way else self.slab(p.y).at[self.span(z, 1 - p.x), :]
        to = p.over_y if way else p.over_x
        return remote(src, self.b_cross.at[way, z], self.sx.at[q, way, z], self.rx.at[q, way, z], to)

    def cross(self):
        p = self.p
        for z in range(p.depth):
            for way in range(2):
                self.corner_copy(z, way).wait_recv()
                slab, s = (self.slab(1 - p.y), self.span(z, p.x, 1)) if way else (self.slab(p.y), self.span(z, 1 - p.x, 0))
                slab[s, :] = (slab[s, :].astype(f32) + self.b_corner[way, z].astype(f32)).astype(bf16)
                self.go(self.cross_copy, z, way)

    def line_copy(self, k):
        p, q = self.p, self.part
        z = (p.z + k) % p.depth
        return remote(self.slab(p.y).at[self.span(z, p.x), :], self.b_line.at[k], self.sl.at[q, k], self.rl.at[q, k], p.along_z(k))

    def column(self, z):
        p = self.p
        for way in range(2):
            self.cross_copy(z, way).wait_recv()
        return self.slab(p.y)[self.span(z, p.x), :].astype(f32) + self.b_cross[0, z].astype(f32) + self.b_cross[1, z].astype(f32)

    def line(self):
        p = self.p
        for k in range(1, p.depth):
            z = (p.z + k) % p.depth
            self.slab(p.y)[self.span(z, p.x), :] = self.column(z).astype(bf16)
            self.go(self.line_copy, k)

    def last(self):
        p = self.p
        total = self.column(p.z)
        for k in range(1, p.depth):
            self.line_copy(k).wait_recv()
            total = total + self.b_line[k].astype(f32)
        self.out[...] = total

    def finish(self):
        for make in self.sent:
            make().wait_send()


def scatter_bufs(n, rows, width):
    return [
        pltpu.VMEM((2, 2 * n * rows, width), bf16), pltpu.VMEM((2, n, rows // 2, width), bf16),
        pltpu.VMEM((2, n, rows, width), bf16), pltpu.VMEM((n, rows, width), bf16),
    ]


def scatter_sems(parts, n):
    dma = pltpu.SemaphoreType.DMA
    return [dma((parts, 2))] * 2 + [dma((parts, 2, n))] * 4 + [dma((parts, n))] * 2


def split3(row):
    hi = row.astype(bf16).astype(f32)
    mid = (row - hi).astype(bf16).astype(f32)
    return hi, mid, row - hi - mid


def aug_rows(*rows):
    width = rows[0].shape[1]
    at = lax.broadcasted_iota(jnp.int32, (16, width), 0)
    out = jnp.zeros((16, width), f32)
    for i, row in enumerate(rows):
        out = jnp.where(at == i, row, out)
    return out.astype(bf16)


def norm(r):
    cent = r - jnp.mean(r, axis=1, keepdims=True)
    rstd = lax.rsqrt(jnp.mean(cent * cent, axis=1, keepdims=True) + eps_norm)
    return cent * rstd, rstd


def any_spec(n):
    return [pl.BlockSpec(memory_space=pl.ANY)] * n


def vmem_spec(n):
    return [pl.BlockSpec(memory_space=pltpu.VMEM)] * n


def run(steps):
    for step in steps:
        step()


def at_step(index, hooks):
    for k, steps in hooks.items():
        pl.when(index == k)(functools.partial(run, steps))


NJ = HC // HD
ROWS = 256
CHUNKS = LEN // ROWS
PARTS = 7

PRE = ((0, 0), (3, 0), (1, 0), (0, 1), (2, 0), (3, 1), (3, 2), (0, 2), (1, 1), (3, 3), (3, 4), (1, 2), (2, 1), (0, 3), (3, 5), (3, 6), (0, 4), (1, 3), (1, 4), (3, 7), (3, 8), (3, 9), (0, 5), (0, 6), (2, 2), (1, 5), (3, 10), (3, 11), (0, 7), (0, 8), (0, 9), (4, 0), (3, 12), (0, 10), (0, 11), (1, 6), (2, 3), (0, 12), (2, 4))
HEAD = {0: ((1, 7), (1, 8), (1, 9), (1, 10), (2, 5), (2, 6), (1, 11), (4, 1), (4, 2), (5, 0), (1, 12), (2, 7), (2, 8), (2, 9), (2, 10)), 3: ((4, 3), (2, 11), (4, 4), (2, 12), (5, 1), (5, 2)), 5: ((4, 5), (4, 6)), 9: ((4, 7), (4, 8), (4, 9), (4, 10), (5, 3), (5, 4)), 10: ((4, 11),), 11: ((4, 12),)}
MID = ((5, 5), (5, 6))
LATE = {6: ((5, 7), (5, 8), (5, 9), (5, 10)), 9: ((5, 11),), 10: ((5, 12),)}


def pack(refs, own_a, own_b, own_1, own_2, r, cb):
    qkv, out, up, down, col, row = refs
    high = -(-r // 128) * 128
    out_t = jnp.concatenate([out[...], jnp.zeros((HC, high - r), f32)], axis=1)
    out_t = jnp.concatenate([out_t, jnp.zeros((256 - HC, high), f32)], axis=0).T[0:r]
    for j in range(NJ):
        s = slice(j * HD, j * HD + HD)
        own_a[j] = jnp.concatenate([qkv[0, :, s], qkv[1, :, s], qkv[2, :, s], out_t[:, s]], axis=1).astype(bf16)
    own_b[...] = jnp.zeros_like(own_b)
    tile = jnp.concatenate([row[...], jnp.zeros((10, r), f32)], axis=0)
    at = lax.broadcasted_iota(jnp.int32, (16, r), 0)
    for k in range(-(-cb // r)):
        wide = min(r, cb - k * r)
        piece = col[:, k * r : k * r + wide]
        if wide < r:
            piece = jnp.concatenate([piece, jnp.zeros((1, r - wide), f32)], axis=1)
        tile = jnp.where(at == 6 + k, piece, tile)
    own_b[0:16, 0:r] = tile.astype(bf16)
    own_1[...] = up[...].astype(bf16)
    own_2[...] = down[...].astype(bf16)


def loss_pull(pooled, groups, index):
    count = pooled.shape[0]
    inv = lax.rsqrt(jnp.sum(pooled * pooled, axis=1, keepdims=True) + eps_norm)
    unit = pooled * inv
    similar = temper * lax.dot_general(unit, unit, (((1,), (1,)), ((), ())), precision=highest, preferred_element_type=f32)
    rows = lax.broadcasted_iota(jnp.int32, (count, count), 0)
    cols = lax.broadcasted_iota(jnp.int32, (count, count), 1)
    others = jnp.where(rows == cols, masked, similar)
    members = groups.astype(f32)
    eye = jnp.where(rows == cols, 1.0, 0.0).astype(bf16)
    turned = nt(eye, members.astype(bf16))

    def pull(table, axis):
        top = jnp.max(others, axis=axis, keepdims=True)
        e = jnp.exp(others - top)
        return e / jnp.sum(e, axis=axis, keepdims=True) - table / jnp.sum(table, axis=axis, keepdims=True)

    both = temper * (pull(members, 1) + pull(turned, 0))
    grad = lax.dot_general(both, unit, (((1,), (0,)), ((), ())), precision=highest, preferred_element_type=f32)
    own = lax.broadcasted_iota(jnp.int32, (count, 1), 0) == index

    def pick(v):
        return jnp.sum(jnp.where(own, v, 0.0), axis=0, keepdims=True)

    unit, grad = pick(unit), pick(grad)
    return pick(inv) * (grad - unit * jnp.sum(unit * grad, axis=1, keepdims=True))


def forward_kernel(n, cb, comm, *refs):
    dp = 2 * n
    r = D // dp
    given, refs = (6, refs[:2] + refs[2:]) if comm else (4, refs)
    len_ref, groups_ref, x_ref = refs[:3]
    weights_in, refs = refs[3 : 3 + given], refs[3 + given :]
    (rstd1_ref, rstd2_ref, gain_ref, row_ref, hb_ref, u_ref,
     out_out, h1_out, xhat1_out, g_out, xhat2_out, ct_out, xt_out, gp_out, q_out, k_out, v_out, wa_out, w1_out, w2_out,
     out_ref, h1_ref, xhat1_ref, g_ref, xhat2_ref, ct_ref, xt,
     wa, w1, w2, table, bcol, col, qt, kt, vt, kn, sb, wo, pool, stage, pool_own, every, pooled,
     local, q_sem, stage_sem, o_sem, *sems) = refs
    length = len_ref[0]
    hooks, middle, late = {}, [], {}
    if comm:
        own_a, own_b, own_1, own_2, *sems = sems
        p = Place(n)
        pack(weights_in, own_a, own_b, own_1, own_2, r, cb)
        enter(p)
        pairs = [(own_a.at[j], wa.at[j]) for j in range(NJ)] + [(own_b, table), (own_1, w1), (own_2, w2), (pool_own, every)]
        straight = (False,) * NJ + (True, False, False, True)
        a0, a1, a2, bias, up, down, pools = [
            Gather(p, i, own, full, sems, way) for i, ((own, full), way) in enumerate(zip(pairs, straight))
        ]

        def begin(g):
            g.start()
            g.local(local).start()

        def end(g):
            g.flow()[-1]()
            g.local(local).wait()

        parts = (a0, a1, a2, bias, up, down)
        flows = [[functools.partial(begin, g)] + g.flow()[:-1] + [functools.partial(end, g)] for g in parts]

        def steps(pairs):
            return [flows[g][k] for g, k in pairs]

        if n == 4:
            run(steps(PRE[:5]))
            xt[...] = x_ref[...].T
            run(steps(PRE[5:]))
            hooks = {h: steps(pairs) for h, pairs in HEAD.items()}
            middle = steps(MID)
            late = {h: steps(pairs) for h, pairs in LATE.items()}
        else:
            xt[...] = x_ref[...].T
            for group in zip(*flows):
                run(group)
    else:
        loads = [pltpu.make_async_copy(src, dst, local.at[i]) for i, (src, dst) in enumerate(zip(weights_in, (wa, table, w1, w2)))]
        for cp in loads:
            cp.start()
        xt[...] = x_ref[...].T
        for cp in loads:
            cp.wait()
    saved = ((out_ref, out_out), (h1_ref, h1_out), (xhat1_ref, xhat1_out), (g_ref, g_out), (xhat2_ref, xhat2_out), (ct_ref, ct_out),
             (xt, xt_out), (wa, wa_out), (w1, w1_out), (w2, w2_out))

    def save(i):
        return pltpu.make_async_copy(*saved[i], o_sem.at[i])

    save(6).start()

    col_rows = -(-cb // r)
    for i in range(dp):
        rows = slice(i * 32, i * 32 + 16)
        row_ref[:, i * r : i * r + r] = table[0, rows, 0:r].astype(f32)
        for t in range(NT):
            tile = table[t, rows, :].astype(f32)
            for k in range(col_rows):
                wide = min(r, cb - k * r)
                col[t, :, i * cb + k * r : i * cb + k * r + wide] = jnp.broadcast_to(tile[6 + k : 7 + k, 0:wide], (8, wide))
    for t in range(NT):
        bcol[t] = jnp.transpose(col[t, :, 0 : 2 * HC])[:, 0:1]
        hb_ref[t] = col[t, 0:1, 2 * HC : 2 * HC + D]

    ones = jnp.ones((1, LEN), f32)
    where = lax.broadcasted_iota(jnp.int32, (1, LEN), 1)
    key_bias = jnp.where(where < length, 0.0, masked).astype(f32)
    kept = ((qt, q_out), (kt, k_out), (vt, v_out))
    key_rows = aug_rows(key_bias, ones, ones, ones)
    one_row = aug_rows(ones)
    half = LEN // 2

    def project(h):
        j, t = h // NT, h % NT
        qkv = tn(wa[j, t, :, 0 : 3 * HD], xt[...])
        qt[h, 0:HD, :] = ((qkv[0:HD] + bcol[t, pl.ds(pl.multiple_of(j * HD, HD), HD), :]) * HD**-0.5).astype(bf16)
        kt[h, 0:HD, :] = qkv[HD : 2 * HD].astype(bf16)
        vt[h] = (qkv[2 * HD : 3 * HD] + bcol[t, pl.ds(pl.multiple_of(HC + j * HD, HD), HD), :]).astype(bf16)
        qt[h, HD:AUG, :] = one_row
        kt[h, HD:AUG, :] = key_rows
        kn[h % 2] = kt[h].T

    def attend(h, i, s):
        where = slice(i * half, i * half + half)
        top = jnp.max(s, axis=0, keepdims=True)
        e = jnp.exp(s - top)
        total = jnp.sum(e, axis=0, keepdims=True)
        ct_ref[pl.ds(pl.multiple_of(h * HD, HD), HD), where] = (nn(vt[h], e.astype(bf16)) * (1.0 / total)).astype(bf16)
        hi, mid, lo = split3(-(top + jnp.log(total)))
        qt[h, HD:AUG, where] = aug_rows(ones[:, where], hi, mid, lo)

    project(0)
    sb[0] = nn(kn[0], qt[0, :, 0:half])

    def head(h, _):
        after = nn(kn[h % 2], qt[h, :, half:LEN])
        attend(h, 0, sb[0])
        sb[1] = after
        nxt = jnp.minimum(h + 1, H - 1)

        @pl.when(h + 1 < H)
        def _():
            project(nxt)

        after = nn(kn[nxt % 2], qt[nxt, :, 0:half])
        attend(h, 1, sb[1])
        sb[0] = after
        for i, (src, dst) in enumerate(kept):
            pltpu.make_async_copy(src.at[h], dst.at[h], q_sem.at[i, h]).start()
        at_step(h, hooks)
        return 0

    lax.fori_loop(0, H, head, 0)
    save(5).start()

    c_nat = out_ref
    c_nat[...] = ct_ref[...].T
    for j in range(NJ):
        for t in range(NT):
            h = j * NT + t
            wo[:, h * HD : h * HD + HD] = wa[j, t, :, 3 * HD : 4 * HD]
    save(7).start()

    def first(i, _):
        s = pl.ds(pl.multiple_of(i * ROWS, ROWS), ROWS)
        r1 = x_ref[s, :].astype(f32) + (nt(c_nat[s, :], wo[...]) + row_ref[0:1])
        xhat, rstd = norm(r1)
        xhat1_ref[s, :] = xhat
        rstd1_ref[s, :] = rstd
        h1_ref[s, :] = (xhat * row_ref[1:2] + row_ref[2:3]).astype(bf16)
        return 0

    lax.fori_loop(0, CHUNKS, first, 0)
    save(1).start()
    save(2).start()
    run(middle)

    def staged(step):
        t, i = step // CHUNKS, step % CHUNKS
        s = pl.ds(pl.multiple_of(i * ROWS, ROWS), ROWS)
        return pltpu.make_async_copy(stage.at[step % 2], gp_out.at[t, s, :], stage_sem.at[step % 2])

    def hidden(step, _):
        t, i = step // CHUNKS, step % CHUNKS
        s = pl.ds(pl.multiple_of(i * ROWS, ROWS), ROWS)
        z = nn(h1_ref[s, :], w1[t]) + hb_ref[t]
        cdf = 0.5 + 0.5 * lax.erf(z * 0.5**0.5)
        g_ref[t, s, :] = (z * cdf).astype(bf16)

        @pl.when(step >= 2)
        def _():
            staged(step - 2).wait()

        stage[step % 2] = cdf + z * (jnp.exp(-0.5 * z * z) * 0.3989422804014327)
        staged(step).start()
        at_step(step, late)
        return 0

    lax.fori_loop(0, NT * CHUNKS, hidden, 0)
    staged(NT * CHUNKS - 2).wait()
    staged(NT * CHUNKS - 1).wait()
    for i in (3, 8, 9):
        save(i).start()
    gain_ref[...] = jnp.zeros_like(gain_ref)
    pool[...] = jnp.zeros_like(pool)

    def second(i, _):
        s = pl.ds(pl.multiple_of(i * ROWS, ROWS), ROWS)
        res = xhat1_ref[s, :] * row_ref[1:2] + row_ref[2:3] + row_ref[3:4]
        for t in range(NT):
            res = res + nt(g_ref[t, s, :], w2[t])
        xhat, rstd = norm(res)
        xhat2_ref[s, :] = xhat
        rstd2_ref[s, :] = rstd
        y = xhat * row_ref[4:5] + row_ref[5:6]
        out_ref[s, :] = y.astype(bf16)
        here = i * ROWS + lax.broadcasted_iota(jnp.int32, (ROWS, 1), 0) < length
        pool[0:1] += jnp.sum(jnp.where(here, y, 0.0), axis=0, keepdims=True)
        gain_ref[...] += jnp.sum(jnp.where(here, xhat, 0.0), axis=0, keepdims=True)
        return 0

    lax.fori_loop(0, CHUNKS, second, 0)
    size = jnp.full((1, 1), length).astype(f32)
    mean = pool[0:1] / size
    pool_own[...] = jnp.zeros_like(pool_own)
    for i in range(D // 128):
        pool_own[i : i + 1, :] = mean[:, i * 128 : i * 128 + 128]
    if comm:
        begin(pools)
    save(0).start()
    save(4).start()
    if comm:
        run(pools.flow()[:-1])
        end(pools)
        for i in range(dp):
            for t in range(NT):
                for k in range(D // 128):
                    pooled[i * NT + t : i * NT + t + 1, k * 128 : k * 128 + 128] = every[t, i * 16 + k : i * 16 + k + 1, :]
        u_ref[...] = loss_pull(pooled[...], groups_ref[...], lax.axis_index("dp") * NT + lax.axis_index("tensor")) / size
        for g in parts + (pools,):
            g.finish()
    else:
        u_ref[...] = mean
    for h in range(H):
        for i, (src, dst) in enumerate(kept):
            pltpu.make_async_copy(src.at[h], dst.at[h], q_sem.at[i, h]).wait()
    for i in range(len(saved)):
        save(i).wait()


def forward(length, groups, x, weights, n, cb, comm):
    s = jax.ShapeDtypeStruct
    dp = 2 * n
    r = D // dp
    dma = pltpu.SemaphoreType.DMA
    shapes = [s((LEN, 1), f32), s((LEN, 1), f32), s((1, D), f32), s((16, D), f32), s((NT, 1, D), f32), s((1, D), f32)]
    big = [s((LEN, D), bf16), s((LEN, D), bf16), s((LEN, D), f32), s((NT, LEN, D), bf16), s((LEN, D), f32), s((D, LEN), bf16), s((D, LEN), bf16)]
    kept = [
        s((NT, LEN, D), f32), s((H, AUG, LEN), bf16), s((H, AUG, LEN), bf16), s((H, HD, LEN), bf16),
        s((NJ, NT, D, 4 * HD), bf16), s((NT, D, D), bf16), s((NT, D, D), bf16),
    ]
    scratch = [pltpu.VMEM(v.shape, v.dtype) for v in big] + [
        pltpu.VMEM((NJ, NT, D, 4 * HD), bf16), pltpu.VMEM((NT, D, D), bf16), pltpu.VMEM((NT, D, D), bf16),
        pltpu.VMEM((NT, dp * 32, 128), bf16), pltpu.VMEM((NT, 2 * HC, 1), f32), pltpu.VMEM((NT, 8, dp * cb), f32),
        pltpu.VMEM((H, AUG, LEN), bf16), pltpu.VMEM((H, AUG, LEN), bf16), pltpu.VMEM((H, HD, LEN), bf16),
        pltpu.VMEM((2, LEN, AUG), bf16), pltpu.VMEM((2, LEN, LEN // 2), f32),
        pltpu.VMEM((D, D), bf16), pltpu.VMEM((8, D), f32), pltpu.VMEM((2, ROWS, D), f32),
        pltpu.VMEM((16, 128), f32), pltpu.VMEM((NT, dp * 16, 128), f32), pltpu.VMEM((dp * NT, D), f32),
        dma((PARTS,)), dma((3, H)), dma((2,)), dma((len(big) + 3,)),
    ]
    if comm:
        scratch += [pltpu.VMEM((NJ, r, 4 * HD), bf16), pltpu.VMEM((32, 128), bf16), pltpu.VMEM((r, D), bf16), pltpu.VMEM((r, D), bf16)]
        scratch += gather_sems(PARTS, n)
        params = pltpu.CompilerParams(collective_id=0, has_side_effects=True, vmem_limit_bytes=VMEM_CAP)
    else:
        params = pltpu.CompilerParams(vmem_limit_bytes=VMEM_CAP)
    return pl.pallas_call(
        functools.partial(forward_kernel, n, cb, comm),
        out_shape=shapes + big + kept,
        in_specs=[pl.BlockSpec(memory_space=pltpu.SMEM)] + vmem_spec(2) + (vmem_spec(6) if comm else any_spec(4)),
        out_specs=vmem_spec(len(shapes)) + any_spec(len(big) + len(kept)),
        scratch_shapes=scratch,
        compiler_params=params,
    )(length, groups, x, *weights)


def feed_back_kernel(
    len_ref, u_ref, gain_ref, xhat2_ref, rstd2_ref, row_ref, w1_ref, w2_ref, g_ref, gp_ref, h1_ref,
    gw1_ref, gw2_ref, dh_ref, ghb_ref, grow_ref,
    df_ref, dft_ref, h1t_ref, dz_ref,
):
    @pl.when(pl.program_id(0) == 0)
    def _():
        length = len_ref[0]
        u = u_ref[...]
        du = u * row_ref[4:5]
        mean_du = jnp.mean(du, axis=1, keepdims=True)
        h1t_ref[...] = h1_ref[...].T
        grow_ref[...] = jnp.zeros_like(grow_ref)

        def rows(i, _):
            s = pl.ds(pl.multiple_of(i * ROWS, ROWS), ROWS)
            here = i * ROWS + lax.broadcasted_iota(jnp.int32, (ROWS, 1), 0) < length
            xhat = xhat2_ref[s, :]
            dot = jnp.mean(xhat * du, axis=1, keepdims=True)
            dr = jnp.where(here, rstd2_ref[s, :] * (du - mean_du - xhat * dot), 0.0)
            dh_ref[s, :] = dr
            low = dr.astype(bf16)
            df_ref[s, :] = low
            grow_ref[3:4] += jnp.sum(low.astype(f32), axis=0, keepdims=True)
            return 0

        lax.fori_loop(0, CHUNKS, rows, 0)
        grow_ref[4:5] = u * gain_ref[...]
        grow_ref[5:6] = u * jnp.full((1, 1), length).astype(f32)
        dft_ref[...] = df_ref[...].T

    hb = jnp.zeros((1, D), f32)
    for i in range(CHUNKS):
        s = pl.ds(i * ROWS, ROWS)
        dz = (nn(df_ref[s, :], w2_ref[0]) * gp_ref[0, s, :]).astype(bf16)
        dz_ref[s, :] = dz
        hb = hb + jnp.sum(dz.astype(f32), axis=0, keepdims=True)
        dh_ref[s, :] += nt(dz, w1_ref[0])
    ghb_ref[0] = hb
    gw1_ref[0] = nn(h1t_ref[...], dz_ref[...]).astype(bf16)
    gw2_ref[0] = nn(dft_ref[...], g_ref[0]).astype(bf16)


def feed_back(length, u, gain, xhat2, rstd2, row, w1, w2, g, gp, h1):
    s = jax.ShapeDtypeStruct

    def part(rows):
        return pl.BlockSpec((1, rows, D), lambda t: (t, 0, 0))

    def all_of(*shape):
        return pl.BlockSpec(shape, lambda t: (0,) * len(shape))

    return pl.pallas_call(
        feed_back_kernel,
        grid=(NT,),
        out_shape=[s((NT, D, D), bf16), s((NT, D, D), bf16), s((LEN, D), f32), s((NT, 1, D), f32), s((16, D), f32)],
        in_specs=[pl.BlockSpec(memory_space=pltpu.SMEM), all_of(1, D), all_of(1, D), all_of(LEN, D), all_of(LEN, 1), all_of(16, D),
                  part(D), part(D), part(LEN), part(LEN), all_of(LEN, D)],
        out_specs=[part(D), part(D), all_of(LEN, D), part(1), all_of(16, D)],
        scratch_shapes=[pltpu.VMEM((LEN, D), bf16), pltpu.VMEM((D, LEN), bf16), pltpu.VMEM((D, LEN), bf16), pltpu.VMEM((LEN, D), bf16)],
        compiler_params=pltpu.CompilerParams(vmem_limit_bytes=VMEM_CAP),
    )(length, u, gain, xhat2, rstd2, row, w1, w2, g, gp, h1)


def backward_kernel(n, cb, comm, *refs):
    dp = 2 * n
    r = D // dp
    (row_ref, rstd_ref, ghb_ref, grow_in, ct_ref, xt, dh_in, xhat_in, wa_in, q_in, k_in, v_in, gw1_in, gw2_in,
     dx_ref, *rest) = refs
    outs, rest = rest[: NJ + 3], rest[NJ + 3 :]
    (wa, qkv, dat, dct, dqkv, wcat, dxt, s_ref, d_ref, p_ref, ds_ref, grow, gcol, gbias, load, q_sem, *rest) = rest
    hooks = {}
    grads = [wa.at[j] for j in range(NJ)]
    if comm:
        own1, own2, *rest = rest
        bufs, sems = rest[:-8], rest[-8:]
        p = Place(n)
        enter(p)
        parts = []
        for i, (rows, src, slab) in enumerate(
            [(r, lambda t: gw1_in.at[t], lambda y: own1.at[y]), (r, lambda t: gw2_in.at[t], lambda y: own2.at[y])]
            + [(r, lambda t, g=g: g.at[t], lambda y, g=g: g.at[y * 2 + p.c]) for g in grads]
            + [(32, lambda t: gbias.at[t], lambda y: gbias.at[y * 2 + p.c])]
        ):
            parts.append(Scatter(p, i, rows, src, slab, outs[i], bufs[4 * i : 4 * i + 4], sems))
        up, down, a0, a1, a2, bias = parts
        up.core()
        down.core()
        owns = [
            pltpu.make_async_copy(src.at[y * 2 + p.c], dst.at[y], load.at[3 + 2 * i + y])
            for i, (src, dst) in enumerate(((gw1_in, own1), (gw2_in, own2))) for y in range(2)
        ]
        hooks = {
            0: [down.corner], 2: [up.cross], 3: [a0.core], 4: [down.cross], 5: [a0.corner], 6: [up.line], 7: [a1.core],
            8: [a0.cross], 9: [down.line, up.last, a1.corner], 10: [a0.line], 11: [a1.cross, a2.core],
        }
    else:
        owns = []
    loads = [
        pltpu.make_async_copy(dh_in, s_ref.at[:, 0:D], load.at[0]), pltpu.make_async_copy(xhat_in, d_ref.at[:, 0:D], load.at[1]),
        pltpu.make_async_copy(wa_in, wa, load.at[2]),
    ]
    for cp in loads + owns:
        cp.start()

    def fetch(h, slot):
        return [
            pltpu.make_async_copy(src.at[h], qkv.at[slot, i, 0 : src.shape[1], :], q_sem.at[slot, i])
            for i, src in enumerate((q_in, k_in, v_in))
        ]

    for cp in fetch(0, 0):
        cp.start()
    dxt[...] = jnp.zeros_like(dxt)
    grow[...] = grow_in[...]
    loads[0].wait()
    loads[1].wait()

    def first(i, _):
        s = pl.ds(pl.multiple_of(i * ROWS, ROWS), ROWS)
        dh = s_ref[s, 0:D]
        xhat = d_ref[s, 0:D]
        grow[1:2] += jnp.sum(dh * xhat, axis=0, keepdims=True)
        grow[2:3] += jnp.sum(dh, axis=0, keepdims=True)
        dn = dh * row_ref[1:2]
        dr = rstd_ref[s, :] * (dn - jnp.mean(dn, axis=1, keepdims=True) - xhat * jnp.mean(dn * xhat, axis=1, keepdims=True))
        dx_ref[s, :] = dr
        low = dr.astype(bf16)
        grow[0:1] += jnp.sum(low.astype(f32), axis=0, keepdims=True)
        dat[:, s] = low.T
        return 0

    for i in range(CHUNKS):
        first(i, 0)
    loads[2].wait()
    for cp in owns:
        cp.wait()
    for j in range(NJ):
        for t in range(NT):
            h = j * NT + t
            wcat[:, h * HD : h * HD + HD] = wa[j, t, :, 3 * HD : 4 * HD]
    for i in range(D // ROWS):
        s = slice(i * ROWS, (i + 1) * ROWS)
        dct[s, :] = tn(wcat[:, s], dat[...]).astype(bf16)
        gwo = nt(dat[s, :], ct_ref[...]).astype(bf16)
        for j in range(NJ):
            for t in range(NT):
                h = j * NT + t
                wa[j, t, s, 3 * HD : 4 * HD] = gwo[:, h * HD : h * HD + HD]
    if comm:
        up.corner()

    def head(h, _):
        j, t = h // NT, h % NT
        slot = h % 2
        for cp in fetch(h, slot):
            cp.wait()

        @pl.when(h + 1 < H)
        def _():
            for cp in fetch(h + 1, 1 - slot):
                cp.start()

        own = pl.ds(pl.multiple_of(h * HD, HD), HD)
        prob = jnp.exp(tn(qkv[slot, 1], qkv[slot, 0]))
        s_ref[...] = prob
        d_ref[...] = tn(qkv[slot, 2, 0:HD, :], dct[own, :])
        p_ref[...] = prob.astype(bf16)
        inner = jnp.sum(s_ref[...] * d_ref[...], axis=0, keepdims=True)
        ds_ref[...] = (s_ref[...] * (d_ref[...] - inner)).astype(bf16)
        at = pl.multiple_of(t * 3 * HD, HD)
        dqkv[pl.ds(at, HD), :] = (nn(qkv[slot, 1, 0:HD, :], ds_ref[...]) * HD**-0.5).astype(bf16)
        dqkv[pl.ds(at + HD, HD), :] = nt(qkv[slot, 0, 0:HD, :], ds_ref[...]).astype(bf16)
        dqkv[pl.ds(at + 2 * HD, HD), :] = nt(dct[own, :], p_ref[...]).astype(bf16)

        @pl.when(t == NT - 1)
        def _():
            for k in range(NT):
                wcat[:, k * 3 * HD : (k + 1) * 3 * HD] = wa[j, k, :, 0 : 3 * HD]
            sums = nt(jnp.ones((16, LEN), bf16), dqkv[...])
            for k in range(NT):
                gcol[j, k] = sums[0:8, k * 3 * HD : (k + 1) * 3 * HD]
            for i in range(D // ROWS):
                s = slice(i * ROWS, (i + 1) * ROWS)
                dxt[s, :] += nn(wcat[s, :], dqkv[...])
                g = nt(xt[s, :], dqkv[...]).astype(bf16)
                for k in range(NT):
                    wa[j, k, s, 0 : 3 * HD] = g[:, k * 3 * HD : (k + 1) * 3 * HD]

        at_step(h, hooks)
        return 0

    lax.fori_loop(0, H, head, 0)

    col_rows = -(-cb // r)
    cols = []
    for t in range(NT):
        pieces = [gcol[j, t, 0:1, 0:HD] for j in range(NJ)] + [gcol[j, t, 0:1, 2 * HD : 3 * HD] for j in range(NJ)]
        cols.append(jnp.concatenate(pieces + [ghb_ref[t]], axis=1))
    at = lax.broadcasted_iota(jnp.int32, (32, 128), 0)
    for i in range(dp):
        rows = jnp.pad(grow[0:8, i * r : i * r + r], ((0, 24), (0, 128 - r)))
        for t in range(NT):
            block = jnp.where(at < 6, rows, 0.0)
            for k in range(col_rows):
                wide = min(r, cb - k * r)
                piece = cols[t][:, i * cb + k * r : i * cb + k * r + wide]
                block = jnp.where(at == 6 + k, jnp.pad(piece, ((0, 0), (0, 128 - wide))), block)
            gbias[t, i * 32 : i * 32 + 32, :] = block.astype(bf16)
    if comm:
        bias.core()
    for i in range(CHUNKS):
        s = pl.ds(i * ROWS, ROWS)
        dx_ref[s, :] += dxt[:, s].T
    if comm:
        a2.corner()
        bias.corner()
        down.last()
        a0.last()
        a1.line()
        a2.cross()
        bias.cross()
        a1.last()
        a2.line()
        bias.line()
        a2.last()
        bias.last()
        for part in parts:
            part.finish()
    else:
        copies = [pltpu.make_async_copy(src, dst, load.at[i]) for i, (src, dst) in enumerate(zip(grads + [gbias], outs))]
        for cp in copies:
            cp.start()
        for cp in copies:
            cp.wait()


def backward(row, rstd1, ghb, grow, ct, xt, dh, xhat1, wa, qt, kt, vt, gw1, gw2, n, cb, comm):
    s = jax.ShapeDtypeStruct
    dp = 2 * n
    r = D // dp
    dma = pltpu.SemaphoreType.DMA
    if comm:
        widths = [(r, D), (r, D)] + [(r, 4 * HD)] * NJ + [(32, 128)]
        sums = [s(shape, f32) for shape in widths]
        sum_specs = vmem_spec(len(sums))
    else:
        widths = []
        sums = [s((NT, D, 4 * HD), bf16)] * NJ + [s((NT, dp * 32, 128), bf16)] + [s((8, 128), f32)] * 2
        sum_specs = any_spec(len(sums))
    scratch = [
        pltpu.VMEM((NJ, NT, D, 4 * HD), bf16), pltpu.VMEM((2, 3, AUG, LEN), bf16), pltpu.VMEM((D, LEN), bf16), pltpu.VMEM((D, LEN), bf16),
        pltpu.VMEM((D, LEN), bf16), pltpu.VMEM((D, D), bf16), pltpu.VMEM((D, LEN), f32),
        pltpu.VMEM((LEN, LEN), f32), pltpu.VMEM((LEN, LEN), f32), pltpu.VMEM((LEN, LEN), bf16), pltpu.VMEM((LEN, LEN), bf16),
        pltpu.VMEM((16, D), f32), pltpu.VMEM((NJ, NT, 8, 3 * HD), f32), pltpu.VMEM((NT, dp * 32, 128), bf16),
        dma((7,)), dma((2, 3)),
    ]
    if comm:
        scratch += [pltpu.VMEM((2, D, D), bf16)] * 2
        for rows, wide in widths:
            scratch += scatter_bufs(n, rows, wide)
        scratch += scatter_sems(len(widths), n)
        params = pltpu.CompilerParams(collective_id=1, has_side_effects=True, vmem_limit_bytes=VMEM_CAP)
    else:
        params = pltpu.CompilerParams(vmem_limit_bytes=VMEM_CAP)
    return pl.pallas_call(
        functools.partial(backward_kernel, n, cb, comm),
        out_shape=[s((LEN, D), f32)] + sums,
        in_specs=vmem_spec(6) + any_spec(8),
        out_specs=vmem_spec(1) + sum_specs,
        scratch_shapes=scratch,
        compiler_params=params,
    )(row, rstd1, ghb, grow, ct, xt, dh, xhat1, wa, qt, kt, vt, gw1, gw2)


def adam_kernel(cb, *refs):
    sums, refs = refs[:6], refs[6:]
    old, new = refs[:24], refs[24:]
    gw1, gw2, ga, gbias = sums[0], sums[1], sums[2:5], sums[5]
    r = gw1.shape[0]

    def wide(k):
        return jnp.concatenate([ga[j][:, k * HD : k * HD + HD] for j in range(NJ)], axis=1)

    def update(i, grad, rate, at=()):
        where = at + (Ellipsis,)
        out = adam_update(*[old[4 * i + k][where] for k in range(4)], grad, rate)
        for k, v in enumerate(out):
            new[4 * i + k][where] = v

    for k in range(3):
        update(0, wide(k), D ** (-0.5), (k,))
    high = -(-r // 128) * 128
    turned = jnp.concatenate([wide(3), jnp.zeros((r, 256 - HC), f32)], axis=1)
    if high > r:
        turned = jnp.concatenate([turned, jnp.zeros((high - r, 256), f32)], axis=0)
    update(1, turned.T[0:HC, 0:r], D ** (-0.5))
    update(2, gw1[...], D ** (-0.5))
    update(3, gw2[...], FF ** (-0.5))
    rows = gbias[...]
    pieces = [rows[6 + k : 7 + k, 0 : min(r, cb - k * r)] for k in range(-(-cb // r))]
    update(4, jnp.concatenate(pieces, axis=1), 0.1)
    update(5, rows[0:6, 0:r], 0.15)


def adam(sums, olds, cb):
    flat = [v for group in olds for v in group]
    s = jax.ShapeDtypeStruct
    shapes = [s(group[0].shape, f32) for group in olds for _ in range(4)]
    return pl.pallas_call(
        functools.partial(adam_kernel, cb),
        out_shape=shapes,
        in_specs=vmem_spec(6 + 24),
        out_specs=vmem_spec(24),
        compiler_params=pltpu.CompilerParams(vmem_limit_bytes=VMEM_CAP),
    )(*sums, *flat)


def gather_plain(own):
    return lax.all_gather(lax.all_gather(own, "dp", axis=0, tiled=True), "tensor", axis=0)


def scatter_plain(full):
    own = lax.psum_scatter(full.astype(f32), "tensor", scatter_dimension=0, tiled=False)
    return lax.psum_scatter(own, "dp", scatter_dimension=0, tiled=True)


def by_head(wide):
    return jnp.moveaxis(wide.reshape(*wide.shape[:-1], NJ, HD), -2, 0)


def packed(qkv_weight, out_weight, up_weight, down_weight, col_bias, row_params, r, cb):
    own_a = jnp.concatenate([by_head(qkv_weight[i]) for i in range(3)] + [by_head(out_weight.T)], axis=-1).astype(bf16)
    col_rows = -(-cb // r)
    col_pad = jnp.pad(col_bias[0], (0, col_rows * r - cb)).reshape(col_rows, r)
    own_b = jnp.pad(jnp.concatenate([row_params, col_pad], axis=0), ((0, 26 - col_rows), (0, 128 - r))).astype(bf16)
    return own_a, own_b, up_weight.astype(bf16), down_weight.T.astype(bf16)


def on_device(
    inputs, lengths, groups, qkv_weight, out_weight, up_weight, down_weight, col_bias, row_params,
    qkv_first, out_first, up_first, down_first, col_first, row_first,
    qkv_second, out_second, up_second, down_second, col_second, row_second,
    qkv_ema, out_ema, up_ema, down_ema, col_ema, row_ema,
):
    dp = lax.axis_size("dp")
    n = dp // 2
    r = D // dp
    cb = col_bias.shape[1]
    length = lax.dynamic_slice_in_dim(lengths, lax.axis_index("tensor"), 1)
    comm = r % 32 == 0
    if comm:
        weights = (qkv_weight, out_weight, up_weight, down_weight.T, col_bias, row_params)
    else:
        own_a, *others = packed(qkv_weight, out_weight, up_weight, down_weight, col_bias, row_params, r, cb)
        own_b, own_1, own_2 = [gather_plain(v) for v in others]
        weights = (jnp.stack([gather_plain(own_a[j]) for j in range(NJ)]), own_b, own_1, own_2)
    (rstd1, rstd2, gain, row, hb, u, outputs, h1, xhat1, g, xhat2, ct, xt, gp, qt, kt, vt, wa, w1, w2) = forward(
        length, groups, inputs, weights, n, cb, comm
    )
    if not comm:
        every = lax.all_gather(u, ("dp", "tensor"), axis=0, tiled=True)
        u = loss_pull(every, groups, lax.axis_index(("dp", "tensor"))) / length[0].astype(f32)

    gw1, gw2, dh, ghb, grow = feed_back(length, u, gain, xhat2, rstd2, row, w1, w2, g, gp, h1)
    input_grad, *sums = backward(row, rstd1, ghb, grow, ct, xt, dh, xhat1, wa, qt, kt, vt, gw1, gw2, n, cb, comm)
    if not comm:
        sums = [scatter_plain(v) for v in (gw1, gw2, *sums[: NJ + 1])]
    olds = (
        (qkv_weight, qkv_first, qkv_second, qkv_ema),
        (out_weight, out_first, out_second, out_ema),
        (up_weight, up_first, up_second, up_ema),
        (down_weight.T, down_first.T, down_second.T, down_ema.T),
        (col_bias, col_first, col_second, col_ema),
        (row_params, row_first, row_second, row_ema),
    )
    new = list(adam(sums, olds, cb))
    new[12:16] = [v.T for v in new[12:16]]
    return (outputs, input_grad, *new)


def solution(mesh):
    tokens = P(("dp", "tensor"), None)
    placed = (P(None, "dp", "tensor"), P("tensor", "dp"), P("dp", "tensor"), P("tensor", "dp"), P("tensor", "dp"), P(None, "dp"))
    new = tuple(spec for spec in placed for _ in range(4))
    return jax.shard_map(
        on_device,
        mesh=mesh,
        in_specs=(tokens, P("dp"), P()) + placed * 4,
        out_specs=(tokens, tokens) + new,
        check_vma=False,
    )
```

```python
import functools

import jax
import jax.numpy as jnp
from jax import lax
from jax.experimental import pallas as pl
from jax.experimental.pallas import tpu as pltpu
from jax.sharding import PartitionSpec as P

D = 768
H = 12
HD = 64
FF = 3072
LEN = 1024
STEP = 5
NT = 4
HC = D // NT
AUG = 80

MESH = pl.DeviceIdType.MESH
f32 = jnp.float32
bf16 = jnp.bfloat16
highest = lax.Precision.HIGHEST
eps_norm = 1e-05
temper = 40.0
masked = -1000000000.0
beta_one = 0.5
beta_two = 0.5
adam_eps = 1e-08
decay_rate = 0.01
ema_keep = 0.9
VMEM_CAP = 60 << 20


def nn(a, b):
    return jnp.dot(a, b, preferred_element_type=f32)


def nt(a, b):
    return lax.dot_general(a, b, (((1,), (1,)), ((), ())), preferred_element_type=f32)


def tn(a, b):
    return lax.dot_general(a, b, (((0,), (0,)), ((), ())), preferred_element_type=f32)


def adam_update(weight, first_old, second, ema_old, gradient, step_rate):
    first_new = beta_one * first_old + (1 - beta_one) * gradient
    second_new = beta_two * second + (1 - beta_two) * gradient * gradient
    first_hat = first_new / (1 - beta_one**STEP)
    second_hat = second_new / (1 - beta_two**STEP)
    weight_new = weight - step_rate * (
        first_hat / (jnp.sqrt(second_hat) + adam_eps) + decay_rate * weight
    )
    ema_new = ema_keep * ema_old + (1 - ema_keep) * weight_new
    return (first_new, second_new, weight_new, ema_new)


class Place:
    def __init__(self, depth):
        dp = lax.axis_index("dp")
        t = lax.axis_index("tensor")
        self.depth = depth
        self.z, self.x, self.y, self.c = dp // 2, dp % 2, t // 2, t % 2
        self.me = (self.z, self.x, self.y, self.c)
        self.over_x = (self.z, 1 - self.x, self.y, self.c)
        self.over_y = (self.z, self.x, 1 - self.y, self.c)
        self.over_xy = (self.z, 1 - self.x, 1 - self.y, self.c)
        self.over_c = (self.z, self.x, self.y, 1 - self.c)

    def along_z(self, k):
        return ((self.z + k) % self.depth, self.x, self.y, self.c)


def device(place):
    z, x, y, c = place
    return (z * 2 + x, y * 2 + c)


def enter(p):
    bar = pltpu.get_barrier_semaphore()
    to = [p.over_x, p.over_y, p.over_c] + [p.along_z(k) for k in range(1, p.depth)]
    for place in to:
        pl.semaphore_signal(bar, inc=1, device_id=device(place), device_id_type=MESH)
    pl.semaphore_wait(bar, len(to))


def remote(src, dst, send, recv, to):
    return pltpu.make_async_remote_copy(
        src_ref=src, dst_ref=dst, send_sem=send, recv_sem=recv, device_id=device(to), device_id_type=MESH
    )


class Gather:
    def __init__(self, p, part, full, sems, straight=False):
        self.p, self.part, self.full, self.straight = p, part, full, straight
        self.rows = full.shape[1] // (2 * p.depth)
        self.recv, self.pair_recv, self.sz, self.sx, self.sy, self.sk, self.sc = sems

    def spot(self, place, wide=1):
        z, x, y, c = place
        r = self.rows
        step = 32 // self.full.dtype.itemsize
        return self.full.at[y * 2 + c, pl.ds(pl.multiple_of((z * 2 + x) * r, step), wide * r), :]

    def copy(self, place, to, send):
        z, x, y, c = place
        ref = self.spot(place)
        return remote(ref, ref, send.at[self.part], self.recv.at[self.part, (z * 2 + x) * 4 + y * 2 + c], to)

    def pair_copy(self, z, y, c):
        ref = self.spot((z, 0, y, c), 2)
        return remote(ref, ref, self.sc.at[self.part], self.pair_recv.at[self.part, z * 2 + y], self.p.over_c)

    def send(self, place, to, send, when=None):
        def start():
            self.copy(place(), to, send).start()

        if when is not None:
            pl.when(when())(start)
        else:
            start()

    def start(self):
        p, n = self.p, self.p.depth

        def me():
            return p.me

        if self.straight:
            for k in range(1, n):
                self.send(me, p.along_z(k), self.sz)
        else:
            self.send(me, p.along_z(1), self.sz, lambda: p.z + 1 < n)
            self.send(me, p.along_z(-1), self.sz, lambda: p.z > 0)
        self.send(me, p.over_x, self.sx)
        self.send(me, p.over_y, self.sy)

    def sides(self, k):
        p, n = self.p, self.p.depth
        if k == 0:
            return [(0, None)]
        if self.straight:
            return [(1, None)]
        return [(-1, lambda: p.z >= k), (1, lambda: p.z + k < n)]

    def each(self, k, step):
        for sign, when in self.sides(k):
            go = functools.partial(step, sign, sign * k)
            if when is not None:
                pl.when(when())(go)
            else:
                go()

    def arrived(self, place):
        self.copy(place, self.p.over_c, self.sx).wait_recv()

    def at(self, k, x, y):
        return ((self.p.z + k) % self.p.depth, x, y, self.p.c)

    def line(self, k):
        p, n = self.p, self.p.depth

        def step(sign, far):
            place = functools.partial(self.at, far, p.x, p.y)
            self.arrived(place())
            if not self.straight:
                self.send(place, p.along_z(-sign), self.sz, (lambda: p.z + 1 < n) if sign < 0 else (lambda: p.z > 0))
            self.send(place, p.over_x, self.sx)
            self.send(place, p.over_y, self.sy)

        self.each(k, step)

    def cross(self, k):
        p = self.p

        def step(sign, far):
            self.arrived(self.at(far, 1 - p.x, p.y))
            self.arrived(self.at(far, p.x, 1 - p.y))
            z = (p.z + far) % p.depth
            odd = (z + self.part) % 2
            x, y = jnp.where(odd == 1, p.x, 1 - p.x), jnp.where(odd == 1, 1 - p.y, p.y)
            to = (p.z, jnp.where(odd == 1, 1 - p.x, p.x), jnp.where(odd == 1, p.y, 1 - p.y), p.c)
            self.copy((z, x, y, p.c), to, self.sk).start()
            self.pair_copy(z, p.y, p.c).start()

        self.each(k, step)

    def corner(self, k):
        p = self.p

        def step(sign, far):
            self.arrived(self.at(far, 1 - p.x, 1 - p.y))
            self.pair_copy((p.z + far) % p.depth, 1 - p.y, p.c).start()

        self.each(k, step)

    def other_core(self):
        for z in range(self.p.depth):
            for y in range(2):
                self.pair_copy(z, y, 1 - self.p.c).wait_recv()

    def flow(self):
        n = self.p.depth
        steps = [functools.partial(self.cross, 0)]
        order = [1, n - 1] + list(range(2, n - 1)) if self.straight and n > 2 else list(range(1, n))
        for k in order:
            steps += [functools.partial(self.line, k), functools.partial(self.cross, k)]
        steps += [functools.partial(self.corner, k) for k in range(n)]
        steps.append(self.other_core)
        return steps

    def finish(self):
        n, r = self.p.depth, self.rows

        def left(ref, sem):
            pltpu.make_async_copy(ref, ref, sem.at[self.part]).wait()

        for sem in (self.sx, self.sy, self.sk):
            left(self.full.at[0, 0 : n * r, :], sem)
        left(self.full.at[0:2], self.sc)
        if self.straight:
            left(self.full.at[0, 0 : (n - 1) * r, :], self.sz)
        else:
            for z in range(n):
                count = (z + 1 if z + 1 < n else 0) + (n - z if z > 0 else 0)
                if count:
                    pl.when(self.p.z == z)(functools.partial(left, self.full.at[0, 0 : count * r, :], self.sz))


def gather_sems(parts, n):
    dma = pltpu.SemaphoreType.DMA
    return [dma((parts, 8 * n)), dma((parts, 2 * n))] + [dma((parts,))] * 5


class Scatter:
    def __init__(self, p, part, rows, grads, out, bufs, temp, load, sems):
        self.p, self.part, self.rows, self.grads, self.out, self.temp, self.load = p, part, rows, grads, out, temp, load
        self.b_core, self.b_corner, self.b_cross, self.b_line = bufs
        self.ss, self.rs, self.sc, self.rc, self.sx, self.rx, self.sl, self.rl = sems

    def slab(self, y):
        return self.grads(y * 2 + self.p.c)

    def span(self, z, x):
        return pl.ds(pl.multiple_of((z * 2 + x) * self.rows, 16), self.rows)

    def which(self, k):
        return self.p.y if k else 1 - self.p.y

    def core_copy(self, k):
        p, q = self.p, self.part
        return remote(self.grads(self.which(k) * 2 + 1 - p.c), self.b_core.at[k], self.ss.at[q], self.rs.at[q, k], p.over_c)

    def core(self, k):
        self.core_copy(k).start()

    def add(self, k):
        r = self.rows
        self.core_copy(k).wait_recv()
        slab = self.slab(self.which(k))
        cp = pltpu.make_async_copy(self.b_core.at[k], self.temp, self.load)
        cp.start()
        cp.wait()

        def one(i, _):
            s = pl.ds(pl.multiple_of(i * r, 16), r)
            slab[s, :] = (slab[s, :].astype(f32) + self.temp[s, :].astype(f32)).astype(bf16)
            return 0

        lax.fori_loop(0, 2 * self.p.depth, one, 0)

    def corner_copy(self, z):
        p, q = self.p, self.part
        src = self.slab(1 - p.y).at[self.span(z, 1 - p.x), :]
        return remote(src, self.b_corner.at[z], self.sc.at[q], self.rc.at[q, z], p.over_x if (z + q) % 2 else p.over_y)

    def corner(self):
        for z in range(self.p.depth):
            self.corner_copy(z).start()

    def cross_copy(self, z, way):
        p, q = self.p, self.part
        src = self.slab(1 - p.y).at[self.span(z, p.x), :] if way else self.slab(p.y).at[self.span(z, 1 - p.x), :]
        to = p.over_y if way else p.over_x
        return remote(src, self.b_cross.at[way, z], self.sx.at[q], self.rx.at[q, way, z], to)

    def cross(self):
        p = self.p
        for z in range(p.depth):
            self.corner_copy(z).wait_recv()
            slab, s = (self.slab(1 - p.y), self.span(z, p.x)) if (z + self.part) % 2 else (self.slab(p.y), self.span(z, 1 - p.x))
            slab[s, :] = (slab[s, :].astype(f32) + self.b_corner[z].astype(f32)).astype(bf16)
            for way in range(2):
                self.cross_copy(z, way).start()

    def line_copy(self, k):
        p, q = self.p, self.part
        z = (p.z + k) % p.depth
        return remote(self.slab(p.y).at[self.span(z, p.x), :], self.b_line.at[k], self.sl.at[q], self.rl.at[q, k], p.along_z(k))

    def column(self, z):
        p = self.p
        for way in range(2):
            self.cross_copy(z, way).wait_recv()
        return self.slab(p.y)[self.span(z, p.x), :].astype(f32) + self.b_cross[0, z].astype(f32) + self.b_cross[1, z].astype(f32)

    def line(self):
        p = self.p
        for k in range(1, p.depth):
            z = (p.z + k) % p.depth
            self.slab(p.y)[self.span(z, p.x), :] = self.column(z).astype(bf16)
            self.line_copy(k).start()

    def last(self):
        p = self.p
        total = self.column(p.z)
        for k in range(1, p.depth):
            self.line_copy(k).wait_recv()
            total = total + self.b_line[k].astype(f32)
        self.out[...] = total

    def finish(self):
        q = self.part
        for ref, sem in ((self.b_core, self.ss), (self.b_corner, self.sc), (self.b_cross, self.sx), (self.b_line.at[1 : self.p.depth], self.sl)):
            pltpu.make_async_copy(ref, ref, sem.at[q]).wait()


def scatter_bufs(n, rows, width):
    return [pltpu.VMEM((n, rows, width), bf16), pltpu.VMEM((2, n, rows, width), bf16), pltpu.VMEM((n, rows, width), bf16)]


def scatter_sems(parts, n):
    dma = pltpu.SemaphoreType.DMA
    return [dma((parts,)), dma((parts, 2)), dma((parts,)), dma((parts, n)), dma((parts,)), dma((parts, 2, n)), dma((parts,)), dma((parts, n))]


def split3(row):
    hi = row.astype(bf16).astype(f32)
    mid = (row - hi).astype(bf16).astype(f32)
    return hi, mid, row - hi - mid


def aug_rows(*rows):
    width = rows[0].shape[1]
    at = lax.broadcasted_iota(jnp.int32, (16, width), 0)
    out = jnp.zeros((16, width), f32)
    for i, row in enumerate(rows):
        out = jnp.where(at == i, row, out)
    return out.astype(bf16)


def norm(r):
    cent = r - jnp.mean(r, axis=1, keepdims=True)
    rstd = lax.rsqrt(jnp.mean(cent * cent, axis=1, keepdims=True) + eps_norm)
    return cent * rstd, rstd


def any_spec(n):
    return [pl.BlockSpec(memory_space=pl.ANY)] * n


def vmem_spec(n):
    return [pl.BlockSpec(memory_space=pltpu.VMEM)] * n


def run(steps):
    for step in steps:
        step()


def at_step(index, hooks):
    for k, steps in hooks.items():
        pl.when(index == k)(functools.partial(run, steps))


NJ = HC // HD
ROWS = 256
CHUNKS = LEN // ROWS
PARTS = 7

PRE = ((0, 0), (3, 0), (1, 0), (0, 1), (0, 2), (3, 1), (3, 2), (1, 1), (1, 2), (0, 3), (0, 4), (3, 3), (3, 4), (1, 3), (1, 4), (0, 5), (2, 0), (0, 6), (3, 5), (3, 6), (0, 7), (4, 0), (0, 8), (0, 9), (0, 10), (1, 5), (1, 6), (2, 1), (0, 11), (3, 7), (3, 8), (0, 12), (3, 9), (2, 2), (4, 1), (4, 2), (5, 0), (1, 7), (3, 10), (3, 11), (1, 8), (1, 9), (3, 12), (1, 10), (2, 3), (2, 4))
HEAD = {2: ((4, 3), (1, 11), (4, 4), (1, 12)), 3: ((2, 5), (2, 6), (5, 1), (5, 2)), 4: ((2, 7), (2, 8), (2, 9), (2, 10)), 6: ((4, 5), (4, 6), (2, 11), (2, 12)), 9: ((4, 7), (4, 8), (4, 9), (4, 10), (5, 3), (5, 4)), 11: ((4, 11),)}
MID = ((4, 12), (5, 5), (5, 6))
LATE = {11: ((5, 7), (5, 8), (5, 9), (5, 10)), 15: ((5, 11), (5, 12))}


def pack(refs, wa, table, w1, w2, p, r, cb):
    qkv, out, up, down, col, row = refs
    dp, t = p.z * 2 + p.x, p.y * 2 + p.c
    at = pl.ds(pl.multiple_of(dp * r, 16), r)
    high = -(-r // 128) * 128
    out_t = jnp.concatenate([out[...], jnp.zeros((HC, high - r), f32)], axis=1)
    out_t = jnp.concatenate([out_t, jnp.zeros((256 - HC, high), f32)], axis=0).T[0:r]
    for j in range(NJ):
        s = slice(j * HD, j * HD + HD)
        wa[j, t, at, :] = jnp.concatenate([qkv[0, :, s], qkv[1, :, s], qkv[2, :, s], out_t[:, s]], axis=1).astype(bf16)
    tile = jnp.concatenate([row[...], jnp.zeros((10, r), f32)], axis=0)
    line = lax.broadcasted_iota(jnp.int32, (16, r), 0)
    for k in range(-(-cb // r)):
        wide = min(r, cb - k * r)
        piece = col[:, k * r : k * r + wide]
        if wide < r:
            piece = jnp.concatenate([piece, jnp.zeros((1, r - wide), f32)], axis=1)
        tile = jnp.where(line == 6 + k, piece, tile)
    tile = jnp.concatenate([tile, jnp.zeros((16, 128 - r), f32)], axis=1)
    own = pl.multiple_of(dp * 32, 32)
    table[t, pl.ds(own, 16), :] = tile.astype(bf16)
    table[t, pl.ds(pl.multiple_of(own + 16, 16), 16), :] = jnp.zeros((16, 128), bf16)
    w1[t, at, :] = up[...].astype(bf16)
    w2[t, at, :] = down[...].astype(bf16)


def loss_pull(pooled, groups, index):
    count = pooled.shape[0]
    inv = lax.rsqrt(jnp.sum(pooled * pooled, axis=1, keepdims=True) + eps_norm)
    unit = pooled * inv
    similar = temper * lax.dot_general(unit, unit, (((1,), (1,)), ((), ())), precision=highest, preferred_element_type=f32)
    rows = lax.broadcasted_iota(jnp.int32, (count, count), 0)
    cols = lax.broadcasted_iota(jnp.int32, (count, count), 1)
    others = jnp.where(rows == cols, masked, similar)
    members = groups.astype(f32)
    eye = jnp.where(rows == cols, 1.0, 0.0).astype(bf16)
    turned = nt(eye, members.astype(bf16))

    def pull(table, axis):
        top = jnp.max(others, axis=axis, keepdims=True)
        e = jnp.exp(others - top)
        return e / jnp.sum(e, axis=axis, keepdims=True) - table / jnp.sum(table, axis=axis, keepdims=True)

    both = temper * (pull(members, 1) + pull(turned, 0))
    grad = lax.dot_general(both, unit, (((1,), (0,)), ((), ())), precision=highest, preferred_element_type=f32)
    own = lax.broadcasted_iota(jnp.int32, (count, 1), 0) == index

    def pick(v):
        return jnp.sum(jnp.where(own, v, 0.0), axis=0, keepdims=True)

    unit, grad = pick(unit), pick(grad)
    return pick(inv) * (grad - unit * jnp.sum(unit * grad, axis=1, keepdims=True))


def forward_kernel(n, cb, comm, *refs):
    dp = 2 * n
    r = D // dp
    given, refs = (6, refs[:2] + refs[2:]) if comm else (4, refs)
    len_ref, groups_ref, x_ref = refs[:3]
    weights_in, refs = refs[3 : 3 + given], refs[3 + given :]
    (rstd1_ref, rstd2_ref, gain_ref, row_ref, hb_ref, u_ref,
     out_out, h1_out, xhat1_out, g_out, xhat2_out, ct_out, xt_out, gp_out, q_out, k_out, v_out, wa_out, w1_out, w2_out,
     out_ref, h1_ref, xhat1_ref, g_ref, xhat2_ref, ct_ref, xt,
     wa, w1, w2, table, bcol, col, qt, kt, vt, kn, sb, wo, pool, stage, every, pooled,
     local, q_sem, stage_sem, o_sem, *sems) = refs
    length = len_ref[0]
    hooks, middle, late = {}, [], {}
    if comm:
        p = Place(n)
        pack(weights_in, wa, table, w1, w2, p, r, cb)
        enter(p)
        wholes = [wa.at[j] for j in range(NJ)] + [table, w1, w2, every]
        straight = (False,) * NJ + (True, False, False, True)
        a0, a1, a2, bias, up, down, pools = [Gather(p, i, full, sems, way) for i, (full, way) in enumerate(zip(wholes, straight))]
        parts = (a0, a1, a2, bias, up, down)
        flows = [[g.start] + g.flow() for g in parts]

        def steps(pairs):
            return [flows[g][k] for g, k in pairs]

        if n == 4:
            run(steps(PRE[:5]))
            xt[...] = x_ref[...].T
            run(steps(PRE[5:]))
            hooks = {h: steps(pairs) for h, pairs in HEAD.items()}
            middle = steps(MID)
            late = {h: steps(pairs) for h, pairs in LATE.items()}
        else:
            xt[...] = x_ref[...].T
            for group in zip(*flows):
                run(group)
    else:
        loads = [pltpu.make_async_copy(src, dst, local.at[i]) for i, (src, dst) in enumerate(zip(weights_in, (wa, table, w1, w2)))]
        for cp in loads:
            cp.start()
        xt[...] = x_ref[...].T
        for cp in loads:
            cp.wait()
    saved = ((out_ref, out_out), (h1_ref, h1_out), (xhat1_ref, xhat1_out), (g_ref, g_out), (xhat2_ref, xhat2_out), (ct_ref, ct_out),
             (xt, xt_out), (wa, wa_out), (w1, w1_out), (w2, w2_out))

    def save(i):
        return pltpu.make_async_copy(*saved[i], o_sem.at[i])

    save(6).start()

    col_rows = -(-cb // r)
    for i in range(dp):
        rows = slice(i * 32, i * 32 + 16)
        row_ref[:, i * r : i * r + r] = table[0, rows, 0:r].astype(f32)
        for t in range(NT):
            tile = table[t, rows, :].astype(f32)
            for k in range(col_rows):
                wide = min(r, cb - k * r)
                col[t, :, i * cb + k * r : i * cb + k * r + wide] = jnp.broadcast_to(tile[6 + k : 7 + k, 0:wide], (8, wide))
    for t in range(NT):
        bcol[t] = jnp.transpose(col[t, :, 0 : 2 * HC])[:, 0:1]
        hb_ref[t] = col[t, 0:1, 2 * HC : 2 * HC + D]

    ones = jnp.ones((1, LEN), f32)
    where = lax.broadcasted_iota(jnp.int32, (1, LEN), 1)
    key_bias = jnp.where(where < length, 0.0, masked).astype(f32)
    kept = ((qt, q_out), (kt, k_out), (vt, v_out))
    key_rows = aug_rows(key_bias, ones, ones, ones)
    one_row = aug_rows(ones)
    half = LEN // 2

    def project(h):
        j, t = h // NT, h % NT
        qkv = tn(wa[j, t, :, 0 : 3 * HD], xt[...])
        qt[h, 0:HD, :] = ((qkv[0:HD] + bcol[t, pl.ds(pl.multiple_of(j * HD, HD), HD), :]) * HD**-0.5).astype(bf16)
        kt[h, 0:HD, :] = qkv[HD : 2 * HD].astype(bf16)
        vt[h] = (qkv[2 * HD : 3 * HD] + bcol[t, pl.ds(pl.multiple_of(HC + j * HD, HD), HD), :]).astype(bf16)
        qt[h, HD:AUG, :] = one_row
        kt[h, HD:AUG, :] = key_rows
        kn[h % 2] = kt[h].T

    def attend(h, i, s):
        where = slice(i * half, i * half + half)
        top = jnp.max(s, axis=0, keepdims=True)
        e = jnp.exp(s - top)
        total = jnp.sum(e, axis=0, keepdims=True)
        ct_ref[pl.ds(pl.multiple_of(h * HD, HD), HD), where] = (nn(vt[h], e.astype(bf16)) * (1.0 / total)).astype(bf16)
        hi, mid, lo = split3(-(top + jnp.log(total)))
        qt[h, HD:AUG, where] = aug_rows(ones[:, where], hi, mid, lo)

    project(0)
    sb[0] = nn(kn[0], qt[0, :, 0:half])

    def head(h, _):
        after = nn(kn[h % 2], qt[h, :, half:LEN])
        attend(h, 0, sb[0])
        sb[1] = after
        nxt = jnp.minimum(h + 1, H - 1)

        @pl.when(h + 1 < H)
        def _():
            project(nxt)

        after = nn(kn[nxt % 2], qt[nxt, :, 0:half])
        attend(h, 1, sb[1])
        sb[0] = after
        for i, (src, dst) in enumerate(kept):
            pltpu.make_async_copy(src.at[h], dst.at[h], q_sem.at[i, h]).start()
        at_step(h, hooks)
        return 0

    lax.fori_loop(0, H, head, 0)
    save(5).start()

    c_nat = out_ref
    c_nat[...] = ct_ref[...].T
    for j in range(NJ):
        for t in range(NT):
            h = j * NT + t
            wo[:, h * HD : h * HD + HD] = wa[j, t, :, 3 * HD : 4 * HD]
    save(7).start()

    def first(i, _):
        s = pl.ds(pl.multiple_of(i * ROWS, ROWS), ROWS)
        r1 = x_ref[s, :].astype(f32) + (nt(c_nat[s, :], wo[...]) + row_ref[0:1])
        xhat, rstd = norm(r1)
        xhat1_ref[s, :] = xhat
        rstd1_ref[s, :] = rstd
        h1_ref[s, :] = (xhat * row_ref[1:2] + row_ref[2:3]).astype(bf16)
        return 0

    lax.fori_loop(0, CHUNKS, first, 0)
    save(1).start()
    save(2).start()
    run(middle)

    def staged(step):
        t, i = step // CHUNKS, step % CHUNKS
        s = pl.ds(pl.multiple_of(i * ROWS, ROWS), ROWS)
        return pltpu.make_async_copy(stage.at[step % 2], gp_out.at[t, s, :], stage_sem.at[step % 2])

    def hidden(step, _):
        t, i = step // CHUNKS, step % CHUNKS
        s = pl.ds(pl.multiple_of(i * ROWS, ROWS), ROWS)
        z = nn(h1_ref[s, :], w1[t]) + hb_ref[t]
        cdf = 0.5 + 0.5 * lax.erf(z * 0.5**0.5)
        g_ref[t, s, :] = (z * cdf).astype(bf16)

        @pl.when(step >= 2)
        def _():
            staged(step - 2).wait()

        stage[step % 2] = cdf + z * (jnp.exp(-0.5 * z * z) * 0.3989422804014327)
        staged(step).start()
        at_step(step, late)
        return 0

    lax.fori_loop(0, NT * CHUNKS, hidden, 0)
    staged(NT * CHUNKS - 2).wait()
    staged(NT * CHUNKS - 1).wait()
    for i in (3, 8, 9):
        save(i).start()
    gain_ref[...] = jnp.zeros_like(gain_ref)
    pool[...] = jnp.zeros_like(pool)

    def second(i, _):
        s = pl.ds(pl.multiple_of(i * ROWS, ROWS), ROWS)
        res = xhat1_ref[s, :] * row_ref[1:2] + row_ref[2:3] + row_ref[3:4]
        for t in range(NT):
            res = res + nt(g_ref[t, s, :], w2[t])
        xhat, rstd = norm(res)
        xhat2_ref[s, :] = xhat
        rstd2_ref[s, :] = rstd
        y = xhat * row_ref[4:5] + row_ref[5:6]
        out_ref[s, :] = y.astype(bf16)
        here = i * ROWS + lax.broadcasted_iota(jnp.int32, (ROWS, 1), 0) < length
        pool[0:1] += jnp.sum(jnp.where(here, y, 0.0), axis=0, keepdims=True)
        gain_ref[...] += jnp.sum(jnp.where(here, xhat, 0.0), axis=0, keepdims=True)
        return 0

    lax.fori_loop(0, CHUNKS, second, 0)
    size = jnp.full((1, 1), length).astype(f32)
    mean = pool[0:1] / size
    if comm:
        block = [mean[:, i * 128 : i * 128 + 128] for i in range(D // 128)] + [jnp.zeros((16 - D // 128, 128), f32)]
        every[p.y * 2 + p.c, pl.ds(pl.multiple_of((p.z * 2 + p.x) * 16, 16), 16), :] = jnp.concatenate(block, axis=0)
        pools.start()
    save(0).start()
    save(4).start()
    if comm:
        run(pools.flow())
        for i in range(dp):
            for t in range(NT):
                for k in range(D // 128):
                    pooled[i * NT + t : i * NT + t + 1, k * 128 : k * 128 + 128] = every[t, i * 16 + k : i * 16 + k + 1, :]
        u_ref[...] = loss_pull(pooled[...], groups_ref[...], lax.axis_index("dp") * NT + lax.axis_index("tensor")) / size
        for g in parts + (pools,):
            g.finish()
    else:
        u_ref[...] = mean
    for h in range(H):
        for i, (src, dst) in enumerate(kept):
            pltpu.make_async_copy(src.at[h], dst.at[h], q_sem.at[i, h]).wait()
    for i in range(len(saved)):
        save(i).wait()


def forward(length, groups, x, weights, n, cb, comm):
    s = jax.ShapeDtypeStruct
    dp = 2 * n
    r = D // dp
    dma = pltpu.SemaphoreType.DMA
    shapes = [s((LEN, 1), f32), s((LEN, 1), f32), s((1, D), f32), s((16, D), f32), s((NT, 1, D), f32), s((1, D), f32)]
    big = [s((LEN, D), bf16), s((LEN, D), bf16), s((LEN, D), f32), s((NT, LEN, D), bf16), s((LEN, D), f32), s((D, LEN), bf16), s((D, LEN), bf16)]
    kept = [
        s((NT, LEN, D), f32), s((H, AUG, LEN), bf16), s((H, AUG, LEN), bf16), s((H, HD, LEN), bf16),
        s((NJ, NT, D, 4 * HD), bf16), s((NT, D, D), bf16), s((NT, D, D), bf16),
    ]
    scratch = [pltpu.VMEM(v.shape, v.dtype) for v in big] + [
        pltpu.VMEM((NJ, NT, D, 4 * HD), bf16), pltpu.VMEM((NT, D, D), bf16), pltpu.VMEM((NT, D, D), bf16),
        pltpu.VMEM((NT, dp * 32, 128), bf16), pltpu.VMEM((NT, 2 * HC, 1), f32), pltpu.VMEM((NT, 8, dp * cb), f32),
        pltpu.VMEM((H, AUG, LEN), bf16), pltpu.VMEM((H, AUG, LEN), bf16), pltpu.VMEM((H, HD, LEN), bf16),
        pltpu.VMEM((2, LEN, AUG), bf16), pltpu.VMEM((2, LEN, LEN // 2), f32),
        pltpu.VMEM((D, D), bf16), pltpu.VMEM((8, D), f32), pltpu.VMEM((2, ROWS, D), f32),
        pltpu.VMEM((NT, dp * 16, 128), f32), pltpu.VMEM((dp * NT, D), f32),
        dma((PARTS,)), dma((3, H)), dma((2,)), dma((len(big) + 3,)),
    ]
    if comm:
        scratch += gather_sems(PARTS, n)
        params = pltpu.CompilerParams(collective_id=0, has_side_effects=True, vmem_limit_bytes=VMEM_CAP)
    else:
        params = pltpu.CompilerParams(vmem_limit_bytes=VMEM_CAP)
    return pl.pallas_call(
        functools.partial(forward_kernel, n, cb, comm),
        out_shape=shapes + big + kept,
        in_specs=[pl.BlockSpec(memory_space=pltpu.SMEM)] + vmem_spec(2) + (vmem_spec(6) if comm else any_spec(4)),
        out_specs=vmem_spec(len(shapes)) + any_spec(len(big) + len(kept)),
        scratch_shapes=scratch,
        compiler_params=params,
    )(length, groups, x, *weights)


def backward_kernel(n, cb, comm, *refs):
    dp = 2 * n
    r = D // dp
    (len_ref, u_ref, gain_ref, rstd1_ref, rstd2_ref, row_ref,
     xhat2_in, xhat1_in, w1_in, w2_in, wa_in, g_in, gp_in, h1_in, ct_in, xt_in, q_in, k_in, v_in, *refs) = refs
    dx_out, *refs = refs
    outs, refs = refs[: NJ + 3], refs[NJ + 3 :]
    landing, refs = (refs[: NJ + 3], refs[NJ + 3 :]) if comm else ([], refs)
    (wa, w1, w2, t1, t2, dqkv, xt, ct, df, dz, dh, sd, pp, turned, qkv, wcat, grow, ghb, gcol, gbias,
     load, s_load, q_sem, x_sem, *refs) = refs
    length = len_ref[0]
    hooks, after, ends = {}, {}, {}
    grads = [wa.at[j] for j in range(NJ)]
    h1t, dft, dat, dct = t1, t2, t1, t2

    loads = [
        pltpu.make_async_copy(src, dst, load.at[i])
        for i, (src, dst) in enumerate(
            ((xhat2_in, sd.at[1, :, 0:D]), (w2_in, w2), (h1_in, dz), (w1_in, w1), (wa_in, wa), (ct_in, ct), (xt_in, xt))
        )
    ]

    def fetch(step):
        t = part_of(step)
        return [
            pltpu.make_async_copy(src.at[t], dst.at[step % 2, :, 0:D], s_load.at[step % 2, i])
            for i, (src, dst) in enumerate(((g_in, pp), (gp_in, sd)))
        ]

    if comm:
        p = Place(n)

        def part_of(step):
            first = jnp.where(step < 2, 1 - p.y, p.y)
            return first * 2 + step % 2
    else:

        def part_of(step):
            return step

    for cp in loads[:2]:
        cp.start()
    for cp in fetch(0):
        cp.start()
    for cp in loads[2:]:
        cp.start()
    if comm:
        temp = wcat
        bufs, sems = refs[:-8], refs[-8:]
        enter(p)
        where = [(lambda t: w1.at[t]), (lambda t: w2.at[t])] + [(lambda t, g=g: g.at[t]) for g in grads] + [lambda t: gbias.at[t]]
        parts = []
        for i, source in enumerate(where):
            rows, width = outs[i].shape
            parts.append(
                Scatter(p, i, rows, source, outs[i], [landing[i]] + list(bufs[3 * i : 3 * i + 3]),
                        temp.at[0 : 2 * n * rows, 0:width], x_sem.at[0], sems)
            )
        up, down, a0, a1, a2, bias = parts

        def call(*pairs):
            return [functools.partial(f, *args) for f, *args in pairs]

        after = {
            1: call((up.core, 0), (down.core, 0)),
            2: call((up.add, 0), (up.corner,), (down.add, 0), (down.corner,)),
            3: call((up.core, 1), (down.core, 1)),
        }
        hooks = {
            0: call((down.cross,)), 3: call((a0.core, 0), (a0.core, 1)), 4: call((up.line,)),
            5: call((a0.add, 0), (a0.corner,), (a0.add, 1)), 6: call((down.line,)), 7: call((a1.core, 0), (a1.core, 1), (a0.cross,)),
            8: call((up.last,)), 9: call((a1.add, 0), (a1.corner,), (a1.add, 1), (a0.line,)), 10: call((down.last,)),
            11: call((a1.cross,), (a2.core, 0), (a2.core, 1)),
        }

    u = u_ref[...]
    du = u * row_ref[4:5]
    mean_du = jnp.mean(du, axis=1, keepdims=True)
    grow[...] = jnp.zeros_like(grow)
    loads[0].wait()

    def outer(i, _):
        s = pl.ds(pl.multiple_of(i * ROWS, ROWS), ROWS)
        here = i * ROWS + lax.broadcasted_iota(jnp.int32, (ROWS, 1), 0) < length
        hat = sd[1, s, 0:D]
        dot = jnp.mean(hat * du, axis=1, keepdims=True)
        dr = jnp.where(here, rstd2_ref[s, :] * (du - mean_du - hat * dot), 0.0)
        dh[s, :] = dr
        low = dr.astype(bf16)
        df[s, :] = low
        grow[3:4] += jnp.sum(low.astype(f32), axis=0, keepdims=True)
        return 0

    lax.fori_loop(0, CHUNKS, outer, 0)
    grow[4:5] = u * gain_ref[...]
    grow[5:6] = u * jnp.full((1, 1), length).astype(f32)
    dft[...] = df[...].T
    loads[2].wait()
    h1t[...] = dz[...].T
    last_hat = pltpu.make_async_copy(xhat1_in, sd.at[0, :, 0:D], load.at[0])
    loads[1].wait()
    loads[3].wait()

    def hidden(step, _):
        t = part_of(step)
        slot = step % 2
        for cp in fetch(step):
            cp.wait()

        @pl.when(step + 1 < NT)
        def _():
            for cp in fetch(step + 1):
                cp.start()

        hb = jnp.zeros((1, D), f32)
        for i in range(CHUNKS):
            s = pl.ds(i * ROWS, ROWS)
            low = (nn(df[s, :], w2[t]) * sd[slot, s, 0:D]).astype(bf16)
            dz[s, :] = low
            hb = hb + jnp.sum(low.astype(f32), axis=0, keepdims=True)
            dh[s, :] += nt(low, w1[t])
        ghb[t] = hb
        for i in range(D // ROWS):
            s = slice(i * ROWS, (i + 1) * ROWS)
            w1[t, s, :] = nn(h1t[s, :], dz[...]).astype(bf16)
            w2[t, s, :] = nn(dft[s, :], pp[slot, :, 0:D]).astype(bf16)
        pl.when(step == NT - 2)(last_hat.start)
        at_step(step, after)
        return 0

    lax.fori_loop(0, NT, hidden, 0)

    def fetch_head(h, slot):
        return [
            pltpu.make_async_copy(src.at[h], qkv.at[slot, i, 0 : src.shape[1], :], q_sem.at[slot, i])
            for i, src in enumerate((q_in, k_in, v_in))
        ]

    for cp in fetch_head(0, 0):
        cp.start()
    last_hat.wait()

    def inner_norm(i, _):
        s = pl.ds(pl.multiple_of(i * ROWS, ROWS), ROWS)
        d = dh[s, :]
        hat = sd[0, s, 0:D]
        grow[1:2] += jnp.sum(d * hat, axis=0, keepdims=True)
        grow[2:3] += jnp.sum(d, axis=0, keepdims=True)
        dn = d * row_ref[1:2]
        dr = rstd1_ref[s, :] * (dn - jnp.mean(dn, axis=1, keepdims=True) - hat * jnp.mean(dn * hat, axis=1, keepdims=True))
        dh[s, :] = dr
        low = dr.astype(bf16)
        grow[0:1] += jnp.sum(low.astype(f32), axis=0, keepdims=True)
        df[s, :] = low
        return 0

    lax.fori_loop(0, CHUNKS, inner_norm, 0)
    dat[...] = df[...].T
    if comm:
        run(call((up.add, 1), (down.add, 1), (up.cross,)))
    loads[4].wait()
    loads[5].wait()
    for j in range(NJ):
        for t in range(NT):
            h = j * NT + t
            wcat[:, h * HD : h * HD + HD] = wa[j, t, :, 3 * HD : 4 * HD]
    for i in range(D // ROWS):
        s = slice(i * ROWS, (i + 1) * ROWS)
        dct[s, :] = tn(wcat[:, s], dat[...]).astype(bf16)
        gwo = nt(dat[s, :], ct[...]).astype(bf16)
        for j in range(NJ):
            for t in range(NT):
                h = j * NT + t
                wa[j, t, s, 3 * HD : 4 * HD] = gwo[:, h * HD : h * HD + HD]
    loads[6].wait()

    def head(h, _):
        j, t = h // NT, h % NT
        slot = h % 2
        for cp in fetch_head(h, slot):
            cp.wait()

        @pl.when(h + 1 < H)
        def _():
            for cp in fetch_head(h + 1, 1 - slot):
                cp.start()

        own = pl.ds(pl.multiple_of(h * HD, HD), HD)
        prob = jnp.exp(tn(qkv[slot, 0], qkv[slot, 1]))
        sd[0] = prob
        sd[1] = tn(dct[own, :], qkv[slot, 2, 0:HD, :])
        pp[0] = prob.astype(bf16)
        inner = jnp.sum(sd[0] * sd[1], axis=1, keepdims=True)
        pp[1] = (sd[0] * (sd[1] - inner)).astype(bf16)
        turned[...] = pp[1].T
        at = pl.multiple_of(t * 3 * HD, HD)
        dqkv[pl.ds(at + HD, HD), :] = nn(qkv[slot, 0, 0:HD, :], pp[1]).astype(bf16)
        dqkv[pl.ds(at + 2 * HD, HD), :] = nn(dct[own, :], pp[0]).astype(bf16)
        dqkv[pl.ds(at, HD), :] = (nn(qkv[slot, 1, 0:HD, :], turned[...]) * HD**-0.5).astype(bf16)

        @pl.when(t == NT - 1)
        def _():
            for k in range(NT):
                wcat[:, k * 3 * HD : (k + 1) * 3 * HD] = wa[j, k, :, 0 : 3 * HD]
            sums = nt(jnp.ones((16, LEN), bf16), dqkv[...])
            for k in range(NT):
                gcol[j, k] = sums[0:8, k * 3 * HD : (k + 1) * 3 * HD]
            for i in range(D // ROWS):
                s = slice(i * ROWS, (i + 1) * ROWS)
                g = nt(xt[s, :], dqkv[...]).astype(bf16)
                for k in range(NT):
                    wa[j, k, s, 0 : 3 * HD] = g[:, k * 3 * HD : (k + 1) * 3 * HD]
            for i in range(CHUNKS):
                s = slice(i * ROWS, (i + 1) * ROWS)
                dh[s, :] += lax.dot_general(dqkv[:, s], wcat[...], (((0,), (1,)), ((), ())), preferred_element_type=f32)

        at_step(h, hooks)
        return 0

    lax.fori_loop(0, H, head, 0)
    dx = pltpu.make_async_copy(dh, dx_out, load.at[0])
    dx.start()

    col_rows = -(-cb // r)
    cols = []
    for t in range(NT):
        pieces = [gcol[j, t, 0:1, 0:HD] for j in range(NJ)] + [gcol[j, t, 0:1, 2 * HD : 3 * HD] for j in range(NJ)]
        cols.append(jnp.concatenate(pieces + [ghb[t]], axis=1))
    at = lax.broadcasted_iota(jnp.int32, (32, 128), 0)
    for i in range(dp):
        rows = jnp.pad(grow[0:8, i * r : i * r + r], ((0, 24), (0, 128 - r)))
        for t in range(NT):
            block = jnp.where(at < 6, rows, 0.0)
            for k in range(col_rows):
                wide = min(r, cb - k * r)
                piece = cols[t][:, i * cb + k * r : i * cb + k * r + wide]
                block = jnp.where(at == 6 + k, jnp.pad(piece, ((0, 0), (0, 128 - wide))), block)
            gbias[t, i * 32 : i * 32 + 32, :] = block.astype(bf16)
    if comm:
        run(call(
            (bias.core, 0), (bias.core, 1), (a2.add, 0), (a2.corner,), (bias.add, 0), (bias.corner,), (a2.add, 1), (bias.add, 1),
            (a0.last,), (a1.line,), (a2.cross,), (bias.cross,), (a1.last,), (a2.line,), (bias.line,), (a2.last,), (bias.last,),
        ))
        for part in parts:
            part.finish()
    else:
        copies = [pltpu.make_async_copy(src, dst, load.at[1 + i]) for i, (src, dst) in enumerate(zip([w1, w2] + grads + [gbias], outs))]
        for cp in copies:
            cp.start()
        for cp in copies:
            cp.wait()
    dx.wait()


def backward(length, u, gain, rstd1, rstd2, row, big, n, cb, comm):
    s = jax.ShapeDtypeStruct
    dp = 2 * n
    r = D // dp
    dma = pltpu.SemaphoreType.DMA
    widths = [(r, D), (r, D)] + [(r, 4 * HD)] * NJ + [(32, 128)]
    if comm:
        sums = [s(shape, f32) for shape in widths]
        landing = [s((2, dp * rows, wide), bf16) for rows, wide in widths]
        specs = vmem_spec(len(sums)) + any_spec(len(landing))
    else:
        sums = [s((NT, dp * rows, wide), bf16) for rows, wide in widths]
        landing = []
        specs = any_spec(len(sums))
    turned = pltpu.VMEM((D, LEN), bf16)
    rows_low = pltpu.VMEM((LEN, D), bf16)
    rows_full = pltpu.VMEM((LEN, D), f32)
    scratch = [
        pltpu.VMEM((NJ, NT, D, 4 * HD), bf16), pltpu.VMEM((NT, D, D), bf16), pltpu.VMEM((NT, D, D), bf16),
        turned, turned, turned, turned, turned, rows_low, rows_low, rows_full,
        pltpu.VMEM((2, LEN, LEN), f32), pltpu.VMEM((2, LEN, LEN), bf16), pltpu.VMEM((LEN, LEN), bf16), pltpu.VMEM((2, 3, AUG, LEN), bf16), pltpu.VMEM((D, D), bf16),
        pltpu.VMEM((16, D), f32), pltpu.VMEM((NT, 1, D), f32), pltpu.VMEM((NJ, NT, 8, 3 * HD), f32), pltpu.VMEM((NT, dp * 32, 128), bf16),
        dma((8,)), dma((2, 2)), dma((2, 3)), dma((1,)),
    ]
    if comm:
        for rows, wide in widths:
            scratch += scatter_bufs(n, rows, wide)
        scratch += scatter_sems(len(widths), n)
        params = pltpu.CompilerParams(collective_id=1, has_side_effects=True, vmem_limit_bytes=VMEM_CAP)
    else:
        params = pltpu.CompilerParams(vmem_limit_bytes=VMEM_CAP)
    return pl.pallas_call(
        functools.partial(backward_kernel, n, cb, comm),
        out_shape=[s((LEN, D), f32)] + sums + landing,
        in_specs=[pl.BlockSpec(memory_space=pltpu.SMEM)] + vmem_spec(5) + any_spec(len(big)),
        out_specs=any_spec(1) + specs,
        scratch_shapes=scratch,
        compiler_params=params,
    )(length, u, gain, rstd1, rstd2, row, *big)


def adam_kernel(cb, *refs):
    moved, sums, old, refs = refs[:2], refs[2:8], refs[8:32], refs[32:]
    landed, new, held, sem = refs[:2], refs[2:26], refs[26:28], refs[28]
    inward = [pltpu.make_async_copy(src, dst, sem.at[i]) for i, (src, dst) in enumerate(zip(moved, held))]
    outward = [pltpu.make_async_copy(src, dst, sem.at[i]) for i, (src, dst) in enumerate(zip(held, landed))]
    for cp in inward:
        cp.start()
    gw1, gw2, ga, gbias = sums[0], sums[1], sums[2:5], sums[5]
    r = gw1.shape[0]

    def wide(k):
        return jnp.concatenate([ga[j][:, k * HD : k * HD + HD] for j in range(NJ)], axis=1)

    def update(i, grad, rate, at=()):
        where = at + (Ellipsis,)
        out = adam_update(*[old[4 * i + k][where] for k in range(4)], grad, rate)
        for k, v in enumerate(out):
            new[4 * i + k][where] = v

    for k in range(3):
        update(0, wide(k), D ** (-0.5), (k,))
    high = -(-r // 128) * 128
    turned = jnp.concatenate([wide(3), jnp.zeros((r, 256 - HC), f32)], axis=1)
    if high > r:
        turned = jnp.concatenate([turned, jnp.zeros((high - r, 256), f32)], axis=0)
    update(1, turned.T[0:HC, 0:r], D ** (-0.5))
    for one, two in zip(inward, outward):
        one.wait()
        two.start()
    update(2, gw1[...], D ** (-0.5))
    update(3, gw2[...], FF ** (-0.5))
    rows = gbias[...]
    pieces = [rows[6 + k : 7 + k, 0 : min(r, cb - k * r)] for k in range(-(-cb // r))]
    update(4, jnp.concatenate(pieces, axis=1), 0.1)
    update(5, rows[0:6, 0:r], 0.15)
    for cp in outward:
        cp.wait()


def adam(moved, sums, olds, cb):
    flat = [v for group in olds for v in group]
    s = jax.ShapeDtypeStruct
    shapes = [s(group[0].shape, f32) for group in olds for _ in range(4)]
    return pl.pallas_call(
        functools.partial(adam_kernel, cb),
        out_shape=[s(v.shape, v.dtype) for v in moved] + shapes,
        in_specs=any_spec(2) + vmem_spec(6 + 24),
        out_specs=any_spec(2) + vmem_spec(24),
        scratch_shapes=[pltpu.VMEM(v.shape, v.dtype) for v in moved] + [pltpu.SemaphoreType.DMA((2,))],
        compiler_params=pltpu.CompilerParams(vmem_limit_bytes=VMEM_CAP),
    )(*moved, *sums, *flat)


def gather_plain(own):
    return lax.all_gather(lax.all_gather(own, "dp", axis=0, tiled=True), "tensor", axis=0)


def scatter_plain(full):
    own = lax.psum_scatter(full.astype(f32), "tensor", scatter_dimension=0, tiled=False)
    return lax.psum_scatter(own, "dp", scatter_dimension=0, tiled=True)


def by_head(wide):
    return jnp.moveaxis(wide.reshape(*wide.shape[:-1], NJ, HD), -2, 0)


def packed(qkv_weight, out_weight, up_weight, down_weight, col_bias, row_params, r, cb):
    own_a = jnp.concatenate([by_head(qkv_weight[i]) for i in range(3)] + [by_head(out_weight.T)], axis=-1).astype(bf16)
    col_rows = -(-cb // r)
    col_pad = jnp.pad(col_bias[0], (0, col_rows * r - cb)).reshape(col_rows, r)
    own_b = jnp.pad(jnp.concatenate([row_params, col_pad], axis=0), ((0, 26 - col_rows), (0, 128 - r))).astype(bf16)
    return own_a, own_b, up_weight.astype(bf16), down_weight.T.astype(bf16)


def on_device(
    inputs, lengths, groups, qkv_weight, out_weight, up_weight, down_weight, col_bias, row_params,
    qkv_first, out_first, up_first, down_first, col_first, row_first,
    qkv_second, out_second, up_second, down_second, col_second, row_second,
    qkv_ema, out_ema, up_ema, down_ema, col_ema, row_ema,
):
    dp = lax.axis_size("dp")
    n = dp // 2
    r = D // dp
    cb = col_bias.shape[1]
    length = lax.dynamic_slice_in_dim(lengths, lax.axis_index("tensor"), 1)
    comm = r % 32 == 0
    if comm:
        weights = (qkv_weight, out_weight, up_weight, down_weight.T, col_bias, row_params)
    else:
        own_a, *others = packed(qkv_weight, out_weight, up_weight, down_weight, col_bias, row_params, r, cb)
        own_b, own_1, own_2 = [gather_plain(v) for v in others]
        weights = (jnp.stack([gather_plain(own_a[j]) for j in range(NJ)]), own_b, own_1, own_2)
    (rstd1, rstd2, gain, row, hb, u, outputs, h1, xhat1, g, xhat2, ct, xt, gp, qt, kt, vt, wa, w1, w2) = forward(
        length, groups, inputs, weights, n, cb, comm
    )
    if not comm:
        every = lax.all_gather(u, ("dp", "tensor"), axis=0, tiled=True)
        u = loss_pull(every, groups, lax.axis_index(("dp", "tensor"))) / length[0].astype(f32)

    big = (xhat2, xhat1, w1, w2, wa, g, gp, h1, ct, xt, qt, kt, vt)
    input_grad, *sums = backward(length, u, gain, rstd1, rstd2, row, big, n, cb, comm)
    sums = sums[: NJ + 3] if comm else [scatter_plain(v) for v in sums]
    olds = (
        (qkv_weight, qkv_first, qkv_second, qkv_ema),
        (out_weight, out_first, out_second, out_ema),
        (up_weight, up_first, up_second, up_ema),
        (down_weight.T, down_first.T, down_second.T, down_ema.T),
        (col_bias, col_first, col_second, col_ema),
        (row_params, row_first, row_second, row_ema),
    )
    outputs, input_grad, *new = adam((outputs, input_grad), sums, olds, cb)
    new[12:16] = [v.T for v in new[12:16]]
    return (outputs, input_grad, *new)


def solution(mesh):
    tokens = P(("dp", "tensor"), None)
    placed = (P(None, "dp", "tensor"), P("tensor", "dp"), P("dp", "tensor"), P("tensor", "dp"), P("tensor", "dp"), P(None, "dp"))
    new = tuple(spec for spec in placed for _ in range(4))
    return jax.shard_map(
        on_device,
        mesh=mesh,
        in_specs=(tokens, P("dp"), P()) + placed * 4,
        out_specs=(tokens, tokens) + new,
        check_vma=False,
    )
```

```python
import functools

import jax
import jax.numpy as jnp
from jax import lax
from jax.experimental import pallas as pl
from jax.experimental.pallas import tpu as pltpu
from jax.sharding import PartitionSpec as P

D = 768
H = 12
HD = 64
FF = 3072
LEN = 1024
STEP = 5
NT = 4
HC = D // NT
AUG = 80

MESH = pl.DeviceIdType.MESH
f32 = jnp.float32
bf16 = jnp.bfloat16
highest = lax.Precision.HIGHEST
eps_norm = 1e-05
temper = 40.0
masked = -1000000000.0
beta_one = 0.5
beta_two = 0.5
adam_eps = 1e-08
decay_rate = 0.01
ema_keep = 0.9
VMEM_CAP = 60 << 20


def nn(a, b):
    return jnp.dot(a, b, preferred_element_type=f32)


def nt(a, b):
    return lax.dot_general(a, b, (((1,), (1,)), ((), ())), preferred_element_type=f32)


def tn(a, b):
    return lax.dot_general(a, b, (((0,), (0,)), ((), ())), preferred_element_type=f32)


def adam_update(weight, first_old, second, ema_old, gradient, step_rate):
    first_new = beta_one * first_old + (1 - beta_one) * gradient
    second_new = beta_two * second + (1 - beta_two) * gradient * gradient
    first_hat = first_new / (1 - beta_one**STEP)
    second_hat = second_new / (1 - beta_two**STEP)
    weight_new = weight - step_rate * (
        first_hat / (jnp.sqrt(second_hat) + adam_eps) + decay_rate * weight
    )
    ema_new = ema_keep * ema_old + (1 - ema_keep) * weight_new
    return (first_new, second_new, weight_new, ema_new)


class Place:
    def __init__(self, depth):
        dp = lax.axis_index("dp")
        t = lax.axis_index("tensor")
        self.depth = depth
        self.z, self.x, self.y, self.c = dp // 2, dp % 2, t // 2, t % 2
        self.me = (self.z, self.x, self.y, self.c)
        self.over_x = (self.z, 1 - self.x, self.y, self.c)
        self.over_y = (self.z, self.x, 1 - self.y, self.c)
        self.over_xy = (self.z, 1 - self.x, 1 - self.y, self.c)
        self.over_c = (self.z, self.x, self.y, 1 - self.c)

    def along_z(self, k):
        return ((self.z + k) % self.depth, self.x, self.y, self.c)


    def others(self):
        return [(z, x, y) for z in range(self.depth) for x in range(2) for y in range(2) if z + x + y > 0]

    def chip(self, z, x, y):
        return ((self.z + z) % self.depth, (self.x + x) % 2, (self.y + y) % 2, self.c)


def device(place):
    z, x, y, c = place
    return (z * 2 + x, y * 2 + c)


def greet(p, everyone=False):
    bar = pltpu.get_barrier_semaphore()
    if everyone:
        to = [p.over_c] + [p.chip(*far) for far in p.others()]
    else:
        to = [p.over_c, p.over_x, p.over_y] + [p.along_z(k) for k in range(1, p.depth)]
    for place in to:
        pl.semaphore_signal(bar, inc=1, device_id=device(place), device_id_type=MESH)
    return len(to)


def enter(count):
    pl.semaphore_wait(pltpu.get_barrier_semaphore(), count)


def remote(src, dst, send, recv, to):
    return pltpu.make_async_remote_copy(
        src_ref=src, dst_ref=dst, send_sem=send, recv_sem=recv, device_id=device(to), device_id_type=MESH
    )


class Gather:
    def __init__(self, p, part, full, sems, straight=False):
        self.p, self.part, self.full, self.straight = p, part, full, straight
        self.rows = full.shape[1] // (2 * p.depth)
        self.recv, self.pair_recv, self.sz, self.sx, self.sy, self.sk, self.sc = sems

    def spot(self, place, wide=1):
        z, x, y, c = place
        r = self.rows
        step = 32 // self.full.dtype.itemsize
        return self.full.at[y * 2 + c, pl.ds(pl.multiple_of((z * 2 + x) * r, step), wide * r), :]

    def copy(self, place, to, send):
        z, x, y, c = place
        ref = self.spot(place)
        return remote(ref, ref, send.at[self.part], self.recv.at[self.part, (z * 2 + x) * 4 + y * 2 + c], to)

    def pair_copy(self, z, y, c):
        ref = self.spot((z, 0, y, c), 2)
        return remote(ref, ref, self.sc.at[self.part], self.pair_recv.at[self.part, z * 2 + y], self.p.over_c)

    def send(self, place, to, send, when=None):
        def start():
            self.copy(place(), to, send).start()

        if when is not None:
            pl.when(when())(start)
        else:
            start()

    def start(self):
        p, n = self.p, self.p.depth

        def me():
            return p.me

        if self.straight:
            for k in range(1, n):
                self.send(me, p.along_z(k), self.sz)
        else:
            self.send(me, p.along_z(1), self.sz, lambda: p.z + 1 < n)
            self.send(me, p.along_z(-1), self.sz, lambda: p.z > 0)
        self.send(me, p.over_x, self.sx)
        self.send(me, p.over_y, self.sy)

    def sides(self, k):
        p, n = self.p, self.p.depth
        if k == 0:
            return [(0, None)]
        if self.straight:
            return [(1, None)]
        return [(-1, lambda: p.z >= k), (1, lambda: p.z + k < n)]

    def each(self, k, step):
        for sign, when in self.sides(k):
            go = functools.partial(step, sign, sign * k)
            if when is not None:
                pl.when(when())(go)
            else:
                go()

    def arrived(self, place):
        self.copy(place, self.p.over_c, self.sx).wait_recv()

    def at(self, k, x, y):
        return ((self.p.z + k) % self.p.depth, x, y, self.p.c)

    def line(self, k):
        p, n = self.p, self.p.depth

        def step(sign, far):
            place = functools.partial(self.at, far, p.x, p.y)
            self.arrived(place())
            if not self.straight:
                self.send(place, p.along_z(-sign), self.sz, (lambda: p.z + 1 < n) if sign < 0 else (lambda: p.z > 0))
            self.send(place, p.over_x, self.sx)
            self.send(place, p.over_y, self.sy)

        self.each(k, step)

    def cross(self, k):
        p = self.p

        def step(sign, far):
            self.arrived(self.at(far, 1 - p.x, p.y))
            self.arrived(self.at(far, p.x, 1 - p.y))
            z = (p.z + far) % p.depth
            odd = (z + self.part) % 2
            x, y = jnp.where(odd == 1, p.x, 1 - p.x), jnp.where(odd == 1, 1 - p.y, p.y)
            to = (p.z, jnp.where(odd == 1, 1 - p.x, p.x), jnp.where(odd == 1, p.y, 1 - p.y), p.c)
            self.copy((z, x, y, p.c), to, self.sk).start()
            self.pair_copy(z, p.y, p.c).start()

        self.each(k, step)

    def corner(self, k):
        p = self.p

        def step(sign, far):
            self.arrived(self.at(far, 1 - p.x, 1 - p.y))
            self.pair_copy((p.z + far) % p.depth, 1 - p.y, p.c).start()

        self.each(k, step)

    def other_core(self):
        for z in range(self.p.depth):
            for y in range(2):
                self.pair_copy(z, y, 1 - self.p.c).wait_recv()

    def flow(self):
        n = self.p.depth
        steps = [functools.partial(self.cross, 0)]
        order = [1, n - 1] + list(range(2, n - 1)) if self.straight and n > 2 else list(range(1, n))
        for k in order:
            steps += [functools.partial(self.line, k), functools.partial(self.cross, k)]
        steps += [functools.partial(self.corner, k) for k in range(n)]
        steps.append(self.other_core)
        return steps

    def finish(self):
        n, r = self.p.depth, self.rows

        def left(ref, sem):
            pltpu.make_async_copy(ref, ref, sem.at[self.part]).wait()

        for sem in (self.sx, self.sy, self.sk):
            left(self.full.at[0, 0 : n * r, :], sem)
        left(self.full.at[0:2], self.sc)
        if self.straight:
            left(self.full.at[0, 0 : (n - 1) * r, :], self.sz)
        else:
            for z in range(n):
                count = (z + 1 if z + 1 < n else 0) + (n - z if z > 0 else 0)
                if count:
                    pl.when(self.p.z == z)(functools.partial(left, self.full.at[0, 0 : count * r, :], self.sz))


class Exchange:
    def __init__(self, p, full, sems):
        self.p, self.full = p, full
        self.sent, self.recv, self.core_sent, self.core_recv = sems

    def spot(self, place):
        z, x, y, c = place
        return self.full.at[c, pl.ds(pl.multiple_of(((z * 2 + x) * 2 + y) * 8, 8), 8), :]

    def copy(self, i, far):
        ref = self.spot(self.p.me)
        return remote(ref, ref, self.sent.at[0], self.recv.at[i], self.p.chip(*far))

    def core_copy(self):
        ref = self.full.at[self.p.c]
        return remote(ref, ref, self.core_sent.at[0], self.core_recv.at[0], self.p.over_c)

    def start(self):
        for i, far in enumerate(self.p.others()):
            self.copy(i, far).start()

    def finish(self):
        others = self.p.others()
        for i, far in enumerate(others):
            self.copy(i, far).wait_recv()
        self.core_copy().start()
        self.core_copy().wait()
        left = self.full.at[0, 0 : 8 * len(others), :]
        pltpu.make_async_copy(left, left, self.sent.at[0]).wait()


def exchange_sems(n):
    dma = pltpu.SemaphoreType.DMA
    return [dma((1,)), dma((4 * n,)), dma((1,)), dma((1,))]


def gather_sems(parts, n):
    dma = pltpu.SemaphoreType.DMA
    return [dma((parts, 8 * n)), dma((parts, 2 * n))] + [dma((parts,))] * 5


class Scatter:
    def __init__(self, p, part, rows, grads, out, bufs, temp, load, sems):
        self.p, self.part, self.rows, self.grads, self.out, self.temp, self.load = p, part, rows, grads, out, temp, load
        self.b_core, self.b_corner, self.b_cross, self.b_line = bufs
        self.ss, self.rs, self.sc, self.rc, self.sx, self.rx, self.sl, self.rl = sems

    def slab(self, y):
        return self.grads(y * 2 + self.p.c)

    def span(self, z, x):
        return pl.ds(pl.multiple_of((z * 2 + x) * self.rows, 16), self.rows)

    def which(self, k):
        return self.p.y if k else 1 - self.p.y

    def core_copy(self, k):
        p, q = self.p, self.part
        return remote(self.grads(self.which(k) * 2 + 1 - p.c), self.b_core.at[k], self.ss.at[q], self.rs.at[q, k], p.over_c)

    def core(self, k):
        self.core_copy(k).start()

    def pulled(self, k):
        return pltpu.make_async_copy(self.b_core.at[k], self.temp, self.load)

    def pull(self, k):
        self.core_copy(k).wait_recv()
        self.pulled(k).start()

    def add(self, k):
        r = self.rows
        slab = self.slab(self.which(k))
        self.pulled(k).wait()

        def one(i, _):
            s = pl.ds(pl.multiple_of(i * r, 16), r)
            slab[s, :] = (slab[s, :].astype(f32) + self.temp[s, :].astype(f32)).astype(bf16)
            return 0

        lax.fori_loop(0, 2 * self.p.depth, one, 0)

    def corner_copy(self, z):
        p, q = self.p, self.part
        src = self.slab(1 - p.y).at[self.span(z, 1 - p.x), :]
        return remote(src, self.b_corner.at[z], self.sc.at[q], self.rc.at[q, z], p.over_x if (z + q) % 2 else p.over_y)

    def corner(self):
        for z in range(self.p.depth):
            self.corner_copy(z).start()

    def cross_copy(self, z, way):
        p, q = self.p, self.part
        src = self.slab(1 - p.y).at[self.span(z, p.x), :] if way else self.slab(p.y).at[self.span(z, 1 - p.x), :]
        to = p.over_y if way else p.over_x
        return remote(src, self.b_cross.at[way, z], self.sx.at[q], self.rx.at[q, way, z], to)

    def cross(self, z):
        self.corner_copy(z).wait_recv()
        p = self.p
        slab, s = (self.slab(1 - p.y), self.span(z, p.x)) if (z + self.part) % 2 else (self.slab(p.y), self.span(z, 1 - p.x))
        slab[s, :] = (slab[s, :].astype(f32) + self.b_corner[z].astype(f32)).astype(bf16)
        for way in range(2):
            self.cross_copy(z, way).start()

    def line_copy(self, k):
        p, q = self.p, self.part
        z = (p.z + k) % p.depth
        return remote(self.slab(p.y).at[self.span(z, p.x), :], self.b_line.at[k], self.sl.at[q], self.rl.at[q, k], p.along_z(k))

    def column(self, z):
        p = self.p
        for way in range(2):
            self.cross_copy(z, way).wait_recv()
        return self.slab(p.y)[self.span(z, p.x), :].astype(f32) + self.b_cross[0, z].astype(f32) + self.b_cross[1, z].astype(f32)

    def line(self, k):
        p = self.p
        z = (p.z + k) % p.depth
        self.slab(p.y)[self.span(z, p.x), :] = self.column(z).astype(bf16)
        self.line_copy(k).start()

    def last(self):
        p = self.p
        total = self.column(p.z)
        for k in range(1, p.depth):
            self.line_copy(k).wait_recv()
            total = total + self.b_line[k].astype(f32)
        self.out[...] = total

    def flow(self, early):
        call, n = functools.partial, self.p.depth
        core = [call(self.core, 0), call(self.core, 1)]
        first = [call(self.pull, 0), call(self.add, 0), self.corner]
        steps = core[:1] + first + core[1:] if early else core + first
        steps += [call(self.pull, 1), call(self.add, 1)]
        steps += [call(self.cross, z) for z in range(n)] + [call(self.line, k) for k in range(1, n)]
        return steps + [self.last]

    def finish(self):
        q = self.part
        for ref, sem in ((self.b_core, self.ss), (self.b_corner, self.sc), (self.b_cross, self.sx), (self.b_line.at[1 : self.p.depth], self.sl)):
            pltpu.make_async_copy(ref, ref, sem.at[q]).wait()


def scatter_bufs(n, rows, width):
    return [pltpu.VMEM((n, rows, width), bf16), pltpu.VMEM((2, n, rows, width), bf16), pltpu.VMEM((n, rows, width), bf16)]


def scatter_sems(parts, n):
    dma = pltpu.SemaphoreType.DMA
    return [dma((parts,)), dma((parts, 2)), dma((parts,)), dma((parts, n)), dma((parts,)), dma((parts, 2, n)), dma((parts,)), dma((parts, n))]


def split3(row):
    hi = row.astype(bf16).astype(f32)
    mid = (row - hi).astype(bf16).astype(f32)
    return hi, mid, row - hi - mid


def aug_rows(*rows):
    width = rows[0].shape[1]
    at = lax.broadcasted_iota(jnp.int32, (16, width), 0)
    out = jnp.zeros((16, width), f32)
    for i, row in enumerate(rows):
        out = jnp.where(at == i, row, out)
    return out.astype(bf16)


def norm(r):
    cent = r - jnp.mean(r, axis=1, keepdims=True)
    rstd = lax.rsqrt(jnp.mean(cent * cent, axis=1, keepdims=True) + eps_norm)
    return cent * rstd, rstd


def any_spec(n):
    return [pl.BlockSpec(memory_space=pl.ANY)] * n


def vmem_spec(n):
    return [pl.BlockSpec(memory_space=pltpu.VMEM)] * n


def run(steps):
    for step in steps:
        step()


def at_step(index, hooks):
    for k, steps in hooks.items():
        if steps:
            pl.when(index == k)(functools.partial(run, steps))


NJ = HC // HD
ROWS = 256
CHUNKS = LEN // ROWS
PARTS = 6

PRE = ((0, 0), (3, 0), (1, 0), (2, 0), (0, 1), (0, 2), (3, 1), (3, 2), (1, 1), (1, 2), (2, 1), (2, 2), (3, 3), (3, 4), (0, 3), (1, 3), (1, 4), (0, 4), (3, 5), (3, 6), (4, 0), (2, 3), (3, 7), (0, 5), (0, 6), (2, 4), (3, 8), (5, 0), (3, 9), (0, 7), (0, 8), (1, 5), (3, 10), (0, 9), (1, 6), (2, 5), (2, 6), (0, 10), (0, 11), (4, 1), (0, 12), (3, 11), (1, 7), (4, 2), (5, 1), (1, 8), (3, 12), (1, 9), (2, 7), (2, 8))
HEAD = {0: ((1, 10),), 1: ((1, 11),), 2: ((5, 2), (2, 9), (1, 12), (2, 10)), 3: ((4, 3),), 4: ((4, 4), (2, 11), (5, 3)), 5: ((5, 4),), 6: ((2, 12),), 8: ((4, 5), (4, 6)), 10: ((5, 5),), 11: ((4, 7), (4, 8), (4, 9), (5, 6), (4, 10))}
MID = ((4, 11), (4, 12))
LATE = {0: ((5, 7), (5, 8)), 2: ((5, 9), (5, 10)), 8: ((5, 11),), 11: ((5, 12),)}
BACK = {0: ((0, 0), (1, 0)), 1: ((0, 1),), 2: ((0, 2), (0, 3), (1, 1)), 3: ((1, 2), (1, 3)), 5: ((0, 4),), 6: ((0, 5), (1, 4)), 7: ((0, 6),), 8: ((0, 7), (1, 5)), 9: ((1, 6), (0, 8), (0, 9), (0, 10)), 10: ((2, 0), (2, 1)), 11: ((1, 7),), 12: ((0, 11), (1, 8), (1, 9), (0, 12), (2, 2)), 13: ((1, 10),), 14: ((2, 3), (2, 4), (2, 5), (3, 0), (3, 1)), 15: ((2, 6), (2, 7), (2, 8), (3, 2), (1, 11)), 16: ((1, 12), (3, 3)), 17: ((3, 4), (3, 5)), 18: ((4, 0), (3, 6), (3, 7), (1, 13), (2, 9), (4, 1), (0, 13), (3, 8), (2, 10), (4, 2), (3, 9), (4, 3), (4, 4)), 19: ((2, 11), (3, 10), (4, 5), (5, 0), (2, 12), (2, 13), (5, 1), (4, 6), (5, 2), (4, 7), (5, 3), (5, 4), (4, 8), (3, 11), (5, 5), (4, 9), (1, 14), (4, 10), (3, 12), (5, 6), (5, 7), (3, 13), (5, 8), (4, 11), (5, 9), (5, 10), (4, 12), (4, 13), (0, 14), (2, 14), (5, 11), (3, 14), (5, 12), (5, 13), (4, 14), (5, 14))}


def pack(refs, wa, table, w1, w2, p, r, cb):
    qkv, out, up, down, col, row = refs
    dp, t = p.z * 2 + p.x, p.y * 2 + p.c
    at = pl.ds(pl.multiple_of(dp * r, 16), r)
    high = -(-r // 128) * 128
    out_t = jnp.concatenate([out[...], jnp.zeros((HC, high - r), f32)], axis=1)
    out_t = jnp.concatenate([out_t, jnp.zeros((256 - HC, high), f32)], axis=0).T[0:r]
    for j in range(NJ):
        s = slice(j * HD, j * HD + HD)
        wa[j, t, at, :] = jnp.concatenate([qkv[0, :, s], qkv[1, :, s], qkv[2, :, s], out_t[:, s]], axis=1).astype(bf16)
    tile = jnp.concatenate([row[...], jnp.zeros((10, r), f32)], axis=0)
    line = lax.broadcasted_iota(jnp.int32, (16, r), 0)
    for k in range(-(-cb // r)):
        wide = min(r, cb - k * r)
        piece = col[:, k * r : k * r + wide]
        if wide < r:
            piece = jnp.concatenate([piece, jnp.zeros((1, r - wide), f32)], axis=1)
        tile = jnp.where(line == 6 + k, piece, tile)
    tile = jnp.concatenate([tile, jnp.zeros((16, 128 - r), f32)], axis=1)
    own = pl.multiple_of(dp * 32, 32)
    table[t, pl.ds(own, 16), :] = tile.astype(bf16)
    table[t, pl.ds(pl.multiple_of(own + 16, 16), 16), :] = jnp.zeros((16, 128), bf16)
    w1[t, at, :] = up[...].astype(bf16)
    w2[t, at, :] = down[...].astype(bf16)


def loss_pull(pooled, groups, index):
    count = pooled.shape[0]
    inv = lax.rsqrt(jnp.sum(pooled * pooled, axis=1, keepdims=True) + eps_norm)
    unit = pooled * inv
    similar = temper * lax.dot_general(unit, unit, (((1,), (1,)), ((), ())), precision=highest, preferred_element_type=f32)
    rows = lax.broadcasted_iota(jnp.int32, (count, count), 0)
    cols = lax.broadcasted_iota(jnp.int32, (count, count), 1)
    others = jnp.where(rows == cols, masked, similar)
    members = groups.astype(f32)
    eye = jnp.where(rows == cols, 1.0, 0.0).astype(bf16)
    turned = nt(eye, members.astype(bf16))

    def pull(table, axis):
        top = jnp.max(others, axis=axis, keepdims=True)
        e = jnp.exp(others - top)
        return e / jnp.sum(e, axis=axis, keepdims=True) - table / jnp.sum(table, axis=axis, keepdims=True)

    both = temper * (pull(members, 1) + pull(turned, 0))
    grad = lax.dot_general(both, unit, (((1,), (0,)), ((), ())), precision=highest, preferred_element_type=f32)
    own = lax.broadcasted_iota(jnp.int32, (count, 1), 0) == index

    def pick(v):
        return jnp.sum(jnp.where(own, v, 0.0), axis=0, keepdims=True)

    unit, grad = pick(unit), pick(grad)
    return pick(inv) * (grad - unit * jnp.sum(unit * grad, axis=1, keepdims=True))


def forward_kernel(n, cb, comm, *refs):
    dp = 2 * n
    r = D // dp
    given, refs = (6, refs[:2] + refs[2:]) if comm else (4, refs)
    len_ref, groups_ref, x_ref = refs[:3]
    weights_in, refs = refs[3 : 3 + given], refs[3 + given :]
    (rstd1_ref, rstd2_ref, gain_ref, row_ref, hb_ref, u_ref,
     out_out, h1_out, xhat1_out, g_out, xhat2_out, ct_out, xt_out, gp_out, q_out, k_out, v_out, wa_out, w1_out, w2_out,
     out_ref, h1_ref, xhat1_ref, g_ref, xhat2_ref, ct_ref, xt,
     wa, w1, w2, table, bcol, col, qt, kt, vt, kn, sb, wo, pool, stage, every, pooled,
     local, q_sem, stage_sem, o_sem, *sems) = refs
    length = len_ref[lax.axis_index("tensor")]
    hooks, middle, late = {}, [], {}
    if comm:
        p = Place(n)
        count = greet(p, True)
        pack(weights_in, wa, table, w1, w2, p, r, cb)
        enter(count)
        wholes = [wa.at[j] for j in range(NJ)] + [table, w1, w2]
        straight = (False,) * NJ + (True, False, False)
        parts = [Gather(p, i, full, sems[:7], way) for i, (full, way) in enumerate(zip(wholes, straight))]
        pools = Exchange(p, every, sems[7:])
        flows = [[g.start] + g.flow() for g in parts]

        def steps(pairs):
            return [flows[g][k] for g, k in pairs]

        if n == 4:
            run(steps(PRE[:5]))
            xt[...] = x_ref[...].T
            run(steps(PRE[5:]))
            hooks = {h: steps(pairs) for h, pairs in HEAD.items()}
            middle = steps(MID)
            late = {h: steps(pairs) for h, pairs in LATE.items()}
        else:
            xt[...] = x_ref[...].T
            for group in zip(*flows):
                run(group)
    else:
        loads = [pltpu.make_async_copy(src, dst, local.at[i]) for i, (src, dst) in enumerate(zip(weights_in, (wa, table, w1, w2)))]
        for cp in loads:
            cp.start()
        xt[...] = x_ref[...].T
        for cp in loads:
            cp.wait()
    saved = ((out_ref, out_out), (h1_ref, h1_out), (xhat1_ref, xhat1_out), (g_ref, g_out), (xhat2_ref, xhat2_out), (ct_ref, ct_out),
             (xt, xt_out), (wa, wa_out), (w1, w1_out), (w2, w2_out))

    def save(i):
        return pltpu.make_async_copy(*saved[i], o_sem.at[i])

    save(6).start()

    col_rows = -(-cb // r)
    for i in range(dp):
        rows = slice(i * 32, i * 32 + 16)
        row_ref[:, i * r : i * r + r] = table[0, rows, 0:r].astype(f32)
        for t in range(NT):
            tile = table[t, rows, :].astype(f32)
            for k in range(col_rows):
                wide = min(r, cb - k * r)
                col[t, :, i * cb + k * r : i * cb + k * r + wide] = jnp.broadcast_to(tile[6 + k : 7 + k, 0:wide], (8, wide))
    for t in range(NT):
        bcol[t] = jnp.transpose(col[t, :, 0 : 2 * HC])[:, 0:1]
        hb_ref[t] = col[t, 0:1, 2 * HC : 2 * HC + D]

    ones = jnp.ones((1, LEN), f32)
    where = lax.broadcasted_iota(jnp.int32, (1, LEN), 1)
    key_bias = jnp.where(where < length, 0.0, masked).astype(f32)
    kept = ((qt, q_out), (kt, k_out), (vt, v_out))
    key_rows = aug_rows(key_bias, ones, ones, ones)
    one_row = aug_rows(ones)
    half = LEN // 2

    def project(h):
        j, t = h // NT, h % NT
        qkv = tn(wa[j, t, :, 0 : 3 * HD], xt[...])
        qt[h, 0:HD, :] = ((qkv[0:HD] + bcol[t, pl.ds(pl.multiple_of(j * HD, HD), HD), :]) * HD**-0.5).astype(bf16)
        kt[h, 0:HD, :] = qkv[HD : 2 * HD].astype(bf16)
        vt[h] = (qkv[2 * HD : 3 * HD] + bcol[t, pl.ds(pl.multiple_of(HC + j * HD, HD), HD), :]).astype(bf16)
        qt[h, HD:AUG, :] = one_row
        kt[h, HD:AUG, :] = key_rows
        kn[h % 2] = kt[h].T

    def attend(h, i, s):
        where = slice(i * half, i * half + half)
        top = jnp.max(s, axis=0, keepdims=True)
        e = jnp.exp(s - top)
        total = jnp.sum(e, axis=0, keepdims=True)
        ct_ref[pl.ds(pl.multiple_of(h * HD, HD), HD), where] = (nn(vt[h], e.astype(bf16)) * (1.0 / total)).astype(bf16)
        hi, mid, lo = split3(-(top + jnp.log(total)))
        qt[h, HD:AUG, where] = aug_rows(ones[:, where], hi, mid, lo)

    project(0)
    sb[0] = nn(kn[0], qt[0, :, 0:half])

    def head(h, _):
        after = nn(kn[h % 2], qt[h, :, half:LEN])
        attend(h, 0, sb[0])
        sb[1] = after
        nxt = jnp.minimum(h + 1, H - 1)

        @pl.when(h + 1 < H)
        def _():
            project(nxt)

        after = nn(kn[nxt % 2], qt[nxt, :, 0:half])
        attend(h, 1, sb[1])
        sb[0] = after
        for i, (src, dst) in enumerate(kept):
            pltpu.make_async_copy(src.at[h], dst.at[h], q_sem.at[i, h]).start()
        at_step(h, hooks)
        return 0

    lax.fori_loop(0, H, head, 0)
    save(5).start()

    c_nat = out_ref
    c_nat[...] = ct_ref[...].T
    for j in range(NJ):
        for t in range(NT):
            h = j * NT + t
            wo[:, h * HD : h * HD + HD] = wa[j, t, :, 3 * HD : 4 * HD]
    save(7).start()

    def first(i, _):
        s = pl.ds(pl.multiple_of(i * ROWS, ROWS), ROWS)
        r1 = x_ref[s, :].astype(f32) + (nt(c_nat[s, :], wo[...]) + row_ref[0:1])
        xhat, rstd = norm(r1)
        xhat1_ref[s, :] = xhat
        rstd1_ref[s, :] = rstd
        h1_ref[s, :] = (xhat * row_ref[1:2] + row_ref[2:3]).astype(bf16)
        return 0

    lax.fori_loop(0, CHUNKS, first, 0)
    save(1).start()
    save(2).start()
    run(middle)

    def staged(step):
        t, i = step // CHUNKS, step % CHUNKS
        s = pl.ds(pl.multiple_of(i * ROWS, ROWS), ROWS)
        return pltpu.make_async_copy(stage.at[step % 2], gp_out.at[t, s, :], stage_sem.at[step % 2])

    def hidden(step, _):
        t, i = step // CHUNKS, step % CHUNKS
        s = pl.ds(pl.multiple_of(i * ROWS, ROWS), ROWS)
        z = nn(h1_ref[s, :], w1[t]) + hb_ref[t]
        cdf = 0.5 + 0.5 * lax.erf(z * 0.5**0.5)
        g_ref[t, s, :] = (z * cdf).astype(bf16)

        @pl.when(step >= 2)
        def _():
            staged(step - 2).wait()

        stage[step % 2] = cdf + z * (jnp.exp(-0.5 * z * z) * 0.3989422804014327)
        staged(step).start()
        at_step(step, late)
        return 0

    lax.fori_loop(0, NT * CHUNKS, hidden, 0)
    staged(NT * CHUNKS - 2).wait()
    staged(NT * CHUNKS - 1).wait()
    for i in (3, 8, 9):
        save(i).start()
    gain_ref[...] = jnp.zeros_like(gain_ref)
    pool[...] = jnp.zeros_like(pool)

    def second(i, _):
        s = pl.ds(pl.multiple_of(i * ROWS, ROWS), ROWS)
        res = xhat1_ref[s, :] * row_ref[1:2] + row_ref[2:3] + row_ref[3:4]
        for t in range(NT):
            res = res + nt(g_ref[t, s, :], w2[t])
        xhat, rstd = norm(res)
        xhat2_ref[s, :] = xhat
        rstd2_ref[s, :] = rstd
        y = xhat * row_ref[4:5] + row_ref[5:6]
        out_ref[s, :] = y.astype(bf16)
        here = i * ROWS + lax.broadcasted_iota(jnp.int32, (ROWS, 1), 0) < length
        pool[0:1] += jnp.sum(jnp.where(here, y, 0.0), axis=0, keepdims=True)
        gain_ref[...] += jnp.sum(jnp.where(here, xhat, 0.0), axis=0, keepdims=True)
        return 0

    lax.fori_loop(0, CHUNKS, second, 0)
    size = jnp.full((1, 1), length).astype(f32)
    mean = pool[0:1] / size
    if comm:
        block = [mean[:, i * 128 : i * 128 + 128] for i in range(D // 128)] + [jnp.zeros((8 - D // 128, 128), f32)]
        every[p.c, pl.ds(pl.multiple_of(((p.z * 2 + p.x) * 2 + p.y) * 8, 8), 8), :] = jnp.concatenate(block, axis=0)
        pools.start()
    save(0).start()
    save(4).start()
    if comm:
        pools.finish()
        for i in range(dp):
            for t in range(NT):
                at = (i * 2 + t // 2) * 8
                for k in range(D // 128):
                    pooled[i * NT + t : i * NT + t + 1, k * 128 : k * 128 + 128] = every[t % 2, at + k : at + k + 1, :]
        u_ref[...] = loss_pull(pooled[...], groups_ref[...], lax.axis_index("dp") * NT + lax.axis_index("tensor")) / size
        for g in parts:
            g.finish()
    else:
        u_ref[...] = mean
    for h in range(H):
        for i, (src, dst) in enumerate(kept):
            pltpu.make_async_copy(src.at[h], dst.at[h], q_sem.at[i, h]).wait()
    for i in range(len(saved)):
        save(i).wait()


def forward(length, groups, x, weights, n, cb, comm):
    s = jax.ShapeDtypeStruct
    dp = 2 * n
    r = D // dp
    dma = pltpu.SemaphoreType.DMA
    shapes = [s((LEN, 1), f32), s((LEN, 1), f32), s((1, D), f32), s((16, D), f32), s((NT, 1, D), f32), s((1, D), f32)]
    big = [s((LEN, D), bf16), s((LEN, D), bf16), s((LEN, D), f32), s((NT, LEN, D), bf16), s((LEN, D), f32), s((D, LEN), bf16), s((D, LEN), bf16)]
    kept = [
        s((NT, LEN, D), f32), s((H, AUG, LEN), bf16), s((H, AUG, LEN), bf16), s((H, HD, LEN), bf16),
        s((NJ, NT, D, 4 * HD), bf16), s((NT, D, D), bf16), s((NT, D, D), bf16),
    ]
    scratch = [pltpu.VMEM(v.shape, v.dtype) for v in big] + [
        pltpu.VMEM((NJ, NT, D, 4 * HD), bf16), pltpu.VMEM((NT, D, D), bf16), pltpu.VMEM((NT, D, D), bf16),
        pltpu.VMEM((NT, dp * 32, 128), bf16), pltpu.VMEM((NT, 2 * HC, 1), f32), pltpu.VMEM((NT, 8, dp * cb), f32),
        pltpu.VMEM((H, AUG, LEN), bf16), pltpu.VMEM((H, AUG, LEN), bf16), pltpu.VMEM((H, HD, LEN), bf16),
        pltpu.VMEM((2, LEN, AUG), bf16), pltpu.VMEM((2, LEN, LEN // 2), f32),
        pltpu.VMEM((D, D), bf16), pltpu.VMEM((8, D), f32), pltpu.VMEM((2, ROWS, D), f32),
        pltpu.VMEM((2, dp * 16, 128), f32), pltpu.VMEM((dp * NT, D), f32),
        dma((PARTS,)), dma((3, H)), dma((2,)), dma((len(big) + 3,)),
    ]
    if comm:
        scratch += gather_sems(PARTS, n) + exchange_sems(n)
        params = pltpu.CompilerParams(collective_id=0, has_side_effects=True, vmem_limit_bytes=VMEM_CAP)
    else:
        params = pltpu.CompilerParams(vmem_limit_bytes=VMEM_CAP)
    return pl.pallas_call(
        functools.partial(forward_kernel, n, cb, comm),
        out_shape=shapes + big + kept,
        in_specs=[pl.BlockSpec(memory_space=pltpu.SMEM)] + vmem_spec(2) + (vmem_spec(6) if comm else any_spec(4)),
        out_specs=vmem_spec(len(shapes)) + any_spec(len(big) + len(kept)),
        scratch_shapes=scratch,
        compiler_params=params,
    )(length, groups, x, *weights)


def backward_kernel(n, cb, comm, *refs):
    dp = 2 * n
    r = D // dp
    (len_ref, u_ref, gain_ref, rstd1_ref, rstd2_ref, row_ref,
     xhat2_in, xhat1_in, w1_in, w2_in, wa_in, g_in, gp_in, h1_in, ct_in, xt_in, q_in, k_in, v_in, *refs) = refs
    dx_out, *refs = refs
    outs, refs = refs[: NJ + 3], refs[NJ + 3 :]
    landing, refs = (refs[: NJ + 3], refs[NJ + 3 :]) if comm else ([], refs)
    (wa, w1, w2, t1, t2, dqkv, xt, ct, df, dz, dh, sd, pp, turned, qkv, wcat, grow, ghb, gcol, gbias,
     load, s_load, q_sem, x_sem, *refs) = refs
    length = len_ref[lax.axis_index("tensor")]
    hooks, after, ends = {}, {}, [[], [], []]
    grads = [wa.at[j] for j in range(NJ)]
    h1t, dft, dat, dct = t1, t2, t1, t2

    loads = [
        pltpu.make_async_copy(src, dst, load.at[i])
        for i, (src, dst) in enumerate(
            ((xhat2_in, sd.at[1, :, 0:D]), (w2_in, w2), (h1_in, dz), (w1_in, w1), (wa_in, wa), (ct_in, ct), (xt_in, xt))
        )
    ]

    def fetch(step):
        t = part_of(step)
        return [
            pltpu.make_async_copy(src.at[t], dst.at[step % 2, :, 0:D], s_load.at[step % 2, i])
            for i, (src, dst) in enumerate(((g_in, pp), (gp_in, sd)))
        ]

    if comm:
        p = Place(n)

        def part_of(step):
            y = jnp.where(step < 2, 1 - p.y, p.y)
            return y * 2 + jnp.where(step % 2 == 0, 1 - p.c, p.c)
    else:

        def part_of(step):
            return step

    for cp in loads[:2]:
        cp.start()
    for cp in fetch(0):
        cp.start()
    for cp in loads[2:]:
        cp.start()
    if comm:
        temp, *refs = refs
        bufs, sems = refs[:-8], refs[-8:]
        count = greet(p)
        where = [(lambda t: w1.at[t]), (lambda t: w2.at[t])] + [(lambda t, g=g: g.at[t]) for g in grads] + [lambda t: gbias.at[t]]
        parts = []
        for i, source in enumerate(where):
            rows, width = outs[i].shape
            parts.append(
                Scatter(p, i, rows, source, outs[i], [landing[i]] + list(bufs[3 * i : 3 * i + 3]),
                        temp.at[0 : 2 * n * rows, 0:width], x_sem.at[0], sems)
            )
        flows = [part.flow(i < 2) for i, part in enumerate(parts)]

        def steps(pairs):
            return [flows[g][k] for g, k in pairs]

        if n == 4:
            plan = {slot: steps(pairs) for slot, pairs in BACK.items()}
        else:
            plan = {1: steps([(g, k) for g in range(2) for k in range(4)]), 3: steps([(g, k) for g in range(2) for k in range(4, 7)])}
            plan[6] = [step for flow in flows[:2] for step in flow[7:]]
            for j in range(NJ):
                plan[7 + j * NT + NT - 1] = flows[2 + j]
            plan[7 + H] = flows[-1]
        after = {k: plan.get(k, []) for k in range(NT)}
        hooks = {h: plan.get(7 + h, []) for h in range(H)}
        ends = [plan.get(5, []), plan.get(6, []), plan.get(7 + H, [])]

    u = u_ref[...]
    du = u * row_ref[4:5]
    mean_du = jnp.mean(du, axis=1, keepdims=True)
    grow[...] = jnp.zeros_like(grow)
    loads[0].wait()

    def outer(i, _):
        s = pl.ds(pl.multiple_of(i * ROWS, ROWS), ROWS)
        here = i * ROWS + lax.broadcasted_iota(jnp.int32, (ROWS, 1), 0) < length
        hat = sd[1, s, 0:D]
        dot = jnp.mean(hat * du, axis=1, keepdims=True)
        dr = jnp.where(here, rstd2_ref[s, :] * (du - mean_du - hat * dot), 0.0)
        dh[s, :] = dr
        low = dr.astype(bf16)
        df[s, :] = low
        grow[3:4] += jnp.sum(low.astype(f32), axis=0, keepdims=True)
        return 0

    lax.fori_loop(0, CHUNKS, outer, 0)
    if comm:
        enter(count)
    grow[4:5] = u * gain_ref[...]
    grow[5:6] = u * jnp.full((1, 1), length).astype(f32)
    dft[...] = df[...].T
    loads[2].wait()
    h1t[...] = dz[...].T
    last_hat = pltpu.make_async_copy(xhat1_in, sd.at[0, :, 0:D], load.at[0])
    loads[1].wait()
    loads[3].wait()

    def hidden(step, _):
        t = part_of(step)
        slot = step % 2
        for cp in fetch(step):
            cp.wait()

        @pl.when(step + 1 < NT)
        def _():
            for cp in fetch(step + 1):
                cp.start()

        hb = jnp.zeros((1, D), f32)
        for i in range(CHUNKS):
            s = pl.ds(i * ROWS, ROWS)
            low = (nn(df[s, :], w2[t]) * sd[slot, s, 0:D]).astype(bf16)
            dz[s, :] = low
            hb = hb + jnp.sum(low.astype(f32), axis=0, keepdims=True)
            dh[s, :] += nt(low, w1[t])
        ghb[t] = hb
        for i in range(D // ROWS):
            s = slice(i * ROWS, (i + 1) * ROWS)
            w1[t, s, :] = nn(h1t[s, :], dz[...]).astype(bf16)
            w2[t, s, :] = nn(dft[s, :], pp[slot, :, 0:D]).astype(bf16)
        pl.when(step == NT - 2)(last_hat.start)
        at_step(step, after)
        return 0

    lax.fori_loop(0, NT, hidden, 0)

    def fetch_head(h, slot):
        return [
            pltpu.make_async_copy(src.at[h], qkv.at[slot, i, 0 : src.shape[1], :], q_sem.at[slot, i])
            for i, src in enumerate((q_in, k_in, v_in))
        ]

    for cp in fetch_head(0, 0):
        cp.start()
    last_hat.wait()

    def inner_norm(i, _):
        s = pl.ds(pl.multiple_of(i * ROWS, ROWS), ROWS)
        d = dh[s, :]
        hat = sd[0, s, 0:D]
        grow[1:2] += jnp.sum(d * hat, axis=0, keepdims=True)
        grow[2:3] += jnp.sum(d, axis=0, keepdims=True)
        dn = d * row_ref[1:2]
        dr = rstd1_ref[s, :] * (dn - jnp.mean(dn, axis=1, keepdims=True) - hat * jnp.mean(dn * hat, axis=1, keepdims=True))
        dh[s, :] = dr
        low = dr.astype(bf16)
        grow[0:1] += jnp.sum(low.astype(f32), axis=0, keepdims=True)
        df[s, :] = low
        return 0

    lax.fori_loop(0, CHUNKS, inner_norm, 0)
    dat[...] = df[...].T
    run(ends[0])
    loads[4].wait()
    loads[5].wait()
    for j in range(NJ):
        for t in range(NT):
            h = j * NT + t
            wcat[:, h * HD : h * HD + HD] = wa[j, t, :, 3 * HD : 4 * HD]
    for i in range(D // ROWS):
        s = slice(i * ROWS, (i + 1) * ROWS)
        dct[s, :] = tn(wcat[:, s], dat[...]).astype(bf16)
        gwo = nt(dat[s, :], ct[...]).astype(bf16)
        for j in range(NJ):
            for t in range(NT):
                h = j * NT + t
                wa[j, t, s, 3 * HD : 4 * HD] = gwo[:, h * HD : h * HD + HD]
    loads[6].wait()
    run(ends[1])

    def head(h, _):
        j, t = h // NT, h % NT
        slot = h % 2
        for cp in fetch_head(h, slot):
            cp.wait()

        @pl.when(h + 1 < H)
        def _():
            for cp in fetch_head(h + 1, 1 - slot):
                cp.start()

        own = pl.ds(pl.multiple_of(h * HD, HD), HD)
        prob = jnp.exp(tn(qkv[slot, 0], qkv[slot, 1]))
        sd[0] = prob
        sd[1] = tn(dct[own, :], qkv[slot, 2, 0:HD, :])
        pp[0] = prob.astype(bf16)
        inner = jnp.sum(sd[0] * sd[1], axis=1, keepdims=True)
        pp[1] = (sd[0] * (sd[1] - inner)).astype(bf16)
        turned[...] = pp[1].T
        at = pl.multiple_of(t * 3 * HD, HD)
        dqkv[pl.ds(at + HD, HD), :] = nn(qkv[slot, 0, 0:HD, :], pp[1]).astype(bf16)
        dqkv[pl.ds(at + 2 * HD, HD), :] = nn(dct[own, :], pp[0]).astype(bf16)
        dqkv[pl.ds(at, HD), :] = (nn(qkv[slot, 1, 0:HD, :], turned[...]) * HD**-0.5).astype(bf16)

        @pl.when(t == NT - 1)
        def _():
            for k in range(NT):
                wcat[:, k * 3 * HD : (k + 1) * 3 * HD] = wa[j, k, :, 0 : 3 * HD]
            sums = nt(jnp.ones((16, LEN), bf16), dqkv[...])
            for k in range(NT):
                gcol[j, k] = sums[0:8, k * 3 * HD : (k + 1) * 3 * HD]
            for i in range(D // ROWS):
                s = slice(i * ROWS, (i + 1) * ROWS)
                g = nt(xt[s, :], dqkv[...]).astype(bf16)
                for k in range(NT):
                    wa[j, k, s, 0 : 3 * HD] = g[:, k * 3 * HD : (k + 1) * 3 * HD]
        at_step(h, hooks)

        @pl.when(t == NT - 1)
        def _():
            for i in range(CHUNKS):
                s = slice(i * ROWS, (i + 1) * ROWS)
                dh[s, :] += lax.dot_general(dqkv[:, s], wcat[...], (((0,), (1,)), ((), ())), preferred_element_type=f32)

        return 0

    lax.fori_loop(0, H, head, 0)
    dx = pltpu.make_async_copy(dh, dx_out, load.at[0])
    dx.start()

    col_rows = -(-cb // r)
    cols = []
    for t in range(NT):
        pieces = [gcol[j, t, 0:1, 0:HD] for j in range(NJ)] + [gcol[j, t, 0:1, 2 * HD : 3 * HD] for j in range(NJ)]
        cols.append(jnp.concatenate(pieces + [ghb[t]], axis=1))
    at = lax.broadcasted_iota(jnp.int32, (32, 128), 0)
    for i in range(dp):
        rows = jnp.pad(grow[0:8, i * r : i * r + r], ((0, 24), (0, 128 - r)))
        for t in range(NT):
            block = jnp.where(at < 6, rows, 0.0)
            for k in range(col_rows):
                wide = min(r, cb - k * r)
                piece = cols[t][:, i * cb + k * r : i * cb + k * r + wide]
                block = jnp.where(at == 6 + k, jnp.pad(piece, ((0, 0), (0, 128 - wide))), block)
            gbias[t, i * 32 : i * 32 + 32, :] = block.astype(bf16)
    run(ends[2])
    if comm:
        for part in parts:
            part.finish()
    else:
        copies = [pltpu.make_async_copy(src, dst, load.at[1 + i]) for i, (src, dst) in enumerate(zip([w1, w2] + grads + [gbias], outs))]
        for cp in copies:
            cp.start()
        for cp in copies:
            cp.wait()
    dx.wait()


def backward(length, u, gain, rstd1, rstd2, row, big, n, cb, comm):
    s = jax.ShapeDtypeStruct
    dp = 2 * n
    r = D // dp
    dma = pltpu.SemaphoreType.DMA
    widths = [(r, D), (r, D)] + [(r, 4 * HD)] * NJ + [(32, 128)]
    if comm:
        sums = [s(shape, f32) for shape in widths]
        landing = [s((2, dp * rows, wide), bf16) for rows, wide in widths]
        specs = vmem_spec(len(sums)) + any_spec(len(landing))
    else:
        sums = [s((NT, dp * rows, wide), bf16) for rows, wide in widths]
        landing = []
        specs = any_spec(len(sums))
    turned = pltpu.VMEM((D, LEN), bf16)
    rows_low = pltpu.VMEM((LEN, D), bf16)
    rows_full = pltpu.VMEM((LEN, D), f32)
    scratch = [
        pltpu.VMEM((NJ, NT, D, 4 * HD), bf16), pltpu.VMEM((NT, D, D), bf16), pltpu.VMEM((NT, D, D), bf16),
        turned, turned, turned, turned, turned, rows_low, rows_low, rows_full,
        pltpu.VMEM((2, LEN, LEN), f32), pltpu.VMEM((2, LEN, LEN), bf16), pltpu.VMEM((LEN, LEN), bf16), pltpu.VMEM((2, 3, AUG, LEN), bf16), pltpu.VMEM((D, D), bf16),
        pltpu.VMEM((16, D), f32), pltpu.VMEM((NT, 1, D), f32), pltpu.VMEM((NJ, NT, 8, 3 * HD), f32), pltpu.VMEM((NT, dp * 32, 128), bf16),
        dma((8,)), dma((2, 2)), dma((2, 3)), dma((1,)),
    ]
    if comm:
        scratch += [pltpu.VMEM((D, D), bf16)]
        for rows, wide in widths:
            scratch += scatter_bufs(n, rows, wide)
        scratch += scatter_sems(len(widths), n)
        params = pltpu.CompilerParams(collective_id=1, has_side_effects=True, vmem_limit_bytes=VMEM_CAP)
    else:
        params = pltpu.CompilerParams(vmem_limit_bytes=VMEM_CAP)
    return pl.pallas_call(
        functools.partial(backward_kernel, n, cb, comm),
        out_shape=[s((LEN, D), f32)] + sums + landing,
        in_specs=[pl.BlockSpec(memory_space=pltpu.SMEM)] + vmem_spec(5) + any_spec(len(big)),
        out_specs=any_spec(1) + specs,
        scratch_shapes=scratch,
        compiler_params=params,
    )(length, u, gain, rstd1, rstd2, row, *big)


def adam_kernel(cb, *refs):
    moved, sums, old, refs = refs[:2], refs[2:8], refs[8:32], refs[32:]
    landed, new, held, sem = refs[:2], refs[2:26], refs[26:28], refs[28]
    inward = [pltpu.make_async_copy(src, dst, sem.at[i]) for i, (src, dst) in enumerate(zip(moved, held))]
    outward = [pltpu.make_async_copy(src, dst, sem.at[i]) for i, (src, dst) in enumerate(zip(held, landed))]
    for cp in inward:
        cp.start()
    gw1, gw2, ga, gbias = sums[0], sums[1], sums[2:5], sums[5]
    r = gw1.shape[0]

    def wide(k):
        return jnp.concatenate([ga[j][:, k * HD : k * HD + HD] for j in range(NJ)], axis=1)

    def update(i, grad, rate, at=()):
        where = at + (Ellipsis,)
        out = adam_update(*[old[4 * i + k][where] for k in range(4)], grad, rate)
        for k, v in enumerate(out):
            new[4 * i + k][where] = v

    for k in range(3):
        update(0, wide(k), D ** (-0.5), (k,))
    high = -(-r // 128) * 128
    turned = jnp.concatenate([wide(3), jnp.zeros((r, 256 - HC), f32)], axis=1)
    if high > r:
        turned = jnp.concatenate([turned, jnp.zeros((high - r, 256), f32)], axis=0)
    update(1, turned.T[0:HC, 0:r], D ** (-0.5))
    for one, two in zip(inward, outward):
        one.wait()
        two.start()
    update(2, gw1[...], D ** (-0.5))
    update(3, gw2[...], FF ** (-0.5))
    rows = gbias[...]
    pieces = [rows[6 + k : 7 + k, 0 : min(r, cb - k * r)] for k in range(-(-cb // r))]
    update(4, jnp.concatenate(pieces, axis=1), 0.1)
    update(5, rows[0:6, 0:r], 0.15)
    for cp in outward:
        cp.wait()


def adam(moved, sums, olds, cb):
    flat = [v for group in olds for v in group]
    s = jax.ShapeDtypeStruct
    shapes = [s(group[0].shape, f32) for group in olds for _ in range(4)]
    return pl.pallas_call(
        functools.partial(adam_kernel, cb),
        out_shape=[s(v.shape, v.dtype) for v in moved] + shapes,
        in_specs=any_spec(2) + vmem_spec(6 + 24),
        out_specs=any_spec(2) + vmem_spec(24),
        scratch_shapes=[pltpu.VMEM(v.shape, v.dtype) for v in moved] + [pltpu.SemaphoreType.DMA((2,))],
        compiler_params=pltpu.CompilerParams(vmem_limit_bytes=VMEM_CAP),
    )(*moved, *sums, *flat)


def gather_plain(own):
    return lax.all_gather(lax.all_gather(own, "dp", axis=0, tiled=True), "tensor", axis=0)


def scatter_plain(full):
    own = lax.psum_scatter(full.astype(f32), "tensor", scatter_dimension=0, tiled=False)
    return lax.psum_scatter(own, "dp", scatter_dimension=0, tiled=True)


def by_head(wide):
    return jnp.moveaxis(wide.reshape(*wide.shape[:-1], NJ, HD), -2, 0)


def packed(qkv_weight, out_weight, up_weight, down_weight, col_bias, row_params, r, cb):
    own_a = jnp.concatenate([by_head(qkv_weight[i]) for i in range(3)] + [by_head(out_weight.T)], axis=-1).astype(bf16)
    col_rows = -(-cb // r)
    col_pad = jnp.pad(col_bias[0], (0, col_rows * r - cb)).reshape(col_rows, r)
    own_b = jnp.pad(jnp.concatenate([row_params, col_pad], axis=0), ((0, 26 - col_rows), (0, 128 - r))).astype(bf16)
    return own_a, own_b, up_weight.astype(bf16), down_weight.T.astype(bf16)


def on_device(
    inputs, lengths, groups, qkv_weight, out_weight, up_weight, down_weight, col_bias, row_params,
    qkv_first, out_first, up_first, down_first, col_first, row_first,
    qkv_second, out_second, up_second, down_second, col_second, row_second,
    qkv_ema, out_ema, up_ema, down_ema, col_ema, row_ema,
):
    dp = lax.axis_size("dp")
    n = dp // 2
    r = D // dp
    cb = col_bias.shape[1]
    comm = r % 32 == 0
    if comm:
        weights = (qkv_weight, out_weight, up_weight, down_weight.T, col_bias, row_params)
    else:
        own_a, *others = packed(qkv_weight, out_weight, up_weight, down_weight, col_bias, row_params, r, cb)
        own_b, own_1, own_2 = [gather_plain(v) for v in others]
        weights = (jnp.stack([gather_plain(own_a[j]) for j in range(NJ)]), own_b, own_1, own_2)
    (rstd1, rstd2, gain, row, hb, u, outputs, h1, xhat1, g, xhat2, ct, xt, gp, qt, kt, vt, wa, w1, w2) = forward(
        lengths, groups, inputs, weights, n, cb, comm
    )
    if not comm:
        every = lax.all_gather(u, ("dp", "tensor"), axis=0, tiled=True)
        u = loss_pull(every, groups, lax.axis_index(("dp", "tensor"))) / lengths[lax.axis_index("tensor")].astype(f32)

    big = (xhat2, xhat1, w1, w2, wa, g, gp, h1, ct, xt, qt, kt, vt)
    input_grad, *sums = backward(lengths, u, gain, rstd1, rstd2, row, big, n, cb, comm)
    sums = sums[: NJ + 3] if comm else [scatter_plain(v) for v in sums]
    olds = (
        (qkv_weight, qkv_first, qkv_second, qkv_ema),
        (out_weight, out_first, out_second, out_ema),
        (up_weight, up_first, up_second, up_ema),
        (down_weight.T, down_first.T, down_second.T, down_ema.T),
        (col_bias, col_first, col_second, col_ema),
        (row_params, row_first, row_second, row_ema),
    )
    outputs, input_grad, *new = adam((outputs, input_grad), sums, olds, cb)
    new[12:16] = [v.T for v in new[12:16]]
    return (outputs, input_grad, *new)


def solution(mesh):
    tokens = P(("dp", "tensor"), None)
    placed = (P(None, "dp", "tensor"), P("tensor", "dp"), P("dp", "tensor"), P("tensor", "dp"), P("tensor", "dp"), P(None, "dp"))
    new = tuple(spec for spec in placed for _ in range(4))
    return jax.shard_map(
        on_device,
        mesh=mesh,
        in_specs=(tokens, P("dp"), P()) + placed * 4,
        out_specs=(tokens, tokens) + new,
        check_vma=False,
    )
```

```python
import functools

import jax
import jax.numpy as jnp
from jax import lax
from jax.experimental import pallas as pl
from jax.experimental.pallas import tpu as pltpu
from jax.sharding import PartitionSpec as P

D = 768
H = 12
HD = 64
FF = 3072
LEN = 1024
STEP = 5
NT = 4
HC = D // NT
AUG = 80

MESH = pl.DeviceIdType.MESH
f32 = jnp.float32
bf16 = jnp.bfloat16
highest = lax.Precision.HIGHEST
eps_norm = 1e-05
temper = 40.0
masked = -1000000000.0
beta_one = 0.5
beta_two = 0.5
adam_eps = 1e-08
decay_rate = 0.01
ema_keep = 0.9
VMEM_CAP = 60 << 20


def nn(a, b):
    return jnp.dot(a, b, preferred_element_type=f32)


def nt(a, b):
    return lax.dot_general(a, b, (((1,), (1,)), ((), ())), preferred_element_type=f32)


def tn(a, b):
    return lax.dot_general(a, b, (((0,), (0,)), ((), ())), preferred_element_type=f32)


def adam_update(weight, first_old, second, ema_old, gradient, step_rate):
    first_new = beta_one * first_old + (1 - beta_one) * gradient
    second_new = beta_two * second + (1 - beta_two) * gradient * gradient
    first_hat = first_new / (1 - beta_one**STEP)
    second_hat = second_new / (1 - beta_two**STEP)
    weight_new = weight - step_rate * (
        first_hat / (jnp.sqrt(second_hat) + adam_eps) + decay_rate * weight
    )
    ema_new = ema_keep * ema_old + (1 - ema_keep) * weight_new
    return (first_new, second_new, weight_new, ema_new)


class Place:
    def __init__(self, depth):
        dp = lax.axis_index("dp")
        t = lax.axis_index("tensor")
        self.depth = depth
        self.z, self.x, self.y, self.c = dp // 2, dp % 2, t // 2, t % 2
        self.me = (self.z, self.x, self.y, self.c)
        self.over_x = (self.z, 1 - self.x, self.y, self.c)
        self.over_y = (self.z, self.x, 1 - self.y, self.c)
        self.over_xy = (self.z, 1 - self.x, 1 - self.y, self.c)
        self.over_c = (self.z, self.x, self.y, 1 - self.c)

    def along_z(self, k):
        return ((self.z + k) % self.depth, self.x, self.y, self.c)


    def others(self):
        return [(z, x, y) for z in range(self.depth) for x in range(2) for y in range(2) if z + x + y > 0]

    def chip(self, z, x, y):
        return ((self.z + z) % self.depth, (self.x + x) % 2, (self.y + y) % 2, self.c)


def device(place):
    z, x, y, c = place
    return (z * 2 + x, y * 2 + c)


def greet(p, everyone=False):
    bar = pltpu.get_barrier_semaphore()
    if everyone:
        to = [p.over_c] + [p.chip(*far) for far in p.others()]
    else:
        to = [p.over_c, p.over_x, p.over_y] + [p.along_z(k) for k in range(1, p.depth)]
    for place in to:
        pl.semaphore_signal(bar, inc=1, device_id=device(place), device_id_type=MESH)
    return len(to)


def enter(count):
    pl.semaphore_wait(pltpu.get_barrier_semaphore(), count)


def remote(src, dst, send, recv, to):
    return pltpu.make_async_remote_copy(
        src_ref=src, dst_ref=dst, send_sem=send, recv_sem=recv, device_id=device(to), device_id_type=MESH
    )


class Gather:
    def __init__(self, p, part, full, sems, straight=False, upright=False):
        self.p, self.part, self.full, self.straight, self.upright = p, part, full, straight, upright
        self.rows = full.shape[1] // (2 * p.depth)
        self.recv, self.pair_recv, self.sz, self.sx, self.sy, self.sk, self.sc = sems

    def spot(self, place, wide=1):
        z, x, y, c = place
        r = self.rows
        step = 32 // self.full.dtype.itemsize
        return self.full.at[y * 2 + c, pl.ds(pl.multiple_of((z * 2 + x) * r, step), wide * r), :]

    def copy(self, place, to, send):
        z, x, y, c = place
        ref = self.spot(place)
        return remote(ref, ref, send.at[self.part], self.recv.at[self.part, (z * 2 + x) * 4 + y * 2 + c], to)

    def pair_copy(self, z, y, c):
        ref = self.spot((z, 0, y, c), 2)
        return remote(ref, ref, self.sc.at[self.part], self.pair_recv.at[self.part, z * 2 + y], self.p.over_c)

    def send(self, place, to, send, when=None):
        def start():
            self.copy(place(), to, send).start()

        if when is not None:
            pl.when(when())(start)
        else:
            start()

    def start(self):
        p, n = self.p, self.p.depth

        def me():
            return p.me

        if self.straight:
            for k in range(1, n):
                self.send(me, p.along_z(k), self.sz)
        else:
            self.send(me, p.along_z(1), self.sz, lambda: p.z + 1 < n)
            self.send(me, p.along_z(-1), self.sz, lambda: p.z > 0)
        self.send(me, p.over_x, self.sx)
        self.send(me, p.over_y, self.sy)

    def sides(self, k):
        p, n = self.p, self.p.depth
        if k == 0:
            return [(0, None)]
        if self.straight:
            return [(1, None)]
        return [(-1, lambda: p.z >= k), (1, lambda: p.z + k < n)]

    def each(self, k, step):
        for sign, when in self.sides(k):
            go = functools.partial(step, sign, sign * k)
            if when is not None:
                pl.when(when())(go)
            else:
                go()

    def arrived(self, place):
        self.copy(place, self.p.over_c, self.sx).wait_recv()

    def at(self, k, x, y):
        return ((self.p.z + k) % self.p.depth, x, y, self.p.c)

    def line(self, k):
        p, n = self.p, self.p.depth

        def step(sign, far):
            place = functools.partial(self.at, far, p.x, p.y)
            self.arrived(place())
            if not self.straight:
                self.send(place, p.along_z(-sign), self.sz, (lambda: p.z + 1 < n) if sign < 0 else (lambda: p.z > 0))
            self.send(place, p.over_x, self.sx)
            self.send(place, p.over_y, self.sy)

        self.each(k, step)

    def cross(self, k):
        p = self.p

        def step(sign, far):
            self.arrived(self.at(far, 1 - p.x, p.y))
            self.arrived(self.at(far, p.x, 1 - p.y))
            z = (p.z + far) % p.depth
            if self.upright and k:
                self.pair_copy(z, p.y, p.c).start()
                return
            odd = (z + self.part) % 2
            x, y = jnp.where(odd == 1, p.x, 1 - p.x), jnp.where(odd == 1, 1 - p.y, p.y)
            to = (p.z, jnp.where(odd == 1, 1 - p.x, p.x), jnp.where(odd == 1, p.y, 1 - p.y), p.c)
            self.copy((z, x, y, p.c), to, self.sk).start()
            self.pair_copy(z, p.y, p.c).start()

        self.each(k, step)

    def corner(self, k):
        p, n = self.p, self.p.depth

        def step(sign, far):
            place = functools.partial(self.at, far, 1 - p.x, 1 - p.y)
            self.arrived(place())
            if self.upright and sign <= 0:
                self.send(place, p.along_z(1), self.sz, lambda: p.z + 1 < n)
            if self.upright and sign >= 0:
                self.send(place, p.along_z(-1), self.sz, lambda: p.z > 0)
            self.pair_copy((p.z + far) % p.depth, 1 - p.y, p.c).start()

        self.each(k, step)

    def other_core(self):
        for z in range(self.p.depth):
            for y in range(2):
                self.pair_copy(z, y, 1 - self.p.c).wait_recv()

    def flow(self):
        n = self.p.depth
        order = [1, n - 1] + list(range(2, n - 1)) if self.straight and n > 2 else list(range(1, n))
        steps = [functools.partial(self.cross, 0)]
        if self.upright:
            steps.append(functools.partial(self.corner, 0))
        for k in order:
            steps += [functools.partial(self.line, k), functools.partial(self.cross, k)]
            if self.upright:
                steps.append(functools.partial(self.corner, k))
        if not self.upright:
            steps += [functools.partial(self.corner, k) for k in range(n)]
        steps.append(self.other_core)
        return steps

    def finish(self):
        n, r = self.p.depth, self.rows

        def left(ref, sem):
            pltpu.make_async_copy(ref, ref, sem.at[self.part]).wait()

        for sem in (self.sx, self.sy):
            left(self.full.at[0, 0 : n * r, :], sem)
        left(self.full.at[0, 0 : r if self.upright else n * r, :], self.sk)
        left(self.full.at[0:2], self.sc)
        if self.straight:
            left(self.full.at[0, 0 : (n - 1) * r, :], self.sz)
        else:
            for z in range(n):
                count = (z + 1 if z + 1 < n else 0) + (n - z if z > 0 else 0)
                if count:
                    ref = self.full.at[0 : 2 if self.upright else 1, 0 : count * r, :]
                    pl.when(self.p.z == z)(functools.partial(left, ref, self.sz))


class Exchange:
    def __init__(self, p, full, sems):
        self.p, self.full = p, full
        self.sent, self.recv, self.core_sent, self.core_recv = sems

    def spot(self, place):
        z, x, y, c = place
        return self.full.at[c, pl.ds(pl.multiple_of(((z * 2 + x) * 2 + y) * 8, 8), 8), :]

    def copy(self, i, far):
        ref = self.spot(self.p.me)
        return remote(ref, ref, self.sent.at[0], self.recv.at[i], self.p.chip(*far))

    def core_copy(self):
        ref = self.full.at[self.p.c]
        return remote(ref, ref, self.core_sent.at[0], self.core_recv.at[0], self.p.over_c)

    def start(self):
        for i, far in enumerate(self.p.others()):
            self.copy(i, far).start()

    def finish(self):
        others = self.p.others()
        for i, far in enumerate(others):
            self.copy(i, far).wait_recv()
        self.core_copy().start()
        self.core_copy().wait()
        left = self.full.at[0, 0 : 8 * len(others), :]
        pltpu.make_async_copy(left, left, self.sent.at[0]).wait()


def exchange_sems(n):
    dma = pltpu.SemaphoreType.DMA
    return [dma((1,)), dma((4 * n,)), dma((1,)), dma((1,))]


def gather_sems(parts, n):
    dma = pltpu.SemaphoreType.DMA
    return [dma((parts, 8 * n)), dma((parts, 2 * n))] + [dma((parts,))] * 5


class Scatter:
    def __init__(self, p, part, rows, grads, out, bufs, temp, load, sems):
        self.p, self.part, self.rows, self.grads, self.out, self.temp, self.load = p, part, rows, grads, out, temp, load
        self.b_core, self.b_corner, self.b_cross, self.b_line = bufs
        self.ss, self.rs, self.sc, self.rc, self.sx, self.rx, self.sl, self.rl = sems

    def slab(self, y):
        return self.grads(y * 2 + self.p.c)

    def span(self, z, x):
        return pl.ds(pl.multiple_of((z * 2 + x) * self.rows, 16), self.rows)

    def which(self, k):
        return self.p.y if k else 1 - self.p.y

    def core_copy(self, k):
        p, q = self.p, self.part
        return remote(self.grads(self.which(k) * 2 + 1 - p.c), self.b_core.at[k], self.ss.at[q], self.rs.at[q, k], p.over_c)

    def core(self, k):
        self.core_copy(k).start()

    def pulled(self, k):
        return pltpu.make_async_copy(self.b_core.at[k], self.temp, self.load)

    def pull(self, k):
        self.core_copy(k).wait_recv()
        self.pulled(k).start()

    def add(self, k):
        r = self.rows
        slab = self.slab(self.which(k))
        self.pulled(k).wait()

        def one(i, _):
            s = pl.ds(pl.multiple_of(i * r, 16), r)
            slab[s, :] = (slab[s, :].astype(f32) + self.temp[s, :].astype(f32)).astype(bf16)
            return 0

        lax.fori_loop(0, 2 * self.p.depth, one, 0)

    def corner_copy(self, z):
        p, q = self.p, self.part
        src = self.slab(1 - p.y).at[self.span(z, 1 - p.x), :]
        return remote(src, self.b_corner.at[z], self.sc.at[q], self.rc.at[q, z], p.over_x if (z + q) % 2 else p.over_y)

    def corner(self):
        for z in range(self.p.depth):
            self.corner_copy(z).start()

    def cross_copy(self, z, way):
        p, q = self.p, self.part
        src = self.slab(1 - p.y).at[self.span(z, p.x), :] if way else self.slab(p.y).at[self.span(z, 1 - p.x), :]
        to = p.over_y if way else p.over_x
        return remote(src, self.b_cross.at[way, z], self.sx.at[q], self.rx.at[q, way, z], to)

    def cross(self, z):
        self.corner_copy(z).wait_recv()
        p = self.p
        slab, s = (self.slab(1 - p.y), self.span(z, p.x)) if (z + self.part) % 2 else (self.slab(p.y), self.span(z, 1 - p.x))
        slab[s, :] = (slab[s, :].astype(f32) + self.b_corner[z].astype(f32)).astype(bf16)
        for way in range(2):
            self.cross_copy(z, way).start()

    def line_copy(self, k):
        p, q = self.p, self.part
        z = (p.z + k) % p.depth
        return remote(self.slab(p.y).at[self.span(z, p.x), :], self.b_line.at[k], self.sl.at[q], self.rl.at[q, k], p.along_z(k))

    def column(self, z):
        p = self.p
        for way in range(2):
            self.cross_copy(z, way).wait_recv()
        return self.slab(p.y)[self.span(z, p.x), :].astype(f32) + self.b_cross[0, z].astype(f32) + self.b_cross[1, z].astype(f32)

    def line(self, k):
        p = self.p
        z = (p.z + k) % p.depth
        self.slab(p.y)[self.span(z, p.x), :] = self.column(z).astype(bf16)
        self.line_copy(k).start()

    def last(self):
        p = self.p
        total = self.column(p.z)
        for k in range(1, p.depth):
            self.line_copy(k).wait_recv()
            total = total + self.b_line[k].astype(f32)
        self.out[...] = total

    def flow(self, early):
        call, n = functools.partial, self.p.depth
        core = [call(self.core, 0), call(self.core, 1)]
        first = [call(self.pull, 0), call(self.add, 0), self.corner]
        steps = core[:1] + first + core[1:] if early else core + first
        steps += [call(self.pull, 1), call(self.add, 1)]
        steps += [call(self.cross, z) for z in range(n)] + [call(self.line, k) for k in range(1, n)]
        return steps + [self.last]

    def finish(self):
        q = self.part
        for ref, sem in ((self.b_core, self.ss), (self.b_corner, self.sc), (self.b_cross, self.sx), (self.b_line.at[1 : self.p.depth], self.sl)):
            pltpu.make_async_copy(ref, ref, sem.at[q]).wait()


def scatter_bufs(n, rows, width):
    return [pltpu.VMEM((n, rows, width), bf16), pltpu.VMEM((2, n, rows, width), bf16), pltpu.VMEM((n, rows, width), bf16)]


def scatter_sems(parts, n):
    dma = pltpu.SemaphoreType.DMA
    return [dma((parts,)), dma((parts, 2)), dma((parts,)), dma((parts, n)), dma((parts,)), dma((parts, 2, n)), dma((parts,)), dma((parts, n))]


def split3(row):
    hi = row.astype(bf16).astype(f32)
    mid = (row - hi).astype(bf16).astype(f32)
    return hi, mid, row - hi - mid


def aug_rows(*rows):
    width = rows[0].shape[1]
    at = lax.broadcasted_iota(jnp.int32, (16, width), 0)
    out = jnp.zeros((16, width), f32)
    for i, row in enumerate(rows):
        out = jnp.where(at == i, row, out)
    return out.astype(bf16)


def norm(r):
    cent = r - jnp.mean(r, axis=1, keepdims=True)
    rstd = lax.rsqrt(jnp.mean(cent * cent, axis=1, keepdims=True) + eps_norm)
    return cent * rstd, rstd


def any_spec(n):
    return [pl.BlockSpec(memory_space=pl.ANY)] * n


def vmem_spec(n):
    return [pl.BlockSpec(memory_space=pltpu.VMEM)] * n


def run(steps):
    for step in steps:
        step()


def at_step(index, hooks):
    for k, steps in hooks.items():
        if steps:
            pl.when(index == k)(functools.partial(run, steps))


NJ = HC // HD
ROWS = 256
CHUNKS = LEN // ROWS
PARTS = 6

PRE = ((0, 0), (3, 0), (2, 0), (1, 0), (0, 1), (3, 1), (0, 2), (3, 2), (1, 1), (1, 2), (2, 1), (3, 3), (3, 4), (4, 0), (1, 3), (0, 3), (0, 4), (2, 2), (1, 4), (4, 1), (2, 3), (3, 5), (3, 6), (1, 5), (0, 5), (1, 6), (0, 6), (2, 4), (1, 7), (1, 8), (4, 2), (0, 7), (3, 7), (4, 3), (1, 9), (3, 8), (1, 10), (0, 8), (0, 9), (3, 9), (0, 10), (5, 0), (3, 10), (0, 11), (3, 11), (2, 5), (3, 12), (2, 6), (0, 12))
HEAD = {1: ((1, 11),), 2: ((2, 7), (4, 4), (2, 8), (2, 9), (4, 5), (1, 12), (5, 1)), 3: ((4, 6),), 5: ((2, 10), (2, 11), (5, 2), (5, 3)), 6: ((2, 12),), 7: ((4, 7), (4, 8), (4, 9)), 10: ((4, 10), (5, 4), (5, 5), (5, 6)), 11: ((4, 11),)}
MID = ((5, 7), (4, 12), (5, 8))
LATE = {2: ((5, 9),), 11: ((5, 10), (5, 11)), 15: ((5, 12),)}
BACK = {0: ((0, 0), (1, 0)), 1: ((0, 1),), 2: ((0, 2), (0, 3), (1, 1)), 3: ((1, 2), (1, 3)), 5: ((0, 4),), 6: ((0, 5), (1, 4)), 7: ((0, 6),), 8: ((0, 7), (1, 5)), 9: ((1, 6), (0, 8), (0, 9), (0, 10)), 10: ((2, 0), (2, 1)), 11: ((1, 7),), 12: ((0, 11), (1, 8), (1, 9), (0, 12), (2, 2)), 13: ((1, 10),), 14: ((2, 3), (2, 4), (2, 5), (3, 0), (3, 1)), 15: ((2, 6), (2, 7), (2, 8), (3, 2), (1, 11)), 16: ((1, 12), (3, 3)), 17: ((3, 4), (3, 5)), 18: ((4, 0), (3, 6), (3, 7), (1, 13), (2, 9), (4, 1), (0, 13), (3, 8), (2, 10), (4, 2), (3, 9), (4, 3), (4, 4)), 19: ((2, 11), (3, 10), (4, 5), (5, 0), (2, 12), (2, 13), (5, 1), (4, 6), (5, 2), (4, 7), (5, 3), (5, 4), (4, 8), (3, 11), (5, 5), (4, 9), (1, 14), (4, 10), (3, 12), (5, 6), (5, 7), (3, 13), (5, 8), (4, 11), (5, 9), (5, 10), (4, 12), (4, 13), (0, 14), (2, 14), (5, 11), (3, 14), (5, 12), (5, 13), (4, 14), (5, 14))}


def pack(refs, wa, table, w1, w2, p, r, cb):
    qkv, out, up, down, col, row = refs
    dp, t = p.z * 2 + p.x, p.y * 2 + p.c
    at = pl.ds(pl.multiple_of(dp * r, 16), r)
    high = -(-r // 128) * 128
    out_t = jnp.concatenate([out[...], jnp.zeros((HC, high - r), f32)], axis=1)
    out_t = jnp.concatenate([out_t, jnp.zeros((256 - HC, high), f32)], axis=0).T[0:r]
    for j in range(NJ):
        s = slice(j * HD, j * HD + HD)
        wa[j, t, at, :] = jnp.concatenate([qkv[0, :, s], qkv[1, :, s], qkv[2, :, s], out_t[:, s]], axis=1).astype(bf16)
    tile = jnp.concatenate([row[...], jnp.zeros((10, r), f32)], axis=0)
    line = lax.broadcasted_iota(jnp.int32, (16, r), 0)
    for k in range(-(-cb // r)):
        wide = min(r, cb - k * r)
        piece = col[:, k * r : k * r + wide]
        if wide < r:
            piece = jnp.concatenate([piece, jnp.zeros((1, r - wide), f32)], axis=1)
        tile = jnp.where(line == 6 + k, piece, tile)
    tile = jnp.concatenate([tile, jnp.zeros((16, 128 - r), f32)], axis=1)
    own = pl.multiple_of(dp * 32, 32)
    table[t, pl.ds(own, 16), :] = tile.astype(bf16)
    table[t, pl.ds(pl.multiple_of(own + 16, 16), 16), :] = jnp.zeros((16, 128), bf16)
    w1[t, at, :] = up[...].astype(bf16)
    w2[t, at, :] = down[...].astype(bf16)


def loss_pull(pooled, groups, index):
    count = pooled.shape[0]
    inv = lax.rsqrt(jnp.sum(pooled * pooled, axis=1, keepdims=True) + eps_norm)
    unit = pooled * inv
    similar = temper * lax.dot_general(unit, unit, (((1,), (1,)), ((), ())), precision=highest, preferred_element_type=f32)
    rows = lax.broadcasted_iota(jnp.int32, (count, count), 0)
    cols = lax.broadcasted_iota(jnp.int32, (count, count), 1)
    others = jnp.where(rows == cols, masked, similar)
    members = groups.astype(f32)
    eye = jnp.where(rows == cols, 1.0, 0.0).astype(bf16)
    turned = nt(eye, members.astype(bf16))

    def pull(table, axis):
        top = jnp.max(others, axis=axis, keepdims=True)
        e = jnp.exp(others - top)
        return e / jnp.sum(e, axis=axis, keepdims=True) - table / jnp.sum(table, axis=axis, keepdims=True)

    both = temper * (pull(members, 1) + pull(turned, 0))
    grad = lax.dot_general(both, unit, (((1,), (0,)), ((), ())), precision=highest, preferred_element_type=f32)
    own = lax.broadcasted_iota(jnp.int32, (count, 1), 0) == index

    def pick(v):
        return jnp.sum(jnp.where(own, v, 0.0), axis=0, keepdims=True)

    unit, grad = pick(unit), pick(grad)
    return pick(inv) * (grad - unit * jnp.sum(unit * grad, axis=1, keepdims=True))


def forward_kernel(n, cb, comm, *refs):
    dp = 2 * n
    r = D // dp
    given, refs = (6, refs[:2] + refs[2:]) if comm else (4, refs)
    len_ref, groups_ref, x_ref = refs[:3]
    weights_in, refs = refs[3 : 3 + given], refs[3 + given :]
    (rstd1_ref, rstd2_ref, gain_ref, row_ref, hb_ref, u_ref,
     out_out, h1_out, xhat1_out, g_out, xhat2_out, ct_out, xt_out, gp_out, q_out, k_out, v_out, wa_out, w1_out, w2_out,
     out_ref, h1_ref, xhat1_ref, g_ref, xhat2_ref, ct_ref, xt,
     wa, w1, w2, table, bcol, col, qt, kt, vt, kn, sb, wo, pool, stage, every, pooled,
     local, q_sem, stage_sem, o_sem, *sems) = refs
    length = len_ref[lax.axis_index("tensor")]
    hooks, middle, late = {}, [], {}
    if comm:
        p = Place(n)
        count = greet(p, True)
        pack(weights_in, wa, table, w1, w2, p, r, cb)
        enter(count)
        wholes = [wa.at[j] for j in range(NJ)] + [table, w1, w2]
        parts = [Gather(p, i, full, sems[:7], i == NJ, i > NJ) for i, full in enumerate(wholes)]
        pools = Exchange(p, every, sems[7:])
        flows = [[g.start] + g.flow() for g in parts]

        def steps(pairs):
            return [flows[g][k] for g, k in pairs]

        if n == 4:
            run(steps(PRE[:5]))
            xt[...] = x_ref[...].T
            run(steps(PRE[5:]))
            hooks = {h: steps(pairs) for h, pairs in HEAD.items()}
            middle = steps(MID)
            late = {h: steps(pairs) for h, pairs in LATE.items()}
        else:
            xt[...] = x_ref[...].T
            for group in zip(*flows):
                run(group)
    else:
        loads = [pltpu.make_async_copy(src, dst, local.at[i]) for i, (src, dst) in enumerate(zip(weights_in, (wa, table, w1, w2)))]
        for cp in loads:
            cp.start()
        xt[...] = x_ref[...].T
        for cp in loads:
            cp.wait()
    saved = ((out_ref, out_out), (h1_ref, h1_out), (xhat1_ref, xhat1_out), (g_ref, g_out), (xhat2_ref, xhat2_out), (ct_ref, ct_out),
             (xt, xt_out), (wa, wa_out), (w1, w1_out), (w2, w2_out))

    def save(i):
        return pltpu.make_async_copy(*saved[i], o_sem.at[i])

    save(6).start()

    col_rows = -(-cb // r)
    for i in range(dp):
        rows = slice(i * 32, i * 32 + 16)
        row_ref[:, i * r : i * r + r] = table[0, rows, 0:r].astype(f32)
        for t in range(NT):
            tile = table[t, rows, :].astype(f32)
            for k in range(col_rows):
                wide = min(r, cb - k * r)
                col[t, :, i * cb + k * r : i * cb + k * r + wide] = jnp.broadcast_to(tile[6 + k : 7 + k, 0:wide], (8, wide))
    for t in range(NT):
        bcol[t] = jnp.transpose(col[t, :, 0 : 2 * HC])[:, 0:1]
        hb_ref[t] = col[t, 0:1, 2 * HC : 2 * HC + D]

    ones = jnp.ones((1, LEN), f32)
    where = lax.broadcasted_iota(jnp.int32, (1, LEN), 1)
    key_bias = jnp.where(where < length, 0.0, masked).astype(f32)
    kept = ((qt, q_out), (kt, k_out), (vt, v_out))
    key_rows = aug_rows(key_bias, ones, ones, ones)
    one_row = aug_rows(ones)
    half = LEN // 2

    def project(h):
        j, t = h // NT, h % NT
        qkv = tn(wa[j, t, :, 0 : 3 * HD], xt[...])
        qt[h, 0:HD, :] = ((qkv[0:HD] + bcol[t, pl.ds(pl.multiple_of(j * HD, HD), HD), :]) * HD**-0.5).astype(bf16)
        kt[h, 0:HD, :] = qkv[HD : 2 * HD].astype(bf16)
        vt[h] = (qkv[2 * HD : 3 * HD] + bcol[t, pl.ds(pl.multiple_of(HC + j * HD, HD), HD), :]).astype(bf16)
        qt[h, HD:AUG, :] = one_row
        kt[h, HD:AUG, :] = key_rows
        kn[h % 2] = kt[h].T

    def attend(h, i, s):
        where = slice(i * half, i * half + half)
        top = jnp.max(s, axis=0, keepdims=True)
        e = jnp.exp(s - top)
        total = jnp.sum(e, axis=0, keepdims=True)
        ct_ref[pl.ds(pl.multiple_of(h * HD, HD), HD), where] = (nn(vt[h], e.astype(bf16)) * (1.0 / total)).astype(bf16)
        hi, mid, lo = split3(-(top + jnp.log(total)))
        qt[h, HD:AUG, where] = aug_rows(ones[:, where], hi, mid, lo)

    project(0)
    sb[0] = nn(kn[0], qt[0, :, 0:half])

    def head(h, _):
        after = nn(kn[h % 2], qt[h, :, half:LEN])
        attend(h, 0, sb[0])
        sb[1] = after
        nxt = jnp.minimum(h + 1, H - 1)

        @pl.when(h + 1 < H)
        def _():
            project(nxt)

        after = nn(kn[nxt % 2], qt[nxt, :, 0:half])
        attend(h, 1, sb[1])
        sb[0] = after
        for i, (src, dst) in enumerate(kept):
            pltpu.make_async_copy(src.at[h], dst.at[h], q_sem.at[i, h]).start()
        at_step(h, hooks)
        return 0

    lax.fori_loop(0, H, head, 0)
    save(5).start()

    c_nat = out_ref
    c_nat[...] = ct_ref[...].T
    for j in range(NJ):
        for t in range(NT):
            h = j * NT + t
            wo[:, h * HD : h * HD + HD] = wa[j, t, :, 3 * HD : 4 * HD]
    save(7).start()

    def first(i, _):
        s = pl.ds(pl.multiple_of(i * ROWS, ROWS), ROWS)
        r1 = x_ref[s, :].astype(f32) + (nt(c_nat[s, :], wo[...]) + row_ref[0:1])
        xhat, rstd = norm(r1)
        xhat1_ref[s, :] = xhat
        rstd1_ref[s, :] = rstd
        h1_ref[s, :] = (xhat * row_ref[1:2] + row_ref[2:3]).astype(bf16)
        return 0

    lax.fori_loop(0, CHUNKS, first, 0)
    save(1).start()
    save(2).start()
    run(middle)

    def staged(step):
        t, i = step // CHUNKS, step % CHUNKS
        s = pl.ds(pl.multiple_of(i * ROWS, ROWS), ROWS)
        return pltpu.make_async_copy(stage.at[step % 2], gp_out.at[t, s, :], stage_sem.at[step % 2])

    def hidden(step, _):
        t, i = step // CHUNKS, step % CHUNKS
        s = pl.ds(pl.multiple_of(i * ROWS, ROWS), ROWS)
        z = nn(h1_ref[s, :], w1[t]) + hb_ref[t]
        cdf = 0.5 + 0.5 * lax.erf(z * 0.5**0.5)
        g_ref[t, s, :] = (z * cdf).astype(bf16)

        @pl.when(step >= 2)
        def _():
            staged(step - 2).wait()

        stage[step % 2] = cdf + z * (jnp.exp(-0.5 * z * z) * 0.3989422804014327)
        staged(step).start()
        at_step(step, late)
        return 0

    lax.fori_loop(0, NT * CHUNKS, hidden, 0)
    staged(NT * CHUNKS - 2).wait()
    staged(NT * CHUNKS - 1).wait()
    for i in (3, 8, 9):
        save(i).start()
    gain_ref[...] = jnp.zeros_like(gain_ref)
    pool[...] = jnp.zeros_like(pool)

    def second(i, _):
        s = pl.ds(pl.multiple_of(i * ROWS, ROWS), ROWS)
        res = xhat1_ref[s, :] * row_ref[1:2] + row_ref[2:3] + row_ref[3:4]
        for t in range(NT):
            res = res + nt(g_ref[t, s, :], w2[t])
        xhat, rstd = norm(res)
        xhat2_ref[s, :] = xhat
        rstd2_ref[s, :] = rstd
        y = xhat * row_ref[4:5] + row_ref[5:6]
        out_ref[s, :] = y.astype(bf16)
        here = i * ROWS + lax.broadcasted_iota(jnp.int32, (ROWS, 1), 0) < length
        pool[0:1] += jnp.sum(jnp.where(here, y, 0.0), axis=0, keepdims=True)
        gain_ref[...] += jnp.sum(jnp.where(here, xhat, 0.0), axis=0, keepdims=True)
        return 0

    lax.fori_loop(0, CHUNKS, second, 0)
    size = jnp.full((1, 1), length).astype(f32)
    mean = pool[0:1] / size
    if comm:
        block = [mean[:, i * 128 : i * 128 + 128] for i in range(D // 128)] + [jnp.zeros((8 - D // 128, 128), f32)]
        every[p.c, pl.ds(pl.multiple_of(((p.z * 2 + p.x) * 2 + p.y) * 8, 8), 8), :] = jnp.concatenate(block, axis=0)
        pools.start()
    save(0).start()
    save(4).start()
    if comm:
        pools.finish()
        for i in range(dp):
            for t in range(NT):
                at = (i * 2 + t // 2) * 8
                for k in range(D // 128):
                    pooled[i * NT + t : i * NT + t + 1, k * 128 : k * 128 + 128] = every[t % 2, at + k : at + k + 1, :]
        u_ref[...] = loss_pull(pooled[...], groups_ref[...], lax.axis_index("dp") * NT + lax.axis_index("tensor")) / size
        for g in parts:
            g.finish()
    else:
        u_ref[...] = mean
    for h in range(H):
        for i, (src, dst) in enumerate(kept):
            pltpu.make_async_copy(src.at[h], dst.at[h], q_sem.at[i, h]).wait()
    for i in range(len(saved)):
        save(i).wait()


def forward(length, groups, x, weights, n, cb, comm):
    s = jax.ShapeDtypeStruct
    dp = 2 * n
    r = D // dp
    dma = pltpu.SemaphoreType.DMA
    shapes = [s((LEN, 1), f32), s((LEN, 1), f32), s((1, D), f32), s((16, D), f32), s((NT, 1, D), f32), s((1, D), f32)]
    big = [s((LEN, D), bf16), s((LEN, D), bf16), s((LEN, D), f32), s((NT, LEN, D), bf16), s((LEN, D), f32), s((D, LEN), bf16), s((D, LEN), bf16)]
    kept = [
        s((NT, LEN, D), f32), s((H, AUG, LEN), bf16), s((H, AUG, LEN), bf16), s((H, HD, LEN), bf16),
        s((NJ, NT, D, 4 * HD), bf16), s((NT, D, D), bf16), s((NT, D, D), bf16),
    ]
    scratch = [pltpu.VMEM(v.shape, v.dtype) for v in big] + [
        pltpu.VMEM((NJ, NT, D, 4 * HD), bf16), pltpu.VMEM((NT, D, D), bf16), pltpu.VMEM((NT, D, D), bf16),
        pltpu.VMEM((NT, dp * 32, 128), bf16), pltpu.VMEM((NT, 2 * HC, 1), f32), pltpu.VMEM((NT, 8, dp * cb), f32),
        pltpu.VMEM((H, AUG, LEN), bf16), pltpu.VMEM((H, AUG, LEN), bf16), pltpu.VMEM((H, HD, LEN), bf16),
        pltpu.VMEM((2, LEN, AUG), bf16), pltpu.VMEM((2, LEN, LEN // 2), f32),
        pltpu.VMEM((D, D), bf16), pltpu.VMEM((8, D), f32), pltpu.VMEM((2, ROWS, D), f32),
        pltpu.VMEM((2, dp * 16, 128), f32), pltpu.VMEM((dp * NT, D), f32),
        dma((PARTS,)), dma((3, H)), dma((2,)), dma((len(big) + 3,)),
    ]
    if comm:
        scratch += gather_sems(PARTS, n) + exchange_sems(n)
        params = pltpu.CompilerParams(collective_id=0, has_side_effects=True, vmem_limit_bytes=VMEM_CAP)
    else:
        params = pltpu.CompilerParams(vmem_limit_bytes=VMEM_CAP)
    return pl.pallas_call(
        functools.partial(forward_kernel, n, cb, comm),
        out_shape=shapes + big + kept,
        in_specs=[pl.BlockSpec(memory_space=pltpu.SMEM)] + vmem_spec(2) + (vmem_spec(6) if comm else any_spec(4)),
        out_specs=vmem_spec(len(shapes)) + any_spec(len(big) + len(kept)),
        scratch_shapes=scratch,
        compiler_params=params,
    )(length, groups, x, *weights)


def backward_kernel(n, cb, comm, *refs):
    dp = 2 * n
    r = D // dp
    (len_ref, u_ref, gain_ref, rstd1_ref, rstd2_ref, row_ref,
     xhat2_in, xhat1_in, w1_in, w2_in, wa_in, g_in, gp_in, h1_in, ct_in, xt_in, q_in, k_in, v_in, *refs) = refs
    dx_out, *refs = refs
    outs, refs = refs[: NJ + 3], refs[NJ + 3 :]
    landing, refs = (refs[: NJ + 3], refs[NJ + 3 :]) if comm else ([], refs)
    (wa, w1, w2, t1, t2, dqkv, xt, ct, df, dz, dh, sd, pp, turned, qkv, wcat, grow, ghb, gcol, gbias,
     load, s_load, q_sem, x_sem, *refs) = refs
    length = len_ref[lax.axis_index("tensor")]
    hooks, after, ends = {}, {}, [[], [], []]
    grads = [wa.at[j] for j in range(NJ)]
    h1t, dft, dat, dct = t1, t2, t1, t2

    loads = [
        pltpu.make_async_copy(src, dst, load.at[i])
        for i, (src, dst) in enumerate(
            ((xhat2_in, sd.at[1, :, 0:D]), (w2_in, w2), (h1_in, dz), (w1_in, w1), (wa_in, wa), (ct_in, ct), (xt_in, xt))
        )
    ]

    def fetch(step):
        t = part_of(step)
        return [
            pltpu.make_async_copy(src.at[t], dst.at[step % 2, :, 0:D], s_load.at[step % 2, i])
            for i, (src, dst) in enumerate(((g_in, pp), (gp_in, sd)))
        ]

    if comm:
        p = Place(n)

        def part_of(step):
            y = jnp.where(step < 2, 1 - p.y, p.y)
            return y * 2 + jnp.where(step % 2 == 0, 1 - p.c, p.c)
    else:

        def part_of(step):
            return step

    for cp in loads[:2]:
        cp.start()
    for cp in fetch(0):
        cp.start()
    for cp in loads[2:]:
        cp.start()
    if comm:
        temp, *refs = refs
        bufs, sems = refs[:-8], refs[-8:]
        count = greet(p)
        where = [(lambda t: w1.at[t]), (lambda t: w2.at[t])] + [(lambda t, g=g: g.at[t]) for g in grads] + [lambda t: gbias.at[t]]
        parts = []
        for i, source in enumerate(where):
            rows, width = outs[i].shape
            parts.append(
                Scatter(p, i, rows, source, outs[i], [landing[i]] + list(bufs[3 * i : 3 * i + 3]),
                        temp.at[0 : 2 * n * rows, 0:width], x_sem.at[0], sems)
            )
        flows = [part.flow(i < 2) for i, part in enumerate(parts)]

        def steps(pairs):
            return [flows[g][k] for g, k in pairs]

        if n == 4:
            plan = {slot: steps(pairs) for slot, pairs in BACK.items()}
        else:
            plan = {1: steps([(g, k) for g in range(2) for k in range(4)]), 3: steps([(g, k) for g in range(2) for k in range(4, 7)])}
            plan[6] = [step for flow in flows[:2] for step in flow[7:]]
            for j in range(NJ):
                plan[7 + j * NT + NT - 1] = flows[2 + j]
            plan[7 + H] = flows[-1]
        after = {k: plan.get(k, []) for k in range(NT)}
        hooks = {h: plan.get(7 + h, []) for h in range(H)}
        ends = [plan.get(5, []), plan.get(6, []), plan.get(7 + H, [])]

    u = u_ref[...]
    du = u * row_ref[4:5]
    mean_du = jnp.mean(du, axis=1, keepdims=True)
    grow[...] = jnp.zeros_like(grow)
    loads[0].wait()

    def outer(i, _):
        s = pl.ds(pl.multiple_of(i * ROWS, ROWS), ROWS)
        here = i * ROWS + lax.broadcasted_iota(jnp.int32, (ROWS, 1), 0) < length
        hat = sd[1, s, 0:D]
        dot = jnp.mean(hat * du, axis=1, keepdims=True)
        dr = jnp.where(here, rstd2_ref[s, :] * (du - mean_du - hat * dot), 0.0)
        dh[s, :] = dr
        low = dr.astype(bf16)
        df[s, :] = low
        grow[3:4] += jnp.sum(low.astype(f32), axis=0, keepdims=True)
        return 0

    lax.fori_loop(0, CHUNKS, outer, 0)
    if comm:
        enter(count)
    grow[4:5] = u * gain_ref[...]
    grow[5:6] = u * jnp.full((1, 1), length).astype(f32)
    dft[...] = df[...].T
    loads[2].wait()
    h1t[...] = dz[...].T
    last_hat = pltpu.make_async_copy(xhat1_in, sd.at[0, :, 0:D], load.at[0])
    loads[1].wait()
    loads[3].wait()

    def hidden(step, _):
        t = part_of(step)
        slot = step % 2
        for cp in fetch(step):
            cp.wait()

        @pl.when(step + 1 < NT)
        def _():
            for cp in fetch(step + 1):
                cp.start()

        hb = jnp.zeros((1, D), f32)
        for i in range(CHUNKS):
            s = pl.ds(i * ROWS, ROWS)
            low = (nn(df[s, :], w2[t]) * sd[slot, s, 0:D]).astype(bf16)
            dz[s, :] = low
            hb = hb + jnp.sum(low.astype(f32), axis=0, keepdims=True)
            dh[s, :] += nt(low, w1[t])
        ghb[t] = hb
        for i in range(D // ROWS):
            s = slice(i * ROWS, (i + 1) * ROWS)
            w1[t, s, :] = nn(h1t[s, :], dz[...]).astype(bf16)
            w2[t, s, :] = nn(dft[s, :], pp[slot, :, 0:D]).astype(bf16)
        pl.when(step == NT - 2)(last_hat.start)
        at_step(step, after)
        return 0

    lax.fori_loop(0, NT, hidden, 0)

    def fetch_head(h, slot):
        return [
            pltpu.make_async_copy(src.at[h], qkv.at[slot, i, 0 : src.shape[1], :], q_sem.at[slot, i])
            for i, src in enumerate((q_in, k_in, v_in))
        ]

    for cp in fetch_head(0, 0):
        cp.start()
    last_hat.wait()

    def inner_norm(i, _):
        s = pl.ds(pl.multiple_of(i * ROWS, ROWS), ROWS)
        d = dh[s, :]
        hat = sd[0, s, 0:D]
        grow[1:2] += jnp.sum(d * hat, axis=0, keepdims=True)
        grow[2:3] += jnp.sum(d, axis=0, keepdims=True)
        dn = d * row_ref[1:2]
        dr = rstd1_ref[s, :] * (dn - jnp.mean(dn, axis=1, keepdims=True) - hat * jnp.mean(dn * hat, axis=1, keepdims=True))
        dh[s, :] = dr
        low = dr.astype(bf16)
        grow[0:1] += jnp.sum(low.astype(f32), axis=0, keepdims=True)
        df[s, :] = low
        return 0

    lax.fori_loop(0, CHUNKS, inner_norm, 0)
    dat[...] = df[...].T
    run(ends[0])
    loads[4].wait()
    loads[5].wait()
    for j in range(NJ):
        for t in range(NT):
            h = j * NT + t
            wcat[:, h * HD : h * HD + HD] = wa[j, t, :, 3 * HD : 4 * HD]
    for i in range(D // ROWS):
        s = slice(i * ROWS, (i + 1) * ROWS)
        dct[s, :] = tn(wcat[:, s], dat[...]).astype(bf16)
        gwo = nt(dat[s, :], ct[...]).astype(bf16)
        for j in range(NJ):
            for t in range(NT):
                h = j * NT + t
                wa[j, t, s, 3 * HD : 4 * HD] = gwo[:, h * HD : h * HD + HD]
    loads[6].wait()
    run(ends[1])

    def head(h, _):
        j, t = h // NT, h % NT
        slot = h % 2
        for cp in fetch_head(h, slot):
            cp.wait()

        @pl.when(h + 1 < H)
        def _():
            for cp in fetch_head(h + 1, 1 - slot):
                cp.start()

        own = pl.ds(pl.multiple_of(h * HD, HD), HD)
        prob = jnp.exp(tn(qkv[slot, 0], qkv[slot, 1]))
        sd[0] = prob
        sd[1] = tn(dct[own, :], qkv[slot, 2, 0:HD, :])
        pp[0] = prob.astype(bf16)
        inner = jnp.sum(sd[0] * sd[1], axis=1, keepdims=True)
        pp[1] = (sd[0] * (sd[1] - inner)).astype(bf16)
        turned[...] = pp[1].T
        at = pl.multiple_of(t * 3 * HD, HD)
        dqkv[pl.ds(at + HD, HD), :] = nn(qkv[slot, 0, 0:HD, :], pp[1]).astype(bf16)
        dqkv[pl.ds(at + 2 * HD, HD), :] = nn(dct[own, :], pp[0]).astype(bf16)
        dqkv[pl.ds(at, HD), :] = (nn(qkv[slot, 1, 0:HD, :], turned[...]) * HD**-0.5).astype(bf16)

        @pl.when(t == NT - 1)
        def _():
            for k in range(NT):
                wcat[:, k * 3 * HD : (k + 1) * 3 * HD] = wa[j, k, :, 0 : 3 * HD]
            sums = nt(jnp.ones((16, LEN), bf16), dqkv[...])
            for k in range(NT):
                gcol[j, k] = sums[0:8, k * 3 * HD : (k + 1) * 3 * HD]
            for i in range(D // ROWS):
                s = slice(i * ROWS, (i + 1) * ROWS)
                g = nt(xt[s, :], dqkv[...]).astype(bf16)
                for k in range(NT):
                    wa[j, k, s, 0 : 3 * HD] = g[:, k * 3 * HD : (k + 1) * 3 * HD]
        at_step(h, hooks)

        @pl.when(t == NT - 1)
        def _():
            for i in range(CHUNKS):
                s = slice(i * ROWS, (i + 1) * ROWS)
                dh[s, :] += lax.dot_general(dqkv[:, s], wcat[...], (((0,), (1,)), ((), ())), preferred_element_type=f32)

        return 0

    lax.fori_loop(0, H, head, 0)
    dx = pltpu.make_async_copy(dh, dx_out, load.at[0])
    dx.start()

    col_rows = -(-cb // r)
    cols = []
    for t in range(NT):
        pieces = [gcol[j, t, 0:1, 0:HD] for j in range(NJ)] + [gcol[j, t, 0:1, 2 * HD : 3 * HD] for j in range(NJ)]
        cols.append(jnp.concatenate(pieces + [ghb[t]], axis=1))
    at = lax.broadcasted_iota(jnp.int32, (32, 128), 0)
    for i in range(dp):
        rows = jnp.pad(grow[0:8, i * r : i * r + r], ((0, 24), (0, 128 - r)))
        for t in range(NT):
            block = jnp.where(at < 6, rows, 0.0)
            for k in range(col_rows):
                wide = min(r, cb - k * r)
                piece = cols[t][:, i * cb + k * r : i * cb + k * r + wide]
                block = jnp.where(at == 6 + k, jnp.pad(piece, ((0, 0), (0, 128 - wide))), block)
            gbias[t, i * 32 : i * 32 + 32, :] = block.astype(bf16)
    run(ends[2])
    if comm:
        for part in parts:
            part.finish()
    else:
        copies = [pltpu.make_async_copy(src, dst, load.at[1 + i]) for i, (src, dst) in enumerate(zip([w1, w2] + grads + [gbias], outs))]
        for cp in copies:
            cp.start()
        for cp in copies:
            cp.wait()
    dx.wait()


def backward(length, u, gain, rstd1, rstd2, row, big, n, cb, comm):
    s = jax.ShapeDtypeStruct
    dp = 2 * n
    r = D // dp
    dma = pltpu.SemaphoreType.DMA
    widths = [(r, D), (r, D)] + [(r, 4 * HD)] * NJ + [(32, 128)]
    if comm:
        sums = [s(shape, f32) for shape in widths]
        landing = [s((2, dp * rows, wide), bf16) for rows, wide in widths]
        specs = vmem_spec(len(sums)) + any_spec(len(landing))
    else:
        sums = [s((NT, dp * rows, wide), bf16) for rows, wide in widths]
        landing = []
        specs = any_spec(len(sums))
    turned = pltpu.VMEM((D, LEN), bf16)
    rows_low = pltpu.VMEM((LEN, D), bf16)
    rows_full = pltpu.VMEM((LEN, D), f32)
    scratch = [
        pltpu.VMEM((NJ, NT, D, 4 * HD), bf16), pltpu.VMEM((NT, D, D), bf16), pltpu.VMEM((NT, D, D), bf16),
        turned, turned, turned, turned, turned, rows_low, rows_low, rows_full,
        pltpu.VMEM((2, LEN, LEN), f32), pltpu.VMEM((2, LEN, LEN), bf16), pltpu.VMEM((LEN, LEN), bf16), pltpu.VMEM((2, 3, AUG, LEN), bf16), pltpu.VMEM((D, D), bf16),
        pltpu.VMEM((16, D), f32), pltpu.VMEM((NT, 1, D), f32), pltpu.VMEM((NJ, NT, 8, 3 * HD), f32), pltpu.VMEM((NT, dp * 32, 128), bf16),
        dma((8,)), dma((2, 2)), dma((2, 3)), dma((1,)),
    ]
    if comm:
        scratch += [pltpu.VMEM((D, D), bf16)]
        for rows, wide in widths:
            scratch += scatter_bufs(n, rows, wide)
        scratch += scatter_sems(len(widths), n)
        params = pltpu.CompilerParams(collective_id=1, has_side_effects=True, vmem_limit_bytes=VMEM_CAP)
    else:
        params = pltpu.CompilerParams(vmem_limit_bytes=VMEM_CAP)
    return pl.pallas_call(
        functools.partial(backward_kernel, n, cb, comm),
        out_shape=[s((LEN, D), f32)] + sums + landing,
        in_specs=[pl.BlockSpec(memory_space=pltpu.SMEM)] + vmem_spec(5) + any_spec(len(big)),
        out_specs=any_spec(1) + specs,
        scratch_shapes=scratch,
        compiler_params=params,
    )(length, u, gain, rstd1, rstd2, row, *big)


def adam_kernel(cb, *refs):
    ins, outs, refs = refs[:32], refs[32:58], refs[58:]
    held, new, sem_in, sem_out = refs[:32], refs[32:56], refs[56], refs[57]
    inward = [pltpu.make_async_copy(src, dst, sem_in.at[i]) for i, (src, dst) in enumerate(zip(ins, held))]
    outward = [pltpu.make_async_copy(src, dst, sem_out.at[i]) for i, (src, dst) in enumerate(zip((*held[:2], *new), outs))]
    for cp in inward:
        cp.start()
    moved, sums, old = held[:2], held[2:8], held[8:]
    gw1, gw2, ga, gbias = sums[0], sums[1], sums[2:5], sums[5]
    r = gw1.shape[0]

    def wide(k):
        return jnp.concatenate([ga[j][:, k * HD : k * HD + HD] for j in range(NJ)], axis=1)

    def group(i):
        for k in range(4):
            inward[8 + 4 * i + k].wait()

    def update(i, grad, rate, at=()):
        where = at + (Ellipsis,)
        out = adam_update(*[old[4 * i + k][where] for k in range(4)], grad, rate)
        for k, v in enumerate(out):
            new[4 * i + k][where] = v

    def leave(*at):
        for i in at:
            outward[i].start()

    for i in range(2):
        inward[i].wait()
    leave(0, 1)
    for i in range(2, 8):
        inward[i].wait()
    group(0)
    for k in range(3):
        update(0, wide(k), D ** (-0.5), (k,))
    leave(2, 3, 4, 5)
    group(2)
    update(2, gw1[...], D ** (-0.5))
    leave(10, 11, 12, 13)
    group(3)
    update(3, gw2[...], FF ** (-0.5))
    leave(14, 15, 16, 17)
    high = -(-r // 128) * 128
    turned = jnp.concatenate([wide(3), jnp.zeros((r, 256 - HC), f32)], axis=1)
    if high > r:
        turned = jnp.concatenate([turned, jnp.zeros((high - r, 256), f32)], axis=0)
    group(1)
    update(1, turned.T[0:HC, 0:r], D ** (-0.5))
    leave(6, 7, 8, 9)
    group(4)
    rows = gbias[...]
    pieces = [rows[6 + k : 7 + k, 0 : min(r, cb - k * r)] for k in range(-(-cb // r))]
    update(4, jnp.concatenate(pieces, axis=1), 0.1)
    group(5)
    update(5, rows[0:6, 0:r], 0.15)
    leave(*range(18, 26))
    for cp in outward:
        cp.wait()


def adam(moved, sums, olds, cb):
    flat = [v for group in olds for v in group]
    s = jax.ShapeDtypeStruct
    shapes = [s(group[0].shape, f32) for group in olds for _ in range(4)]
    ins = [*moved, *sums, *flat]
    return pl.pallas_call(
        functools.partial(adam_kernel, cb),
        out_shape=[s(v.shape, v.dtype) for v in moved] + shapes,
        in_specs=any_spec(32),
        out_specs=any_spec(26),
        scratch_shapes=[pltpu.VMEM(v.shape, v.dtype) for v in ins + shapes] + [pltpu.SemaphoreType.DMA((32,)), pltpu.SemaphoreType.DMA((26,))],
        compiler_params=pltpu.CompilerParams(vmem_limit_bytes=VMEM_CAP),
    )(*ins)


def gather_plain(own):
    return lax.all_gather(lax.all_gather(own, "dp", axis=0, tiled=True), "tensor", axis=0)


def scatter_plain(full):
    own = lax.psum_scatter(full.astype(f32), "tensor", scatter_dimension=0, tiled=False)
    return lax.psum_scatter(own, "dp", scatter_dimension=0, tiled=True)


def by_head(wide):
    return jnp.moveaxis(wide.reshape(*wide.shape[:-1], NJ, HD), -2, 0)


def packed(qkv_weight, out_weight, up_weight, down_weight, col_bias, row_params, r, cb):
    own_a = jnp.concatenate([by_head(qkv_weight[i]) for i in range(3)] + [by_head(out_weight.T)], axis=-1).astype(bf16)
    col_rows = -(-cb // r)
    col_pad = jnp.pad(col_bias[0], (0, col_rows * r - cb)).reshape(col_rows, r)
    own_b = jnp.pad(jnp.concatenate([row_params, col_pad], axis=0), ((0, 26 - col_rows), (0, 128 - r))).astype(bf16)
    return own_a, own_b, up_weight.astype(bf16), down_weight.T.astype(bf16)


def on_device(
    inputs, lengths, groups, qkv_weight, out_weight, up_weight, down_weight, col_bias, row_params,
    qkv_first, out_first, up_first, down_first, col_first, row_first,
    qkv_second, out_second, up_second, down_second, col_second, row_second,
    qkv_ema, out_ema, up_ema, down_ema, col_ema, row_ema,
):
    dp = lax.axis_size("dp")
    n = dp // 2
    r = D // dp
    cb = col_bias.shape[1]
    comm = r % 32 == 0
    if comm:
        weights = (qkv_weight, out_weight, up_weight, down_weight.T, col_bias, row_params)
    else:
        own_a, *others = packed(qkv_weight, out_weight, up_weight, down_weight, col_bias, row_params, r, cb)
        own_b, own_1, own_2 = [gather_plain(v) for v in others]
        weights = (jnp.stack([gather_plain(own_a[j]) for j in range(NJ)]), own_b, own_1, own_2)
    (rstd1, rstd2, gain, row, hb, u, outputs, h1, xhat1, g, xhat2, ct, xt, gp, qt, kt, vt, wa, w1, w2) = forward(
        lengths, groups, inputs, weights, n, cb, comm
    )
    if not comm:
        every = lax.all_gather(u, ("dp", "tensor"), axis=0, tiled=True)
        u = loss_pull(every, groups, lax.axis_index(("dp", "tensor"))) / lengths[lax.axis_index("tensor")].astype(f32)

    big = (xhat2, xhat1, w1, w2, wa, g, gp, h1, ct, xt, qt, kt, vt)
    input_grad, *sums = backward(lengths, u, gain, rstd1, rstd2, row, big, n, cb, comm)
    sums = sums[: NJ + 3] if comm else [scatter_plain(v) for v in sums]
    olds = (
        (qkv_weight, qkv_first, qkv_second, qkv_ema),
        (out_weight, out_first, out_second, out_ema),
        (up_weight, up_first, up_second, up_ema),
        (down_weight.T, down_first.T, down_second.T, down_ema.T),
        (col_bias, col_first, col_second, col_ema),
        (row_params, row_first, row_second, row_ema),
    )
    outputs, input_grad, *new = adam((outputs, input_grad), sums, olds, cb)
    new[12:16] = [v.T for v in new[12:16]]
    return (outputs, input_grad, *new)


def solution(mesh):
    tokens = P(("dp", "tensor"), None)
    placed = (P(None, "dp", "tensor"), P("tensor", "dp"), P("dp", "tensor"), P("tensor", "dp"), P("tensor", "dp"), P(None, "dp"))
    new = tuple(spec for spec in placed for _ in range(4))
    return jax.shard_map(
        on_device,
        mesh=mesh,
        in_specs=(tokens, P("dp"), P()) + placed * 4,
        out_specs=(tokens, tokens) + new,
        check_vma=False,
    )
```

```python
import functools

import jax
import jax.numpy as jnp
from jax import lax
from jax.experimental import pallas as pl
from jax.experimental.pallas import tpu as pltpu
from jax.sharding import PartitionSpec as P

D = 768
H = 12
HD = 64
FF = 3072
LEN = 1024
STEP = 5
NT = 4
HC = D // NT
AUG = 80

MESH = pl.DeviceIdType.MESH
f32 = jnp.float32
bf16 = jnp.bfloat16
highest = lax.Precision.HIGHEST
eps_norm = 1e-05
temper = 40.0
masked = -1000000000.0
beta_one = 0.5
beta_two = 0.5
adam_eps = 1e-08
decay_rate = 0.01
ema_keep = 0.9
VMEM_CAP = 60 << 20


def nn(a, b):
    return jnp.dot(a, b, preferred_element_type=f32)


def nt(a, b):
    return lax.dot_general(a, b, (((1,), (1,)), ((), ())), preferred_element_type=f32)


def tn(a, b):
    return lax.dot_general(a, b, (((0,), (0,)), ((), ())), preferred_element_type=f32)


def adam_update(weight, first_old, second, ema_old, gradient, step_rate):
    first_new = beta_one * first_old + (1 - beta_one) * gradient
    second_new = beta_two * second + (1 - beta_two) * gradient * gradient
    first_hat = first_new / (1 - beta_one**STEP)
    second_hat = second_new / (1 - beta_two**STEP)
    weight_new = weight - step_rate * (
        first_hat / (jnp.sqrt(second_hat) + adam_eps) + decay_rate * weight
    )
    ema_new = ema_keep * ema_old + (1 - ema_keep) * weight_new
    return (first_new, second_new, weight_new, ema_new)


class Place:
    def __init__(self, depth):
        dp = lax.axis_index("dp")
        t = lax.axis_index("tensor")
        self.depth = depth
        self.z, self.x, self.y, self.c = dp // 2, dp % 2, t // 2, t % 2
        self.me = (self.z, self.x, self.y, self.c)
        self.over_x = (self.z, 1 - self.x, self.y, self.c)
        self.over_y = (self.z, self.x, 1 - self.y, self.c)
        self.over_xy = (self.z, 1 - self.x, 1 - self.y, self.c)
        self.over_c = (self.z, self.x, self.y, 1 - self.c)

    def along_z(self, k):
        return ((self.z + k) % self.depth, self.x, self.y, self.c)


    def others(self):
        return [(z, x, y) for z in range(self.depth) for x in range(2) for y in range(2) if z + x + y > 0]

    def chip(self, z, x, y):
        return ((self.z + z) % self.depth, (self.x + x) % 2, (self.y + y) % 2, self.c)


def device(place):
    z, x, y, c = place
    return (z * 2 + x, y * 2 + c)


def greet(p, everyone=False):
    bar = pltpu.get_barrier_semaphore()
    if everyone:
        to = [p.over_c] + [p.chip(*far) for far in p.others()]
    else:
        to = [p.over_c, p.over_x, p.over_y] + [p.along_z(k) for k in range(1, p.depth)]
    for place in to:
        pl.semaphore_signal(bar, inc=1, device_id=device(place), device_id_type=MESH)
    return len(to)


def enter(count):
    pl.semaphore_wait(pltpu.get_barrier_semaphore(), count)


def remote(src, dst, send, recv, to):
    return pltpu.make_async_remote_copy(
        src_ref=src, dst_ref=dst, send_sem=send, recv_sem=recv, device_id=device(to), device_id_type=MESH
    )


class Gather:
    def __init__(self, p, part, full, sems, straight=False, upright=False):
        self.p, self.part, self.full, self.straight, self.upright = p, part, full, straight, upright
        self.rows = full.shape[1] // (2 * p.depth)
        self.recv, self.pair_recv, self.sz, self.sx, self.sy, self.sk, self.sc = sems

    def spot(self, place, wide=1):
        z, x, y, c = place
        r = self.rows
        step = 32 // self.full.dtype.itemsize
        return self.full.at[y * 2 + c, pl.ds(pl.multiple_of((z * 2 + x) * r, step), wide * r), :]

    def copy(self, place, to, send):
        z, x, y, c = place
        ref = self.spot(place)
        return remote(ref, ref, send.at[self.part], self.recv.at[self.part, (z * 2 + x) * 4 + y * 2 + c], to)

    def pair_copy(self, z, y, c):
        ref = self.spot((z, 0, y, c), 2)
        return remote(ref, ref, self.sc.at[self.part], self.pair_recv.at[self.part, z * 2 + y], self.p.over_c)

    def send(self, place, to, send, when=None):
        def start():
            self.copy(place(), to, send).start()

        if when is not None:
            pl.when(when())(start)
        else:
            start()

    def start(self):
        p, n = self.p, self.p.depth

        def me():
            return p.me

        if self.straight:
            for k in range(1, n):
                self.send(me, p.along_z(k), self.sz)
        else:
            self.send(me, p.along_z(1), self.sz, lambda: p.z + 1 < n)
            self.send(me, p.along_z(-1), self.sz, lambda: p.z > 0)
        self.send(me, p.over_x, self.sx)
        self.send(me, p.over_y, self.sy)

    def sides(self, k):
        p, n = self.p, self.p.depth
        if k == 0:
            return [(0, None)]
        if self.straight:
            return [(1, None)]
        return [(-1, lambda: p.z >= k), (1, lambda: p.z + k < n)]

    def each(self, k, step):
        for sign, when in self.sides(k):
            go = functools.partial(step, sign, sign * k)
            if when is not None:
                pl.when(when())(go)
            else:
                go()

    def arrived(self, place):
        self.copy(place, self.p.over_c, self.sx).wait_recv()

    def at(self, k, x, y):
        return ((self.p.z + k) % self.p.depth, x, y, self.p.c)

    def line(self, k):
        p, n = self.p, self.p.depth

        def step(sign, far):
            place = functools.partial(self.at, far, p.x, p.y)
            self.arrived(place())
            if not self.straight:
                self.send(place, p.along_z(-sign), self.sz, (lambda: p.z + 1 < n) if sign < 0 else (lambda: p.z > 0))
            self.send(place, p.over_x, self.sx)
            self.send(place, p.over_y, self.sy)

        self.each(k, step)

    def cross(self, k):
        p = self.p

        def step(sign, far):
            self.arrived(self.at(far, 1 - p.x, p.y))
            self.arrived(self.at(far, p.x, 1 - p.y))
            z = (p.z + far) % p.depth
            if self.upright and k:
                self.pair_copy(z, p.y, p.c).start()
                return
            odd = (z + self.part) % 2
            x, y = jnp.where(odd == 1, p.x, 1 - p.x), jnp.where(odd == 1, 1 - p.y, p.y)
            to = (p.z, jnp.where(odd == 1, 1 - p.x, p.x), jnp.where(odd == 1, p.y, 1 - p.y), p.c)
            self.copy((z, x, y, p.c), to, self.sk).start()
            self.pair_copy(z, p.y, p.c).start()

        self.each(k, step)

    def corner(self, k):
        p, n = self.p, self.p.depth

        def step(sign, far):
            place = functools.partial(self.at, far, 1 - p.x, 1 - p.y)
            self.arrived(place())
            if self.upright and sign <= 0:
                self.send(place, p.along_z(1), self.sz, lambda: p.z + 1 < n)
            if self.upright and sign >= 0:
                self.send(place, p.along_z(-1), self.sz, lambda: p.z > 0)
            self.pair_copy((p.z + far) % p.depth, 1 - p.y, p.c).start()

        self.each(k, step)

    def other_core(self):
        for z in range(self.p.depth):
            for y in range(2):
                self.pair_copy(z, y, 1 - self.p.c).wait_recv()

    def flow(self):
        n = self.p.depth
        order = [1, n - 1] + list(range(2, n - 1)) if self.straight and n > 2 else list(range(1, n))
        steps = [functools.partial(self.cross, 0)]
        if self.upright:
            steps.append(functools.partial(self.corner, 0))
        for k in order:
            steps += [functools.partial(self.line, k), functools.partial(self.cross, k)]
            if self.upright:
                steps.append(functools.partial(self.corner, k))
        if not self.upright:
            steps += [functools.partial(self.corner, k) for k in range(n)]
        steps.append(self.other_core)
        return steps

    def finish(self):
        n, r = self.p.depth, self.rows

        def left(ref, sem):
            pltpu.make_async_copy(ref, ref, sem.at[self.part]).wait()

        for sem in (self.sx, self.sy):
            left(self.full.at[0, 0 : n * r, :], sem)
        left(self.full.at[0, 0 : r if self.upright else n * r, :], self.sk)
        left(self.full.at[0:2], self.sc)
        if self.straight:
            left(self.full.at[0, 0 : (n - 1) * r, :], self.sz)
        else:
            for z in range(n):
                count = (z + 1 if z + 1 < n else 0) + (n - z if z > 0 else 0)
                if count:
                    ref = self.full.at[0 : 2 if self.upright else 1, 0 : count * r, :]
                    pl.when(self.p.z == z)(functools.partial(left, ref, self.sz))


class Exchange:
    def __init__(self, p, full, sems):
        self.p, self.full = p, full
        self.sent, self.recv, self.core_sent, self.core_recv = sems

    def spot(self, place):
        z, x, y, c = place
        return self.full.at[c, pl.ds(pl.multiple_of(((z * 2 + x) * 2 + y) * 8, 8), 8), :]

    def copy(self, i, far):
        ref = self.spot(self.p.me)
        return remote(ref, ref, self.sent.at[0], self.recv.at[i], self.p.chip(*far))

    def core_copy(self):
        ref = self.full.at[self.p.c]
        return remote(ref, ref, self.core_sent.at[0], self.core_recv.at[0], self.p.over_c)

    def start(self):
        for i, far in enumerate(self.p.others()):
            self.copy(i, far).start()

    def finish(self):
        others = self.p.others()
        for i, far in enumerate(others):
            self.copy(i, far).wait_recv()
        self.core_copy().start()
        self.core_copy().wait()
        left = self.full.at[0, 0 : 8 * len(others), :]
        pltpu.make_async_copy(left, left, self.sent.at[0]).wait()


def exchange_sems(n):
    dma = pltpu.SemaphoreType.DMA
    return [dma((1,)), dma((4 * n,)), dma((1,)), dma((1,))]


def gather_sems(parts, n):
    dma = pltpu.SemaphoreType.DMA
    return [dma((parts, 8 * n)), dma((parts, 2 * n))] + [dma((parts,))] * 5


class Scatter:
    def __init__(self, p, part, rows, grads, out, bufs, temp, load, sems):
        self.p, self.part, self.rows, self.grads, self.out, self.temp, self.load = p, part, rows, grads, out, temp, load
        self.b_core, self.b_corner, self.b_cross, self.b_line = bufs
        self.ss, self.rs, self.sc, self.rc, self.sx, self.rx, self.sl, self.rl = sems

    def slab(self, y):
        return self.grads(y * 2 + self.p.c)

    def span(self, z, x):
        return pl.ds(pl.multiple_of((z * 2 + x) * self.rows, 16), self.rows)

    def which(self, k):
        return self.p.y if k else 1 - self.p.y

    def core_copy(self, k):
        p, q = self.p, self.part
        return remote(self.grads(self.which(k) * 2 + 1 - p.c), self.b_core.at[k], self.ss.at[q], self.rs.at[q, k], p.over_c)

    def core(self, k):
        self.core_copy(k).start()

    def pulled(self, k):
        return pltpu.make_async_copy(self.b_core.at[k], self.temp, self.load)

    def pull(self, k):
        self.core_copy(k).wait_recv()
        self.pulled(k).start()

    def add(self, k):
        r = self.rows
        slab = self.slab(self.which(k))
        self.pulled(k).wait()

        def one(i, _):
            s = pl.ds(pl.multiple_of(i * r, 16), r)
            slab[s, :] = (slab[s, :].astype(f32) + self.temp[s, :].astype(f32)).astype(bf16)
            return 0

        lax.fori_loop(0, 2 * self.p.depth, one, 0)

    def corner_copy(self, z):
        p, q = self.p, self.part
        src = self.slab(1 - p.y).at[self.span(z, 1 - p.x), :]
        return remote(src, self.b_corner.at[z], self.sc.at[q], self.rc.at[q, z], p.over_x if (z + q) % 2 else p.over_y)

    def corner(self):
        for z in range(self.p.depth):
            self.corner_copy(z).start()

    def cross_copy(self, z, way):
        p, q = self.p, self.part
        src = self.slab(1 - p.y).at[self.span(z, p.x), :] if way else self.slab(p.y).at[self.span(z, 1 - p.x), :]
        to = p.over_y if way else p.over_x
        return remote(src, self.b_cross.at[way, z], self.sx.at[q], self.rx.at[q, way, z], to)

    def cross(self, z):
        self.corner_copy(z).wait_recv()
        p = self.p
        slab, s = (self.slab(1 - p.y), self.span(z, p.x)) if (z + self.part) % 2 else (self.slab(p.y), self.span(z, 1 - p.x))
        slab[s, :] = (slab[s, :].astype(f32) + self.b_corner[z].astype(f32)).astype(bf16)
        for way in range(2):
            self.cross_copy(z, way).start()

    def line_copy(self, k):
        p, q = self.p, self.part
        z = (p.z + k) % p.depth
        return remote(self.slab(p.y).at[self.span(z, p.x), :], self.b_line.at[k], self.sl.at[q], self.rl.at[q, k], p.along_z(k))

    def column(self, z):
        p = self.p
        for way in range(2):
            self.cross_copy(z, way).wait_recv()
        return self.slab(p.y)[self.span(z, p.x), :].astype(f32) + self.b_cross[0, z].astype(f32) + self.b_cross[1, z].astype(f32)

    def line(self, k):
        p = self.p
        z = (p.z + k) % p.depth
        self.slab(p.y)[self.span(z, p.x), :] = self.column(z).astype(bf16)
        self.line_copy(k).start()

    def last(self):
        p = self.p
        total = self.column(p.z)
        for k in range(1, p.depth):
            self.line_copy(k).wait_recv()
            total = total + self.b_line[k].astype(f32)
        self.out[...] = total

    def flow(self, early):
        call, n = functools.partial, self.p.depth
        core = [call(self.core, 0), call(self.core, 1)]
        first = [call(self.pull, 0), call(self.add, 0), self.corner]
        steps = core[:1] + first + core[1:] if early else core + first
        steps += [call(self.pull, 1), call(self.add, 1)]
        steps += [call(self.cross, z) for z in range(n)] + [call(self.line, k) for k in range(1, n)]
        return steps + [self.last]

    def finish(self):
        q = self.part
        for ref, sem in ((self.b_core, self.ss), (self.b_corner, self.sc), (self.b_cross, self.sx), (self.b_line.at[1 : self.p.depth], self.sl)):
            pltpu.make_async_copy(ref, ref, sem.at[q]).wait()


def scatter_bufs(n, rows, width):
    return [pltpu.VMEM((n, rows, width), bf16), pltpu.VMEM((2, n, rows, width), bf16), pltpu.VMEM((n, rows, width), bf16)]


def scatter_sems(parts, n):
    dma = pltpu.SemaphoreType.DMA
    return [dma((parts,)), dma((parts, 2)), dma((parts,)), dma((parts, n)), dma((parts,)), dma((parts, 2, n)), dma((parts,)), dma((parts, n))]


def split3(row):
    hi = row.astype(bf16).astype(f32)
    mid = (row - hi).astype(bf16).astype(f32)
    return hi, mid, row - hi - mid


def aug_rows(*rows):
    width = rows[0].shape[1]
    at = lax.broadcasted_iota(jnp.int32, (16, width), 0)
    out = jnp.zeros((16, width), f32)
    for i, row in enumerate(rows):
        out = jnp.where(at == i, row, out)
    return out.astype(bf16)


def norm(r):
    cent = r - jnp.mean(r, axis=1, keepdims=True)
    rstd = lax.rsqrt(jnp.mean(cent * cent, axis=1, keepdims=True) + eps_norm)
    return cent * rstd, rstd


def any_spec(n):
    return [pl.BlockSpec(memory_space=pl.ANY)] * n


def vmem_spec(n):
    return [pl.BlockSpec(memory_space=pltpu.VMEM)] * n


def run(steps):
    for step in steps:
        step()


def at_step(index, hooks):
    for k, steps in hooks.items():
        if steps:
            pl.when(index == k)(functools.partial(run, steps))


NJ = HC // HD
ROWS = 256
CHUNKS = LEN // ROWS
PARTS = 6

PRE = ((0, 0), (3, 0), (2, 0), (1, 0), (0, 1), (3, 1), (2, 1), (3, 2), (1, 1), (4, 0), (3, 3), (3, 4), (1, 2), (1, 3), (0, 2), (0, 3), (3, 5), (2, 2), (3, 6), (4, 1), (2, 3), (1, 4), (1, 5), (1, 6), (3, 7), (0, 4), (0, 5), (3, 8), (3, 9), (0, 6), (5, 0), (1, 7), (1, 8), (1, 9), (2, 4), (0, 7), (0, 8), (0, 9), (2, 5), (4, 2), (2, 6), (3, 10), (1, 10), (4, 3), (3, 11), (1, 11), (0, 10), (0, 11), (3, 12), (1, 12), (5, 1), (0, 12))
HEAD = {2: ((2, 7), (2, 8), (2, 9), (4, 4), (4, 5)), 3: ((4, 6),), 4: ((5, 2), (5, 3), (2, 10), (2, 11)), 6: ((2, 12), (4, 7)), 7: ((4, 8), (4, 9)), 10: ((5, 4), (4, 10), (5, 5), (5, 6)), 11: ((4, 11),)}
MID = ((4, 12), (5, 7))
LATE = {0: ((5, 8),), 2: ((5, 9),), 11: ((5, 10), (5, 11)), 15: ((5, 12),)}
BACK = {0: ((0, 0),), 1: ((0, 1), (1, 0)), 2: ((0, 2), (0, 3), (1, 1)), 3: ((0, 4), (1, 2), (1, 3)), 5: ((0, 5), (1, 4)), 6: ((0, 6), (1, 5), (0, 7)), 7: ((0, 8),), 8: ((0, 9), (0, 10), (1, 6)), 9: ((1, 7),), 10: ((2, 0),), 11: ((2, 1), (2, 2), (1, 8), (1, 9), (0, 11), (1, 10), (2, 3), (2, 4), (0, 12)), 13: ((2, 5),), 14: ((2, 6), (1, 11), (1, 12), (2, 7), (3, 0), (2, 8), (3, 1), (2, 9), (2, 10)), 15: ((1, 13), (3, 2)), 16: ((3, 3), (3, 4), (3, 5)), 17: ((3, 6),), 18: ((4, 0), (3, 7), (2, 11), (3, 8), (4, 1)), 19: ((4, 2), (3, 9), (2, 12), (0, 13), (4, 3), (5, 0), (5, 1), (4, 4), (3, 10), (4, 5), (2, 13)), 20: ((4, 6), (5, 2), (5, 3), (5, 4), (5, 5), (4, 7), (4, 8), (4, 9), (3, 11), (5, 6), (4, 10), (3, 12), (5, 7), (5, 8), (5, 9)), 21: ((5, 10), (2, 14), (3, 13), (4, 11), (0, 14), (4, 12), (4, 13), (1, 14), (5, 11)), 22: ((5, 12), (3, 14), (5, 13), (4, 14), (5, 14))}


def pack(refs, wa, table, w1, w2, p, r, cb):
    qkv, out, up, down, col, row = refs
    dp, t = p.z * 2 + p.x, p.y * 2 + p.c
    at = pl.ds(pl.multiple_of(dp * r, 16), r)
    high = -(-r // 128) * 128
    out_t = jnp.concatenate([out[...], jnp.zeros((HC, high - r), f32)], axis=1)
    out_t = jnp.concatenate([out_t, jnp.zeros((256 - HC, high), f32)], axis=0).T[0:r]
    for j in range(NJ):
        s = slice(j * HD, j * HD + HD)
        wa[j, t, at, :] = jnp.concatenate([qkv[0, :, s], qkv[1, :, s], qkv[2, :, s], out_t[:, s]], axis=1).astype(bf16)
    tile = jnp.concatenate([row[...], jnp.zeros((10, r), f32)], axis=0)
    line = lax.broadcasted_iota(jnp.int32, (16, r), 0)
    for k in range(-(-cb // r)):
        wide = min(r, cb - k * r)
        piece = col[:, k * r : k * r + wide]
        if wide < r:
            piece = jnp.concatenate([piece, jnp.zeros((1, r - wide), f32)], axis=1)
        tile = jnp.where(line == 6 + k, piece, tile)
    tile = jnp.concatenate([tile, jnp.zeros((16, 128 - r), f32)], axis=1)
    own = pl.multiple_of(dp * 32, 32)
    table[t, pl.ds(own, 16), :] = tile.astype(bf16)
    table[t, pl.ds(pl.multiple_of(own + 16, 16), 16), :] = jnp.zeros((16, 128), bf16)
    w1[t, at, :] = up[...].astype(bf16)
    w2[t, at, :] = down[...].astype(bf16)


def loss_pull(pooled, groups, index):
    count = pooled.shape[0]
    inv = lax.rsqrt(jnp.sum(pooled * pooled, axis=1, keepdims=True) + eps_norm)
    unit = pooled * inv
    similar = temper * lax.dot_general(unit, unit, (((1,), (1,)), ((), ())), precision=highest, preferred_element_type=f32)
    rows = lax.broadcasted_iota(jnp.int32, (count, count), 0)
    cols = lax.broadcasted_iota(jnp.int32, (count, count), 1)
    others = jnp.where(rows == cols, masked, similar)
    members = groups.astype(f32)
    eye = jnp.where(rows == cols, 1.0, 0.0).astype(bf16)
    turned = nt(eye, members.astype(bf16))

    def pull(table, axis):
        top = jnp.max(others, axis=axis, keepdims=True)
        e = jnp.exp(others - top)
        return e / jnp.sum(e, axis=axis, keepdims=True) - table / jnp.sum(table, axis=axis, keepdims=True)

    both = temper * (pull(members, 1) + pull(turned, 0))
    grad = lax.dot_general(both, unit, (((1,), (0,)), ((), ())), precision=highest, preferred_element_type=f32)
    own = lax.broadcasted_iota(jnp.int32, (count, 1), 0) == index

    def pick(v):
        return jnp.sum(jnp.where(own, v, 0.0), axis=0, keepdims=True)

    unit, grad = pick(unit), pick(grad)
    return pick(inv) * (grad - unit * jnp.sum(unit * grad, axis=1, keepdims=True))


def forward_kernel(n, cb, comm, *refs):
    dp = 2 * n
    r = D // dp
    given, refs = (6, refs[:2] + refs[2:]) if comm else (4, refs)
    len_ref, x_ref = refs[:2]
    weights_in, refs = refs[2 : 2 + given], refs[2 + given :]
    (rstd_ref, gain_ref, row_ref, hb_ref, pooled,
     out_out, h1_out, xhat1_out, g_out, xhat2_out, ct_out, xt_out, gp_out, q_out, k_out, v_out, wa_out, w1_out, w2_out,
     out_ref, h1_ref, xhat1_ref, g_ref, xhat2_ref, ct_ref, xt,
     wa, w1, w2, table, bcol, col, qt, kt, vt, kn, sb, wo, pool, stage, every,
     local, q_sem, stage_sem, o_sem, *sems) = refs
    length = len_ref[lax.axis_index("tensor")]
    hooks, middle, late = {}, [], {}
    if comm:
        p = Place(n)
        count = greet(p, True)
        pack(weights_in, wa, table, w1, w2, p, r, cb)
        enter(count)
        wholes = [wa.at[j] for j in range(NJ)] + [table, w1, w2]
        parts = [Gather(p, i, full, sems[:7], i == NJ, i != NJ) for i, full in enumerate(wholes)]
        pools = Exchange(p, every, sems[7:])
        flows = [[g.start] + g.flow() for g in parts]

        def steps(pairs):
            return [flows[g][k] for g, k in pairs]

        if n == 4:
            run(steps(PRE[:5]))
            xt[...] = x_ref[...].T
            run(steps(PRE[5:]))
            hooks = {h: steps(pairs) for h, pairs in HEAD.items()}
            middle = steps(MID)
            late = {h: steps(pairs) for h, pairs in LATE.items()}
        else:
            xt[...] = x_ref[...].T
            for group in zip(*flows):
                run(group)
    else:
        loads = [pltpu.make_async_copy(src, dst, local.at[i]) for i, (src, dst) in enumerate(zip(weights_in, (wa, table, w1, w2)))]
        for cp in loads:
            cp.start()
        xt[...] = x_ref[...].T
        for cp in loads:
            cp.wait()
    saved = ((out_ref, out_out), (h1_ref, h1_out), (xhat1_ref, xhat1_out), (g_ref, g_out), (xhat2_ref, xhat2_out), (ct_ref, ct_out),
             (xt, xt_out), (wa, wa_out), (w1, w1_out), (w2, w2_out))

    def save(i):
        return pltpu.make_async_copy(*saved[i], o_sem.at[i])

    save(6).start()

    col_rows = -(-cb // r)
    for i in range(dp):
        rows = slice(i * 32, i * 32 + 16)
        row_ref[:, i * r : i * r + r] = table[0, rows, 0:r].astype(f32)
        for t in range(NT):
            tile = table[t, rows, :].astype(f32)
            for k in range(col_rows):
                wide = min(r, cb - k * r)
                col[t, :, i * cb + k * r : i * cb + k * r + wide] = jnp.broadcast_to(tile[6 + k : 7 + k, 0:wide], (8, wide))
    for t in range(NT):
        bcol[t] = jnp.transpose(col[t, :, 0 : 2 * HC])[:, 0:1]
        hb_ref[t] = col[t, 0:1, 2 * HC : 2 * HC + D]

    ones = jnp.ones((1, LEN), f32)
    where = lax.broadcasted_iota(jnp.int32, (1, LEN), 1)
    key_bias = jnp.where(where < length, 0.0, masked).astype(f32)
    kept = ((qt, q_out), (kt, k_out), (vt, v_out))
    key_rows = aug_rows(key_bias, ones, ones, ones)
    one_row = aug_rows(ones)
    half = LEN // 2

    def project(h):
        j, t = h // NT, h % NT
        qkv = tn(wa[j, t, :, 0 : 3 * HD], xt[...])
        qt[h, 0:HD, :] = ((qkv[0:HD] + bcol[t, pl.ds(pl.multiple_of(j * HD, HD), HD), :]) * HD**-0.5).astype(bf16)
        kt[h, 0:HD, :] = qkv[HD : 2 * HD].astype(bf16)
        vt[h] = (qkv[2 * HD : 3 * HD] + bcol[t, pl.ds(pl.multiple_of(HC + j * HD, HD), HD), :]).astype(bf16)
        qt[h, HD:AUG, :] = one_row
        kt[h, HD:AUG, :] = key_rows
        kn[h % 2] = kt[h].T

    def attend(h, i, s):
        where = slice(i * half, i * half + half)
        top = jnp.max(s, axis=0, keepdims=True)
        e = jnp.exp(s - top)
        total = jnp.sum(e, axis=0, keepdims=True)
        ct_ref[pl.ds(pl.multiple_of(h * HD, HD), HD), where] = (nn(vt[h], e.astype(bf16)) * (1.0 / total)).astype(bf16)
        hi, mid, lo = split3(-(top + jnp.log(total)))
        qt[h, HD:AUG, where] = aug_rows(ones[:, where], hi, mid, lo)

    project(0)
    sb[0] = nn(kn[0], qt[0, :, 0:half])

    def head(h, _):
        after = nn(kn[h % 2], qt[h, :, half:LEN])
        attend(h, 0, sb[0])
        sb[1] = after
        nxt = jnp.minimum(h + 1, H - 1)

        @pl.when(h + 1 < H)
        def _():
            project(nxt)

        after = nn(kn[nxt % 2], qt[nxt, :, 0:half])
        attend(h, 1, sb[1])
        sb[0] = after
        for i, (src, dst) in enumerate(kept):
            pltpu.make_async_copy(src.at[h], dst.at[h], q_sem.at[i, h]).start()
        at_step(h, hooks)
        return 0

    lax.fori_loop(0, H, head, 0)
    save(5).start()

    c_nat = out_ref
    c_nat[...] = ct_ref[...].T
    for j in range(NJ):
        for t in range(NT):
            h = j * NT + t
            wo[:, h * HD : h * HD + HD] = wa[j, t, :, 3 * HD : 4 * HD]
    save(7).start()

    def first(i, _):
        s = pl.ds(pl.multiple_of(i * ROWS, ROWS), ROWS)
        r1 = x_ref[s, :].astype(f32) + (nt(c_nat[s, :], wo[...]) + row_ref[0:1])
        xhat, rstd = norm(r1)
        xhat1_ref[s, :] = xhat
        rstd_ref[s, 0:1] = rstd
        h1_ref[s, :] = (xhat * row_ref[1:2] + row_ref[2:3]).astype(bf16)
        return 0

    lax.fori_loop(0, CHUNKS, first, 0)
    save(1).start()
    save(2).start()
    run(middle)

    def staged(step):
        t, i = step // CHUNKS, step % CHUNKS
        s = pl.ds(pl.multiple_of(i * ROWS, ROWS), ROWS)
        return pltpu.make_async_copy(stage.at[step % 2], gp_out.at[t, s, :], stage_sem.at[step % 2])

    def hidden(step, _):
        t, i = step // CHUNKS, step % CHUNKS
        s = pl.ds(pl.multiple_of(i * ROWS, ROWS), ROWS)
        z = nn(h1_ref[s, :], w1[t]) + hb_ref[t]
        cdf = 0.5 + 0.5 * lax.erf(z * 0.5**0.5)
        g_ref[t, s, :] = (z * cdf).astype(bf16)

        @pl.when(step >= 2)
        def _():
            staged(step - 2).wait()

        stage[step % 2] = cdf + z * (jnp.exp(-0.5 * z * z) * 0.3989422804014327)
        staged(step).start()
        at_step(step, late)
        return 0

    lax.fori_loop(0, NT * CHUNKS, hidden, 0)
    staged(NT * CHUNKS - 2).wait()
    staged(NT * CHUNKS - 1).wait()
    for i in (3, 8, 9):
        save(i).start()
    gain_ref[...] = jnp.zeros_like(gain_ref)
    pool[...] = jnp.zeros_like(pool)

    def second(i, _):
        s = pl.ds(pl.multiple_of(i * ROWS, ROWS), ROWS)
        res = xhat1_ref[s, :] * row_ref[1:2] + row_ref[2:3] + row_ref[3:4]
        for t in range(NT):
            res = res + nt(g_ref[t, s, :], w2[t])
        xhat, rstd = norm(res)
        xhat2_ref[s, :] = xhat
        rstd_ref[s, 1:2] = rstd
        y = xhat * row_ref[4:5] + row_ref[5:6]
        out_ref[s, :] = y.astype(bf16)
        here = i * ROWS + lax.broadcasted_iota(jnp.int32, (ROWS, 1), 0) < length
        pool[0:1] += jnp.sum(jnp.where(here, y, 0.0), axis=0, keepdims=True)
        gain_ref[...] += jnp.sum(jnp.where(here, xhat, 0.0), axis=0, keepdims=True)
        return 0

    lax.fori_loop(0, CHUNKS, second, 0)
    size = jnp.full((1, 1), length).astype(f32)
    mean = pool[0:1] / size
    if comm:
        block = [mean[:, i * 128 : i * 128 + 128] for i in range(D // 128)] + [jnp.zeros((8 - D // 128, 128), f32)]
        every[p.c, pl.ds(pl.multiple_of(((p.z * 2 + p.x) * 2 + p.y) * 8, 8), 8), :] = jnp.concatenate(block, axis=0)
        pools.start()
    save(0).start()
    save(4).start()
    if comm:
        pools.finish()
        for i in range(dp):
            for t in range(NT):
                at = (i * 2 + t // 2) * 8
                for k in range(D // 128):
                    pooled[i * NT + t : i * NT + t + 1, k * 128 : k * 128 + 128] = every[t % 2, at + k : at + k + 1, :]
        for g in parts:
            g.finish()
    else:
        pooled[...] = mean
    for h in range(H):
        for i, (src, dst) in enumerate(kept):
            pltpu.make_async_copy(src.at[h], dst.at[h], q_sem.at[i, h]).wait()
    for i in range(len(saved)):
        save(i).wait()


def forward(length, x, weights, n, cb, comm):
    s = jax.ShapeDtypeStruct
    dp = 2 * n
    r = D // dp
    dma = pltpu.SemaphoreType.DMA
    shapes = [s((LEN, 2), f32), s((1, D), f32), s((16, D), f32), s((NT, 1, D), f32), s((dp * NT if comm else 1, D), f32)]
    big = [s((LEN, D), bf16), s((LEN, D), bf16), s((LEN, D), f32), s((NT, LEN, D), bf16), s((LEN, D), f32), s((D, LEN), bf16), s((D, LEN), bf16)]
    kept = [
        s((NT, LEN, D), f32), s((H, AUG, LEN), bf16), s((H, AUG, LEN), bf16), s((H, HD, LEN), bf16),
        s((NJ, NT, D, 4 * HD), bf16), s((NT, D, D), bf16), s((NT, D, D), bf16),
    ]
    scratch = [pltpu.VMEM(v.shape, v.dtype) for v in big] + [
        pltpu.VMEM((NJ, NT, D, 4 * HD), bf16), pltpu.VMEM((NT, D, D), bf16), pltpu.VMEM((NT, D, D), bf16),
        pltpu.VMEM((NT, dp * 32, 128), bf16), pltpu.VMEM((NT, 2 * HC, 1), f32), pltpu.VMEM((NT, 8, dp * cb), f32),
        pltpu.VMEM((H, AUG, LEN), bf16), pltpu.VMEM((H, AUG, LEN), bf16), pltpu.VMEM((H, HD, LEN), bf16),
        pltpu.VMEM((2, LEN, AUG), bf16), pltpu.VMEM((2, LEN, LEN // 2), f32),
        pltpu.VMEM((D, D), bf16), pltpu.VMEM((8, D), f32), pltpu.VMEM((2, ROWS, D), f32),
        pltpu.VMEM((2, dp * 16, 128), f32),
        dma((PARTS,)), dma((3, H)), dma((2,)), dma((len(big) + 3,)),
    ]
    if comm:
        scratch += gather_sems(PARTS, n) + exchange_sems(n)
        params = pltpu.CompilerParams(collective_id=0, has_side_effects=True, vmem_limit_bytes=VMEM_CAP)
    else:
        params = pltpu.CompilerParams(vmem_limit_bytes=VMEM_CAP)
    return pl.pallas_call(
        functools.partial(forward_kernel, n, cb, comm),
        out_shape=shapes + big + kept,
        in_specs=[pl.BlockSpec(memory_space=pltpu.SMEM)] + vmem_spec(1) + (vmem_spec(6) if comm else any_spec(4)),
        out_specs=vmem_spec(len(shapes)) + any_spec(len(big) + len(kept)),
        scratch_shapes=scratch,
        compiler_params=params,
    )(length, x, *weights)


def backward_kernel(n, cb, comm, *refs):
    dp = 2 * n
    r = D // dp
    (len_ref, pooled_ref, groups_ref, gain_ref, rstd_ref, row_ref,
     xhat2_in, xhat1_in, w1_in, w2_in, wa_in, g_in, gp_in, h1_in, ct_in, xt_in, q_in, k_in, v_in, *refs) = refs
    dx_out, *refs = refs
    outs, refs = refs[: NJ + 3], refs[NJ + 3 :]
    landing, refs = (refs[: NJ + 3], refs[NJ + 3 :]) if comm else ([], refs)
    (wa, w1, w2, t2, dqkv, xt, df, dz, dh, sd, pp, turned, qkv, wcat, grow, ghb, gcol, gbias,
     load, s_load, q_sem, x_sem, *refs) = refs
    length = len_ref[lax.axis_index("tensor")]
    hooks, after, ends = {}, {}, [[]] * 6
    grads = [wa.at[j] for j in range(NJ)]
    h1t = dat = dqkv.at[1]
    ct = dqkv.at[2]
    dft = dct = t2
    folded = [df.at[0:D, :], dz.at[0:D, :], wcat]

    loads = [
        pltpu.make_async_copy(src, dst, load.at[i])
        for i, (src, dst) in enumerate(
            ((xhat2_in, sd.at[1, :, 0:D]), (w2_in, w2), (h1_in, dz), (w1_in, w1), (wa_in, wa), (ct_in, ct), (xt_in, xt))
        )
    ]

    def fetch(step):
        t = part_of(step)
        return [
            pltpu.make_async_copy(src.at[t], dst.at[step % 2, :, 0:D], s_load.at[step % 2, i])
            for i, (src, dst) in enumerate(((g_in, pp), (gp_in, sd)))
        ]

    if comm:
        p = Place(n)

        def part_of(step):
            y = jnp.where(step < 2, 1 - p.y, p.y)
            return y * 2 + jnp.where(step % 2 == 0, 1 - p.c, p.c)
    else:

        def part_of(step):
            return step

    for cp in loads[:2]:
        cp.start()
    for cp in fetch(0):
        cp.start()
    for cp in loads[2:]:
        cp.start()
    if comm:
        temp, *refs = refs
        bufs, sems = refs[:-8], refs[-8:]
        count = greet(p)
        where = [(lambda t: w1.at[t]), (lambda t: w2.at[t])] + [(lambda t, g=g: g.at[t]) for g in grads] + [lambda t: gbias.at[t]]
        parts = []
        for i, source in enumerate(where):
            rows, width = outs[i].shape
            parts.append(
                Scatter(p, i, rows, source, outs[i], [landing[i]] + list(bufs[3 * i : 3 * i + 3]),
                        temp.at[0 : 2 * n * rows, 0:width], x_sem.at[0], sems)
            )
        flows = [part.flow(i < 2) for i, part in enumerate(parts)]

        def steps(pairs):
            return [flows[g][k] for g, k in pairs]

        if n == 4:
            plan = {slot: steps(pairs) for slot, pairs in BACK.items()}
        else:
            plan = {1: steps([(g, k) for g in range(2) for k in range(4)]), 3: steps([(g, k) for g in range(2) for k in range(4, 7)])}
            plan[6] = [step for flow in flows[:2] for step in flow[7:]]
            for j in range(NJ):
                plan[7 + j * NT + NT - 1] = flows[2 + j]
            plan[7 + H] = flows[-1]
        after = {k: plan.get(k, []) for k in range(NT)}
        hooks = {h: plan.get(7 + h, []) for h in range(H)}
        ends = [plan.get(k, []) for k in (5, 6, 7 + H, 8 + H, 9 + H, 10 + H)]

    size = jnp.full((1, 1), length).astype(f32)
    u = loss_pull(pooled_ref[...], groups_ref[...], lax.axis_index("dp") * NT + lax.axis_index("tensor")) / size
    du = u * row_ref[4:5]
    mean_du = jnp.mean(du, axis=1, keepdims=True)
    grow[...] = jnp.zeros_like(grow)
    loads[0].wait()

    def outer(i, _):
        s = pl.ds(pl.multiple_of(i * ROWS, ROWS), ROWS)
        here = i * ROWS + lax.broadcasted_iota(jnp.int32, (ROWS, 1), 0) < length
        hat = sd[1, s, 0:D]
        dot = jnp.mean(hat * du, axis=1, keepdims=True)
        dr = jnp.where(here, rstd_ref[s, 1:2] * (du - mean_du - hat * dot), 0.0)
        dh[s, :] = dr
        low = dr.astype(bf16)
        df[s, :] = low
        grow[3:4] += jnp.sum(low.astype(f32), axis=0, keepdims=True)
        return 0

    lax.fori_loop(0, CHUNKS, outer, 0)
    if comm:
        enter(count)
    grow[4:5] = u * gain_ref[...]
    grow[5:6] = u * size
    dft[...] = df[...].T
    loads[2].wait()
    h1t[...] = dz[...].T
    last_hat = pltpu.make_async_copy(xhat1_in, sd.at[0, :, 0:D], load.at[0])
    loads[1].wait()
    loads[3].wait()

    def hidden(step, _):
        t = part_of(step)
        slot = step % 2
        for cp in fetch(step):
            cp.wait()

        @pl.when(step + 1 < NT)
        def _():
            for cp in fetch(step + 1):
                cp.start()

        hb = jnp.zeros((1, D), f32)
        for i in range(CHUNKS):
            s = pl.ds(i * ROWS, ROWS)
            low = (nn(df[s, :], w2[t]) * sd[slot, s, 0:D]).astype(bf16)
            dz[s, :] = low
            hb = hb + jnp.sum(low.astype(f32), axis=0, keepdims=True)
            dh[s, :] += nt(low, w1[t])
        ghb[t] = hb
        for i in range(D // ROWS):
            s = slice(i * ROWS, (i + 1) * ROWS)
            w1[t, s, :] = nn(h1t[s, :], dz[...]).astype(bf16)
            w2[t, s, :] = nn(dft[s, :], pp[slot, :, 0:D]).astype(bf16)
        pl.when(step == NT - 2)(last_hat.start)
        at_step(step, after)
        return 0

    lax.fori_loop(0, NT, hidden, 0)

    def fetch_head(h, slot):
        return [
            pltpu.make_async_copy(src.at[h], qkv.at[slot, i, 0 : src.shape[1], :], q_sem.at[slot, i])
            for i, src in enumerate((q_in, k_in, v_in))
        ]

    for cp in fetch_head(0, 0):
        cp.start()
    last_hat.wait()

    def inner_norm(i, _):
        s = pl.ds(pl.multiple_of(i * ROWS, ROWS), ROWS)
        d = dh[s, :]
        hat = sd[0, s, 0:D]
        grow[1:2] += jnp.sum(d * hat, axis=0, keepdims=True)
        grow[2:3] += jnp.sum(d, axis=0, keepdims=True)
        dn = d * row_ref[1:2]
        dr = rstd_ref[s, 0:1] * (dn - jnp.mean(dn, axis=1, keepdims=True) - hat * jnp.mean(dn * hat, axis=1, keepdims=True))
        dh[s, :] = dr
        low = dr.astype(bf16)
        grow[0:1] += jnp.sum(low.astype(f32), axis=0, keepdims=True)
        df[s, :] = low
        return 0

    lax.fori_loop(0, CHUNKS, inner_norm, 0)
    dat[...] = df[...].T
    run(ends[0])
    loads[4].wait()
    loads[5].wait()
    for j in range(NJ):
        for t in range(NT):
            h = j * NT + t
            wcat[:, h * HD : h * HD + HD] = wa[j, t, :, 3 * HD : 4 * HD]
    for i in range(D // ROWS):
        s = slice(i * ROWS, (i + 1) * ROWS)
        dct[s, :] = tn(wcat[:, s], dat[...]).astype(bf16)
        gwo = nt(dat[s, :], ct[...]).astype(bf16)
        for j in range(NJ):
            for t in range(NT):
                h = j * NT + t
                wa[j, t, s, 3 * HD : 4 * HD] = gwo[:, h * HD : h * HD + HD]
    loads[6].wait()
    run(ends[1])

    def head(h, _):
        j, t = h // NT, h % NT
        slot = h % 2
        for cp in fetch_head(h, slot):
            cp.wait()

        @pl.when(h + 1 < H)
        def _():
            for cp in fetch_head(h + 1, 1 - slot):
                cp.start()

        own = pl.ds(pl.multiple_of(h * HD, HD), HD)
        prob = jnp.exp(tn(qkv[slot, 0], qkv[slot, 1]))
        sd[0] = prob
        sd[1] = tn(dct[own, :], qkv[slot, 2, 0:HD, :])
        pp[0] = prob.astype(bf16)
        inner = jnp.sum(sd[0] * sd[1], axis=1, keepdims=True)
        pp[1] = (sd[0] * (sd[1] - inner)).astype(bf16)
        turned[...] = pp[1].T
        at = pl.multiple_of(t * 3 * HD, HD)
        dqkv[j, pl.ds(at + HD, HD), :] = nn(qkv[slot, 0, 0:HD, :], pp[1]).astype(bf16)
        dqkv[j, pl.ds(at + 2 * HD, HD), :] = nn(dct[own, :], pp[0]).astype(bf16)
        dqkv[j, pl.ds(at, HD), :] = (nn(qkv[slot, 1, 0:HD, :], turned[...]) * HD**-0.5).astype(bf16)

        @pl.when(t == NT - 1)
        def _():
            for i in range(NJ):

                @pl.when(j == i)
                def _(i=i):
                    for k in range(NT):
                        folded[i][:, k * 3 * HD : (k + 1) * 3 * HD] = wa[i, k, :, 0 : 3 * HD]

            sums = nt(jnp.ones((16, LEN), bf16), dqkv[j])
            for k in range(NT):
                gcol[j, k] = sums[0:8, k * 3 * HD : (k + 1) * 3 * HD]
            for i in range(D // ROWS):
                s = slice(i * ROWS, (i + 1) * ROWS)
                g = nt(xt[s, :], dqkv[j]).astype(bf16)
                for k in range(NT):
                    wa[j, k, s, 0 : 3 * HD] = g[:, k * 3 * HD : (k + 1) * 3 * HD]

        at_step(h, hooks)
        return 0

    lax.fori_loop(0, H, head, 0)

    col_rows = -(-cb // r)
    cols = []
    for t in range(NT):
        pieces = [gcol[j, t, 0:1, 0:HD] for j in range(NJ)] + [gcol[j, t, 0:1, 2 * HD : 3 * HD] for j in range(NJ)]
        cols.append(jnp.concatenate(pieces + [ghb[t]], axis=1))
    at = lax.broadcasted_iota(jnp.int32, (32, 128), 0)
    for i in range(dp):
        rows = jnp.pad(grow[0:8, i * r : i * r + r], ((0, 24), (0, 128 - r)))
        for t in range(NT):
            block = jnp.where(at < 6, rows, 0.0)
            for k in range(col_rows):
                wide = min(r, cb - k * r)
                piece = cols[t][:, i * cb + k * r : i * cb + k * r + wide]
                block = jnp.where(at == 6 + k, jnp.pad(piece, ((0, 0), (0, 128 - wide))), block)
            gbias[t, i * 32 : i * 32 + 32, :] = block.astype(bf16)
    run(ends[2])
    for j in range(NJ):
        for i in range(CHUNKS):
            s = slice(i * ROWS, (i + 1) * ROWS)
            dh[s, :] += lax.dot_general(dqkv[j, :, s], folded[j][...], (((0,), (1,)), ((), ())), preferred_element_type=f32)
        if j == NJ - 1:
            dx = pltpu.make_async_copy(dh, dx_out, load.at[0])
            dx.start()
        run(ends[3 + j])
    if comm:
        for part in parts:
            part.finish()
    else:
        copies = [pltpu.make_async_copy(src, dst, load.at[1 + i]) for i, (src, dst) in enumerate(zip([w1, w2] + grads + [gbias], outs))]
        for cp in copies:
            cp.start()
        for cp in copies:
            cp.wait()
    dx.wait()


def backward(length, pooled, groups, gain, rstd, row, big, n, cb, comm):
    s = jax.ShapeDtypeStruct
    dp = 2 * n
    r = D // dp
    dma = pltpu.SemaphoreType.DMA
    widths = [(r, D), (r, D)] + [(r, 4 * HD)] * NJ + [(32, 128)]
    if comm:
        sums = [s(shape, f32) for shape in widths]
        landing = [s((2, dp * rows, wide), bf16) for rows, wide in widths]
        specs = vmem_spec(len(sums)) + any_spec(len(landing))
    else:
        sums = [s((NT, dp * rows, wide), bf16) for rows, wide in widths]
        landing = []
        specs = any_spec(len(sums))
    turned = pltpu.VMEM((D, LEN), bf16)
    rows_low = pltpu.VMEM((LEN, D), bf16)
    rows_full = pltpu.VMEM((LEN, D), f32)
    scratch = [
        pltpu.VMEM((NJ, NT, D, 4 * HD), bf16), pltpu.VMEM((NT, D, D), bf16), pltpu.VMEM((NT, D, D), bf16),
        turned, pltpu.VMEM((NJ, D, LEN), bf16), turned, rows_low, rows_low, rows_full,
        pltpu.VMEM((2, LEN, LEN), f32), pltpu.VMEM((2, LEN, LEN), bf16), pltpu.VMEM((LEN, LEN), bf16), pltpu.VMEM((2, 3, AUG, LEN), bf16), pltpu.VMEM((D, D), bf16),
        pltpu.VMEM((16, D), f32), pltpu.VMEM((NT, 1, D), f32), pltpu.VMEM((NJ, NT, 8, 3 * HD), f32), pltpu.VMEM((NT, dp * 32, 128), bf16),
        dma((8,)), dma((2, 2)), dma((2, 3)), dma((1,)),
    ]
    if comm:
        scratch += [pltpu.VMEM((D, D), bf16)]
        for rows, wide in widths:
            scratch += scatter_bufs(n, rows, wide)
        scratch += scatter_sems(len(widths), n)
        params = pltpu.CompilerParams(collective_id=1, has_side_effects=True, vmem_limit_bytes=VMEM_CAP)
    else:
        params = pltpu.CompilerParams(vmem_limit_bytes=VMEM_CAP)
    return pl.pallas_call(
        functools.partial(backward_kernel, n, cb, comm),
        out_shape=[s((LEN, D), f32)] + sums + landing,
        in_specs=[pl.BlockSpec(memory_space=pltpu.SMEM)] + vmem_spec(5) + any_spec(len(big)),
        out_specs=any_spec(1) + specs,
        scratch_shapes=scratch,
        compiler_params=params,
    )(length, pooled, groups, gain, rstd, row, *big)


def adam_kernel(cb, *refs):
    ins, outs, refs = refs[:32], refs[32:58], refs[58:]
    held, new, sem_in, sem_out = refs[:32], refs[32:56], refs[56], refs[57]
    inward = [pltpu.make_async_copy(src, dst, sem_in.at[i]) for i, (src, dst) in enumerate(zip(ins, held))]
    outward = [pltpu.make_async_copy(src, dst, sem_out.at[i]) for i, (src, dst) in enumerate(zip((*held[:2], *new), outs))]
    for cp in inward:
        cp.start()
    moved, sums, old = held[:2], held[2:8], held[8:]
    gw1, gw2, ga, gbias = sums[0], sums[1], sums[2:5], sums[5]
    r = gw1.shape[0]

    def wide(k):
        return jnp.concatenate([ga[j][:, k * HD : k * HD + HD] for j in range(NJ)], axis=1)

    def group(i):
        for k in range(4):
            inward[8 + 4 * i + k].wait()

    def update(i, grad, rate, at=()):
        where = at + (Ellipsis,)
        out = adam_update(*[old[4 * i + k][where] for k in range(4)], grad, rate)
        for k, v in enumerate(out):
            new[4 * i + k][where] = v

    def leave(*at):
        for i in at:
            outward[i].start()

    for i in range(2):
        inward[i].wait()
    leave(0, 1)
    for i in range(2, 8):
        inward[i].wait()
    group(0)
    for k in range(3):
        update(0, wide(k), D ** (-0.5), (k,))
    leave(2, 3, 4, 5)
    group(2)
    update(2, gw1[...], D ** (-0.5))
    leave(10, 11, 12, 13)
    group(3)
    update(3, gw2[...], FF ** (-0.5))
    leave(14, 15, 16, 17)
    high = -(-r // 128) * 128
    turned = jnp.concatenate([wide(3), jnp.zeros((r, 256 - HC), f32)], axis=1)
    if high > r:
        turned = jnp.concatenate([turned, jnp.zeros((high - r, 256), f32)], axis=0)
    group(1)
    update(1, turned.T[0:HC, 0:r], D ** (-0.5))
    leave(6, 7, 8, 9)
    group(4)
    rows = gbias[...]
    pieces = [rows[6 + k : 7 + k, 0 : min(r, cb - k * r)] for k in range(-(-cb // r))]
    update(4, jnp.concatenate(pieces, axis=1), 0.1)
    group(5)
    update(5, rows[0:6, 0:r], 0.15)
    leave(*range(18, 26))
    for cp in outward:
        cp.wait()


def adam(moved, sums, olds, cb):
    flat = [v for group in olds for v in group]
    s = jax.ShapeDtypeStruct
    shapes = [s(group[0].shape, f32) for group in olds for _ in range(4)]
    ins = [*moved, *sums, *flat]
    return pl.pallas_call(
        functools.partial(adam_kernel, cb),
        out_shape=[s(v.shape, v.dtype) for v in moved] + shapes,
        in_specs=any_spec(32),
        out_specs=any_spec(26),
        scratch_shapes=[pltpu.VMEM(v.shape, v.dtype) for v in ins + shapes] + [pltpu.SemaphoreType.DMA((32,)), pltpu.SemaphoreType.DMA((26,))],
        compiler_params=pltpu.CompilerParams(vmem_limit_bytes=VMEM_CAP),
    )(*ins)


def gather_plain(own):
    return lax.all_gather(lax.all_gather(own, "dp", axis=0, tiled=True), "tensor", axis=0)


def scatter_plain(full):
    own = lax.psum_scatter(full.astype(f32), "tensor", scatter_dimension=0, tiled=False)
    return lax.psum_scatter(own, "dp", scatter_dimension=0, tiled=True)


def by_head(wide):
    return jnp.moveaxis(wide.reshape(*wide.shape[:-1], NJ, HD), -2, 0)


def packed(qkv_weight, out_weight, up_weight, down_weight, col_bias, row_params, r, cb):
    own_a = jnp.concatenate([by_head(qkv_weight[i]) for i in range(3)] + [by_head(out_weight.T)], axis=-1).astype(bf16)
    col_rows = -(-cb // r)
    col_pad = jnp.pad(col_bias[0], (0, col_rows * r - cb)).reshape(col_rows, r)
    own_b = jnp.pad(jnp.concatenate([row_params, col_pad], axis=0), ((0, 26 - col_rows), (0, 128 - r))).astype(bf16)
    return own_a, own_b, up_weight.astype(bf16), down_weight.T.astype(bf16)


def on_device(
    inputs, lengths, groups, qkv_weight, out_weight, up_weight, down_weight, col_bias, row_params,
    qkv_first, out_first, up_first, down_first, col_first, row_first,
    qkv_second, out_second, up_second, down_second, col_second, row_second,
    qkv_ema, out_ema, up_ema, down_ema, col_ema, row_ema,
):
    dp = lax.axis_size("dp")
    n = dp // 2
    r = D // dp
    cb = col_bias.shape[1]
    comm = r % 32 == 0
    if comm:
        weights = (qkv_weight, out_weight, up_weight, down_weight.T, col_bias, row_params)
    else:
        own_a, *others = packed(qkv_weight, out_weight, up_weight, down_weight, col_bias, row_params, r, cb)
        own_b, own_1, own_2 = [gather_plain(v) for v in others]
        weights = (jnp.stack([gather_plain(own_a[j]) for j in range(NJ)]), own_b, own_1, own_2)
    (rstd, gain, row, hb, pooled, outputs, h1, xhat1, g, xhat2, ct, xt, gp, qt, kt, vt, wa, w1, w2) = forward(
        lengths, inputs, weights, n, cb, comm
    )
    if not comm:
        pooled = lax.all_gather(pooled, ("dp", "tensor"), axis=0, tiled=True)
    big = (xhat2, xhat1, w1, w2, wa, g, gp, h1, ct, xt, qt, kt, vt)
    input_grad, *sums = backward(lengths, pooled, groups, gain, rstd, row, big, n, cb, comm)
    sums = sums[: NJ + 3] if comm else [scatter_plain(v) for v in sums]
    olds = (
        (qkv_weight, qkv_first, qkv_second, qkv_ema),
        (out_weight, out_first, out_second, out_ema),
        (up_weight, up_first, up_second, up_ema),
        (down_weight.T, down_first.T, down_second.T, down_ema.T),
        (col_bias, col_first, col_second, col_ema),
        (row_params, row_first, row_second, row_ema),
    )
    outputs, input_grad, *new = adam((outputs, input_grad), sums, olds, cb)
    new[12:16] = [v.T for v in new[12:16]]
    return (outputs, input_grad, *new)


def solution(mesh):
    tokens = P(("dp", "tensor"), None)
    placed = (P(None, "dp", "tensor"), P("tensor", "dp"), P("dp", "tensor"), P("tensor", "dp"), P("tensor", "dp"), P(None, "dp"))
    new = tuple(spec for spec in placed for _ in range(4))
    return jax.shard_map(
        on_device,
        mesh=mesh,
        in_specs=(tokens, P("dp"), P()) + placed * 4,
        out_specs=(tokens, tokens) + new,
        check_vma=False,
    )
```

```python
import functools

import jax
import jax.numpy as jnp
from jax import lax
from jax.experimental import pallas as pl
from jax.experimental.pallas import tpu as pltpu
from jax.sharding import PartitionSpec as P

D = 768
H = 12
HD = 64
FF = 3072
LEN = 1024
STEP = 5
NT = 4
HC = D // NT
AUG = 80

MESH = pl.DeviceIdType.MESH
f32 = jnp.float32
bf16 = jnp.bfloat16
highest = lax.Precision.HIGHEST
eps_norm = 1e-05
temper = 40.0
masked = -1000000000.0
beta_one = 0.5
beta_two = 0.5
adam_eps = 1e-08
decay_rate = 0.01
ema_keep = 0.9
VMEM_CAP = 60 << 20


def nn(a, b):
    return jnp.dot(a, b, preferred_element_type=f32)


def nt(a, b):
    return lax.dot_general(a, b, (((1,), (1,)), ((), ())), preferred_element_type=f32)


def tn(a, b):
    return lax.dot_general(a, b, (((0,), (0,)), ((), ())), preferred_element_type=f32)


def adam_update(weight, first_old, second, ema_old, gradient, step_rate):
    first_new = beta_one * first_old + (1 - beta_one) * gradient
    second_new = beta_two * second + (1 - beta_two) * gradient * gradient
    first_hat = first_new / (1 - beta_one**STEP)
    second_hat = second_new / (1 - beta_two**STEP)
    weight_new = weight - step_rate * (
        first_hat / (jnp.sqrt(second_hat) + adam_eps) + decay_rate * weight
    )
    ema_new = ema_keep * ema_old + (1 - ema_keep) * weight_new
    return (first_new, second_new, weight_new, ema_new)


class Place:
    def __init__(self, depth):
        dp = lax.axis_index("dp")
        t = lax.axis_index("tensor")
        self.depth = depth
        self.z, self.x, self.y, self.c = dp // 2, dp % 2, t // 2, t % 2
        self.me = (self.z, self.x, self.y, self.c)
        self.over_x = (self.z, 1 - self.x, self.y, self.c)
        self.over_y = (self.z, self.x, 1 - self.y, self.c)
        self.over_xy = (self.z, 1 - self.x, 1 - self.y, self.c)
        self.over_c = (self.z, self.x, self.y, 1 - self.c)

    def along_z(self, k):
        return ((self.z + k) % self.depth, self.x, self.y, self.c)


    def others(self):
        return [(z, x, y) for z in range(self.depth) for x in range(2) for y in range(2) if z + x + y > 0]

    def chip(self, z, x, y):
        return ((self.z + z) % self.depth, (self.x + x) % 2, (self.y + y) % 2, self.c)


def device(place):
    z, x, y, c = place
    return (z * 2 + x, y * 2 + c)


def greet(p, everyone=False):
    bar = pltpu.get_barrier_semaphore()
    if everyone:
        to = [p.over_c] + [p.chip(*far) for far in p.others()]
    else:
        to = [p.over_c, p.over_x, p.over_y] + [p.along_z(k) for k in range(1, p.depth)]
    for place in to:
        pl.semaphore_signal(bar, inc=1, device_id=device(place), device_id_type=MESH)
    return len(to)


def enter(count):
    pl.semaphore_wait(pltpu.get_barrier_semaphore(), count)


def remote(src, dst, send, recv, to):
    return pltpu.make_async_remote_copy(
        src_ref=src, dst_ref=dst, send_sem=send, recv_sem=recv, device_id=device(to), device_id_type=MESH
    )


class Gather:
    def __init__(self, p, part, full, sems, straight=False, upright=False):
        self.p, self.part, self.full, self.straight, self.upright = p, part, full, straight, upright
        self.rows = full.shape[1] // (2 * p.depth)
        self.recv, self.pair_recv, self.sz, self.sx, self.sy, self.sk, self.sc = sems

    def spot(self, place, wide=1):
        z, x, y, c = place
        r = self.rows
        step = 32 // self.full.dtype.itemsize
        return self.full.at[y * 2 + c, pl.ds(pl.multiple_of((z * 2 + x) * r, step), wide * r), :]

    def copy(self, place, to, send):
        z, x, y, c = place
        ref = self.spot(place)
        return remote(ref, ref, send.at[self.part], self.recv.at[self.part, (z * 2 + x) * 4 + y * 2 + c], to)

    def pair_copy(self, z, y, c):
        ref = self.spot((z, 0, y, c), 2)
        return remote(ref, ref, self.sc.at[self.part], self.pair_recv.at[self.part, z * 2 + y], self.p.over_c)

    def send(self, place, to, send, when=None):
        def start():
            self.copy(place(), to, send).start()

        if when is not None:
            pl.when(when())(start)
        else:
            start()

    def start(self):
        p, n = self.p, self.p.depth

        def me():
            return p.me

        if self.straight:
            for k in range(1, n):
                self.send(me, p.along_z(k), self.sz)
        else:
            self.send(me, p.along_z(1), self.sz, lambda: p.z + 1 < n)
            self.send(me, p.along_z(-1), self.sz, lambda: p.z > 0)
        self.send(me, p.over_x, self.sx)
        self.send(me, p.over_y, self.sy)

    def sides(self, k):
        p, n = self.p, self.p.depth
        if k == 0:
            return [(0, None)]
        if self.straight:
            return [(1, None)]
        return [(-1, lambda: p.z >= k), (1, lambda: p.z + k < n)]

    def each(self, k, step):
        for sign, when in self.sides(k):
            go = functools.partial(step, sign, sign * k)
            if when is not None:
                pl.when(when())(go)
            else:
                go()

    def arrived(self, place):
        self.copy(place, self.p.over_c, self.sx).wait_recv()

    def at(self, k, x, y):
        return ((self.p.z + k) % self.p.depth, x, y, self.p.c)

    def line(self, k):
        p, n = self.p, self.p.depth

        def step(sign, far):
            place = functools.partial(self.at, far, p.x, p.y)
            self.arrived(place())
            if not self.straight:
                self.send(place, p.along_z(-sign), self.sz, (lambda: p.z + 1 < n) if sign < 0 else (lambda: p.z > 0))
            self.send(place, p.over_x, self.sx)
            self.send(place, p.over_y, self.sy)

        self.each(k, step)

    def cross(self, k):
        p = self.p

        def step(sign, far):
            self.arrived(self.at(far, 1 - p.x, p.y))
            self.arrived(self.at(far, p.x, 1 - p.y))
            z = (p.z + far) % p.depth
            if self.upright and k:
                self.pair_copy(z, p.y, p.c).start()
                return
            odd = (z + self.part) % 2
            x, y = jnp.where(odd == 1, p.x, 1 - p.x), jnp.where(odd == 1, 1 - p.y, p.y)
            to = (p.z, jnp.where(odd == 1, 1 - p.x, p.x), jnp.where(odd == 1, p.y, 1 - p.y), p.c)
            self.copy((z, x, y, p.c), to, self.sk).start()
            self.pair_copy(z, p.y, p.c).start()

        self.each(k, step)

    def corner(self, k):
        p, n = self.p, self.p.depth

        def step(sign, far):
            place = functools.partial(self.at, far, 1 - p.x, 1 - p.y)
            self.arrived(place())
            if self.upright and sign <= 0:
                self.send(place, p.along_z(1), self.sz, lambda: p.z + 1 < n)
            if self.upright and sign >= 0:
                self.send(place, p.along_z(-1), self.sz, lambda: p.z > 0)
            self.pair_copy((p.z + far) % p.depth, 1 - p.y, p.c).start()

        self.each(k, step)

    def other_core(self):
        for z in range(self.p.depth):
            for y in range(2):
                self.pair_copy(z, y, 1 - self.p.c).wait_recv()

    def flow(self):
        n = self.p.depth
        order = [1, n - 1] + list(range(2, n - 1)) if self.straight and n > 2 else list(range(1, n))
        steps = [functools.partial(self.cross, 0)]
        if self.upright:
            steps.append(functools.partial(self.corner, 0))
        for k in order:
            steps += [functools.partial(self.line, k), functools.partial(self.cross, k)]
            if self.upright:
                steps.append(functools.partial(self.corner, k))
        if not self.upright:
            steps += [functools.partial(self.corner, k) for k in range(n)]
        steps.append(self.other_core)
        return steps

    def finish(self):
        n, r = self.p.depth, self.rows

        def left(ref, sem):
            pltpu.make_async_copy(ref, ref, sem.at[self.part]).wait()

        for sem in (self.sx, self.sy):
            left(self.full.at[0, 0 : n * r, :], sem)
        left(self.full.at[0, 0 : r if self.upright else n * r, :], self.sk)
        left(self.full.at[0:2], self.sc)
        if self.straight:
            left(self.full.at[0, 0 : (n - 1) * r, :], self.sz)
        else:
            for z in range(n):
                count = (z + 1 if z + 1 < n else 0) + (n - z if z > 0 else 0)
                if count:
                    ref = self.full.at[0 : 2 if self.upright else 1, 0 : count * r, :]
                    pl.when(self.p.z == z)(functools.partial(left, ref, self.sz))


class Exchange:
    def __init__(self, p, full, sems):
        self.p, self.full = p, full
        self.sent, self.recv, self.core_sent, self.core_recv = sems

    def spot(self, place):
        z, x, y, c = place
        return self.full.at[c, pl.ds(pl.multiple_of(((z * 2 + x) * 2 + y) * 8, 8), 8), :]

    def copy(self, i, far):
        ref = self.spot(self.p.me)
        return remote(ref, ref, self.sent.at[0], self.recv.at[i], self.p.chip(*far))

    def core_copy(self):
        ref = self.full.at[self.p.c]
        return remote(ref, ref, self.core_sent.at[0], self.core_recv.at[0], self.p.over_c)

    def start(self):
        for i, far in enumerate(self.p.others()):
            self.copy(i, far).start()

    def finish(self):
        others = self.p.others()
        for i, far in enumerate(others):
            self.copy(i, far).wait_recv()
        self.core_copy().start()
        self.core_copy().wait()
        left = self.full.at[0, 0 : 8 * len(others), :]
        pltpu.make_async_copy(left, left, self.sent.at[0]).wait()


def exchange_sems(n):
    dma = pltpu.SemaphoreType.DMA
    return [dma((1,)), dma((4 * n,)), dma((1,)), dma((1,))]


def gather_sems(parts, n):
    dma = pltpu.SemaphoreType.DMA
    return [dma((parts, 8 * n)), dma((parts, 2 * n))] + [dma((parts,))] * 5


class Scatter:
    def __init__(self, p, part, rows, grads, out, bufs, temp, load, sems):
        self.p, self.part, self.rows, self.grads, self.out, self.temp, self.load = p, part, rows, grads, out, temp, load
        self.b_core, self.b_corner, self.b_cross, self.b_line = bufs
        self.ss, self.rs, self.sc, self.rc, self.sx, self.rx, self.sl, self.rl = sems

    def slab(self, y):
        return self.grads(y * 2 + self.p.c)

    def span(self, z, x):
        return pl.ds(pl.multiple_of((z * 2 + x) * self.rows, 16), self.rows)

    def which(self, k):
        return self.p.y if k else 1 - self.p.y

    def core_copy(self, k):
        p, q = self.p, self.part
        return remote(self.grads(self.which(k) * 2 + 1 - p.c), self.b_core.at[k], self.ss.at[q], self.rs.at[q, k], p.over_c)

    def core(self, k):
        self.core_copy(k).start()

    def pulled(self, k):
        return pltpu.make_async_copy(self.b_core.at[k], self.temp, self.load)

    def pull(self, k):
        self.core_copy(k).wait_recv()
        self.pulled(k).start()

    def add(self, k):
        r = self.rows
        slab = self.slab(self.which(k))
        self.pulled(k).wait()

        def one(i, _):
            s = pl.ds(pl.multiple_of(i * r, 16), r)
            slab[s, :] = (slab[s, :].astype(f32) + self.temp[s, :].astype(f32)).astype(bf16)
            return 0

        lax.fori_loop(0, 2 * self.p.depth, one, 0)

    def corner_copy(self, z):
        p, q = self.p, self.part
        src = self.slab(1 - p.y).at[self.span(z, 1 - p.x), :]
        return remote(src, self.b_corner.at[z], self.sc.at[q], self.rc.at[q, z], p.over_x if (z + q) % 2 else p.over_y)

    def corner(self):
        for z in range(self.p.depth):
            self.corner_copy(z).start()

    def cross_copy(self, z, way):
        p, q = self.p, self.part
        src = self.slab(1 - p.y).at[self.span(z, p.x), :] if way else self.slab(p.y).at[self.span(z, 1 - p.x), :]
        to = p.over_y if way else p.over_x
        return remote(src, self.b_cross.at[way, z], self.sx.at[q], self.rx.at[q, way, z], to)

    def cross(self, z):
        self.corner_copy(z).wait_recv()
        p = self.p
        slab, s = (self.slab(1 - p.y), self.span(z, p.x)) if (z + self.part) % 2 else (self.slab(p.y), self.span(z, 1 - p.x))
        slab[s, :] = (slab[s, :].astype(f32) + self.b_corner[z].astype(f32)).astype(bf16)
        for way in range(2):
            self.cross_copy(z, way).start()

    def line_copy(self, k):
        p, q = self.p, self.part
        z = (p.z + k) % p.depth
        return remote(self.slab(p.y).at[self.span(z, p.x), :], self.b_line.at[k], self.sl.at[q], self.rl.at[q, k], p.along_z(k))

    def column(self, z):
        p = self.p
        for way in range(2):
            self.cross_copy(z, way).wait_recv()
        return self.slab(p.y)[self.span(z, p.x), :].astype(f32) + self.b_cross[0, z].astype(f32) + self.b_cross[1, z].astype(f32)

    def line(self, k):
        p = self.p
        z = (p.z + k) % p.depth
        self.slab(p.y)[self.span(z, p.x), :] = self.column(z).astype(bf16)
        self.line_copy(k).start()

    def last(self):
        p = self.p
        total = self.column(p.z)
        for k in range(1, p.depth):
            self.line_copy(k).wait_recv()
            total = total + self.b_line[k].astype(f32)
        self.out[...] = total

    def flow(self, early):
        call, n = functools.partial, self.p.depth
        core = [call(self.core, 0), call(self.core, 1)]
        first = [call(self.pull, 0), call(self.add, 0), self.corner]
        steps = core[:1] + first + core[1:] if early else core + first
        steps += [call(self.pull, 1), call(self.add, 1)]
        steps += [call(self.cross, z) for z in range(n)] + [call(self.line, k) for k in range(1, n)]
        return steps + [self.last]

    def finish(self):
        q = self.part
        for ref, sem in ((self.b_core, self.ss), (self.b_corner, self.sc), (self.b_cross, self.sx), (self.b_line.at[1 : self.p.depth], self.sl)):
            pltpu.make_async_copy(ref, ref, sem.at[q]).wait()


def scatter_bufs(n, rows, width):
    return [pltpu.VMEM((n, rows, width), bf16), pltpu.VMEM((2, n, rows, width), bf16), pltpu.VMEM((n, rows, width), bf16)]


def scatter_sems(parts, n):
    dma = pltpu.SemaphoreType.DMA
    return [dma((parts,)), dma((parts, 2)), dma((parts,)), dma((parts, n)), dma((parts,)), dma((parts, 2, n)), dma((parts,)), dma((parts, n))]


def split3(row):
    hi = row.astype(bf16).astype(f32)
    mid = (row - hi).astype(bf16).astype(f32)
    return hi, mid, row - hi - mid


def aug_rows(*rows):
    width = rows[0].shape[1]
    at = lax.broadcasted_iota(jnp.int32, (16, width), 0)
    out = jnp.zeros((16, width), f32)
    for i, row in enumerate(rows):
        out = jnp.where(at == i, row, out)
    return out.astype(bf16)


def norm(r):
    cent = r - jnp.mean(r, axis=1, keepdims=True)
    rstd = lax.rsqrt(jnp.mean(cent * cent, axis=1, keepdims=True) + eps_norm)
    return cent * rstd, rstd


def any_spec(n):
    return [pl.BlockSpec(memory_space=pl.ANY)] * n


def vmem_spec(n):
    return [pl.BlockSpec(memory_space=pltpu.VMEM)] * n


def run(steps):
    for step in steps:
        step()


def at_step(index, hooks):
    for k, steps in hooks.items():
        if steps:
            pl.when(index == k)(functools.partial(run, steps))


NJ = HC // HD
ROWS = 256
CHUNKS = LEN // ROWS
PARTS = 6

PRE = ((0, 0), (2, 0), (3, 0), (1, 0), (0, 1), (4, 0), (1, 1), (3, 1), (3, 2), (2, 1), (0, 2), (0, 3), (3, 3), (3, 4), (1, 2), (1, 3), (2, 2), (2, 3), (0, 4), (0, 5), (3, 5), (0, 6), (3, 6), (1, 4), (1, 5), (1, 6), (4, 1), (0, 7), (3, 7), (3, 8), (0, 8), (2, 4), (1, 7), (2, 5), (3, 9), (2, 6), (3, 10), (1, 8), (0, 9), (1, 9), (5, 0), (3, 11), (0, 10), (0, 11), (1, 10), (2, 7), (4, 2), (2, 8), (2, 9), (0, 12), (4, 3), (1, 11), (3, 12))
HEAD = {0: ((1, 12),), 1: ((2, 10), (5, 1)), 3: ((2, 11), (4, 4), (4, 5)), 4: ((2, 12), (4, 6)), 6: ((5, 2), (5, 3)), 7: ((4, 7), (4, 8)), 8: ((4, 9),), 10: ((5, 4), (5, 5)), 11: ((5, 6), (4, 10))}
MID = ((4, 11), (5, 7), (5, 8), (4, 12))
LATE = {2: ((5, 9),), 11: ((5, 10), (5, 11)), 15: ((5, 12),)}
BACK = {0: ((0, 0),), 1: ((0, 1), (1, 0)), 2: ((0, 2), (0, 3), (1, 1)), 3: ((0, 4), (1, 2), (1, 3)), 5: ((0, 5), (1, 4)), 6: ((0, 6), (1, 5), (0, 7)), 7: ((0, 8),), 8: ((0, 9), (0, 10), (1, 6)), 9: ((1, 7),), 10: ((2, 0),), 11: ((2, 1), (2, 2), (1, 8), (1, 9), (0, 11), (1, 10), (2, 3), (2, 4), (0, 12)), 13: ((2, 5),), 14: ((2, 6), (1, 11), (1, 12), (2, 7), (3, 0), (2, 8), (3, 1), (2, 9), (2, 10)), 15: ((1, 13), (3, 2)), 16: ((3, 3), (3, 4), (3, 5)), 17: ((3, 6),), 18: ((4, 0), (3, 7), (2, 11), (3, 8), (4, 1)), 19: ((4, 2), (3, 9), (2, 12), (0, 13), (4, 3), (5, 0), (5, 1), (4, 4), (3, 10), (4, 5), (2, 13)), 20: ((4, 6), (5, 2), (5, 3), (5, 4), (5, 5), (4, 7), (4, 8), (4, 9), (3, 11), (5, 6), (4, 10), (3, 12), (5, 7), (5, 8), (5, 9)), 21: ((5, 10), (2, 14), (3, 13), (4, 11), (0, 14), (4, 12), (4, 13), (1, 14), (5, 11)), 22: ((5, 12), (3, 14), (5, 13), (4, 14), (5, 14))}


def pack(refs, wa, table, w1, w2, p, r, cb):
    qkv, out, up, down, col, row = refs
    dp, t = p.z * 2 + p.x, p.y * 2 + p.c
    at = pl.ds(pl.multiple_of(dp * r, 16), r)
    high = -(-r // 128) * 128
    out_t = jnp.concatenate([out[...], jnp.zeros((HC, high - r), f32)], axis=1)
    out_t = jnp.concatenate([out_t, jnp.zeros((256 - HC, high), f32)], axis=0).T[0:r]
    for j in range(NJ):
        s = slice(j * HD, j * HD + HD)
        wa[j, t, at, :] = jnp.concatenate([qkv[0, :, s], qkv[1, :, s], qkv[2, :, s], out_t[:, s]], axis=1).astype(bf16)
    tile = jnp.concatenate([row[...], jnp.zeros((10, r), f32)], axis=0)
    line = lax.broadcasted_iota(jnp.int32, (16, r), 0)
    for k in range(-(-cb // r)):
        wide = min(r, cb - k * r)
        piece = col[:, k * r : k * r + wide]
        if wide < r:
            piece = jnp.concatenate([piece, jnp.zeros((1, r - wide), f32)], axis=1)
        tile = jnp.where(line == 6 + k, piece, tile)
    tile = jnp.concatenate([tile, jnp.zeros((16, 128 - r), f32)], axis=1)
    own = pl.multiple_of(dp * 32, 32)
    table[t, pl.ds(own, 16), :] = tile.astype(bf16)
    table[t, pl.ds(pl.multiple_of(own + 16, 16), 16), :] = jnp.zeros((16, 128), bf16)
    w1[t, at, :] = up[...].astype(bf16)
    w2[t, at, :] = down[...].astype(bf16)


def loss_pull(pooled, groups, index):
    count = pooled.shape[0]
    inv = lax.rsqrt(jnp.sum(pooled * pooled, axis=1, keepdims=True) + eps_norm)
    unit = pooled * inv
    similar = temper * lax.dot_general(unit, unit, (((1,), (1,)), ((), ())), precision=highest, preferred_element_type=f32)
    rows = lax.broadcasted_iota(jnp.int32, (count, count), 0)
    cols = lax.broadcasted_iota(jnp.int32, (count, count), 1)
    others = jnp.where(rows == cols, masked, similar)
    members = groups.astype(f32)
    eye = jnp.where(rows == cols, 1.0, 0.0).astype(bf16)
    turned = nt(eye, members.astype(bf16))

    def pull(table, axis):
        top = jnp.max(others, axis=axis, keepdims=True)
        e = jnp.exp(others - top)
        return e / jnp.sum(e, axis=axis, keepdims=True) - table / jnp.sum(table, axis=axis, keepdims=True)

    both = temper * (pull(members, 1) + pull(turned, 0))
    grad = lax.dot_general(both, unit, (((1,), (0,)), ((), ())), precision=highest, preferred_element_type=f32)
    own = lax.broadcasted_iota(jnp.int32, (count, 1), 0) == index

    def pick(v):
        return jnp.sum(jnp.where(own, v, 0.0), axis=0, keepdims=True)

    unit, grad = pick(unit), pick(grad)
    return pick(inv) * (grad - unit * jnp.sum(unit * grad, axis=1, keepdims=True))


def forward_kernel(n, cb, comm, *refs):
    dp = 2 * n
    r = D // dp
    given, refs = (6, refs[:2] + refs[2:]) if comm else (4, refs)
    len_ref, x_ref = refs[:2]
    weights_in, refs = refs[2 : 2 + given], refs[2 + given :]
    (rstd_ref, gain_ref, row_ref, hb_ref, pooled,
     out_out, h1_out, xhat1_out, g_out, xhat2_out, ct_out, xt_out, gp_out, q_out, k_out, v_out, wa_out, w1_out, w2_out,
     out_ref, h1_ref, xhat1_ref, g_ref, xhat2_ref, ct_ref, xt,
     wa, w1, w2, table, bcol, col, qt, kt, vt, kn, sb, wo, pool, stage, every,
     local, q_sem, stage_sem, o_sem, *sems) = refs
    length = len_ref[lax.axis_index("tensor")]
    hooks, middle, late = {}, [], {}
    if comm:
        p = Place(n)
        count = greet(p, True)
        pack(weights_in, wa, table, w1, w2, p, r, cb)
        enter(count)
        wholes = [wa.at[j] for j in range(NJ)] + [table, w1, w2]
        parts = [Gather(p, i, full, sems[:7], i == NJ, i != NJ) for i, full in enumerate(wholes)]
        pools = Exchange(p, every, sems[7:])
        flows = [[g.start] + g.flow() for g in parts]

        def steps(pairs):
            return [flows[g][k] for g, k in pairs]

        if n == 4:
            run(steps(PRE[:5]))
            xt[...] = x_ref[...].T
            run(steps(PRE[5:]))
            hooks = {h: steps(pairs) for h, pairs in HEAD.items()}
            middle = steps(MID)
            late = {h: steps(pairs) for h, pairs in LATE.items()}
        else:
            xt[...] = x_ref[...].T
            for group in zip(*flows):
                run(group)
    else:
        loads = [pltpu.make_async_copy(src, dst, local.at[i]) for i, (src, dst) in enumerate(zip(weights_in, (wa, table, w1, w2)))]
        for cp in loads:
            cp.start()
        xt[...] = x_ref[...].T
        for cp in loads:
            cp.wait()
    saved = ((out_ref, out_out), (h1_ref, h1_out), (xhat1_ref, xhat1_out), (g_ref, g_out), (xhat2_ref, xhat2_out), (ct_ref, ct_out),
             (xt, xt_out), (wa, wa_out), (w1, w1_out), (w2, w2_out))

    def save(i):
        return pltpu.make_async_copy(*saved[i], o_sem.at[i])

    save(6).start()

    col_rows = -(-cb // r)
    for i in range(dp):
        rows = slice(i * 32, i * 32 + 16)
        row_ref[:, i * r : i * r + r] = table[0, rows, 0:r].astype(f32)
        for t in range(NT):
            tile = table[t, rows, :].astype(f32)
            for k in range(col_rows):
                wide = min(r, cb - k * r)
                col[t, :, i * cb + k * r : i * cb + k * r + wide] = jnp.broadcast_to(tile[6 + k : 7 + k, 0:wide], (8, wide))
    for t in range(NT):
        bcol[t] = jnp.transpose(col[t, :, 0 : 2 * HC])[:, 0:1]
        hb_ref[t] = col[t, 0:1, 2 * HC : 2 * HC + D]

    ones = jnp.ones((1, LEN), f32)
    where = lax.broadcasted_iota(jnp.int32, (1, LEN), 1)
    key_bias = jnp.where(where < length, 0.0, masked).astype(f32)
    kept = ((qt, q_out), (kt, k_out), (vt, v_out))
    key_rows = aug_rows(key_bias, ones, ones, ones)
    one_row = aug_rows(ones)
    half = LEN // 2

    def project(h):
        j, t = h // NT, h % NT
        qkv = tn(wa[j, t, :, 0 : 3 * HD], xt[...])
        qt[h, 0:HD, :] = ((qkv[0:HD] + bcol[t, pl.ds(pl.multiple_of(j * HD, HD), HD), :]) * HD**-0.5).astype(bf16)
        kt[h, 0:HD, :] = qkv[HD : 2 * HD].astype(bf16)
        vt[h] = (qkv[2 * HD : 3 * HD] + bcol[t, pl.ds(pl.multiple_of(HC + j * HD, HD), HD), :]).astype(bf16)
        qt[h, HD:AUG, :] = one_row
        kt[h, HD:AUG, :] = key_rows
        kn[h % 2] = kt[h].T

    def attend(h, i, s):
        where = slice(i * half, i * half + half)
        top = jnp.max(s, axis=0, keepdims=True)
        e = jnp.exp(s - top)
        total = jnp.sum(e, axis=0, keepdims=True)
        ct_ref[pl.ds(pl.multiple_of(h * HD, HD), HD), where] = (nn(vt[h], e.astype(bf16)) * (1.0 / total)).astype(bf16)
        hi, mid, lo = split3(-(top + jnp.log(total)))
        qt[h, HD:AUG, where] = aug_rows(ones[:, where], hi, mid, lo)

    project(0)
    sb[0] = nn(kn[0], qt[0, :, 0:half])

    def head(h, _):
        after = nn(kn[h % 2], qt[h, :, half:LEN])
        attend(h, 0, sb[0])
        sb[1] = after
        nxt = jnp.minimum(h + 1, H - 1)

        @pl.when(h + 1 < H)
        def _():
            project(nxt)

        after = nn(kn[nxt % 2], qt[nxt, :, 0:half])
        attend(h, 1, sb[1])
        sb[0] = after
        for i, (src, dst) in enumerate(kept):
            pltpu.make_async_copy(src.at[h], dst.at[h], q_sem.at[i, h]).start()
        at_step(h, hooks)
        return 0

    lax.fori_loop(0, H, head, 0)
    save(5).start()

    c_nat = out_ref
    c_nat[...] = ct_ref[...].T
    for j in range(NJ):
        for t in range(NT):
            h = j * NT + t
            wo[:, h * HD : h * HD + HD] = wa[j, t, :, 3 * HD : 4 * HD]
    save(7).start()

    def first(i, _):
        s = pl.ds(pl.multiple_of(i * ROWS, ROWS), ROWS)
        r1 = x_ref[s, :].astype(f32) + (nt(c_nat[s, :], wo[...]) + row_ref[0:1])
        xhat, rstd = norm(r1)
        xhat1_ref[s, :] = xhat
        rstd_ref[s, 0:1] = rstd
        h1_ref[s, :] = (xhat * row_ref[1:2] + row_ref[2:3]).astype(bf16)
        return 0

    lax.fori_loop(0, CHUNKS, first, 0)
    save(1).start()
    save(2).start()
    run(middle)

    def staged(step):
        t, i = step // CHUNKS, step % CHUNKS
        s = pl.ds(pl.multiple_of(i * ROWS, ROWS), ROWS)
        return pltpu.make_async_copy(stage.at[step % 2], gp_out.at[t, s, :], stage_sem.at[step % 2])

    def hidden(step, _):
        t, i = step // CHUNKS, step % CHUNKS
        s = pl.ds(pl.multiple_of(i * ROWS, ROWS), ROWS)
        z = nn(h1_ref[s, :], w1[t]) + hb_ref[t]
        cdf = 0.5 + 0.5 * lax.erf(z * 0.5**0.5)
        g_ref[t, s, :] = (z * cdf).astype(bf16)

        @pl.when(step >= 2)
        def _():
            staged(step - 2).wait()

        stage[step % 2] = cdf + z * (jnp.exp(-0.5 * z * z) * 0.3989422804014327)
        staged(step).start()
        at_step(step, late)
        return 0

    lax.fori_loop(0, NT * CHUNKS, hidden, 0)
    staged(NT * CHUNKS - 2).wait()
    staged(NT * CHUNKS - 1).wait()
    for i in (3, 8, 9):
        save(i).start()
    gain_ref[...] = jnp.zeros_like(gain_ref)
    pool[...] = jnp.zeros_like(pool)

    def second(i, _):
        s = pl.ds(pl.multiple_of(i * ROWS, ROWS), ROWS)
        res = xhat1_ref[s, :] * row_ref[1:2] + row_ref[2:3] + row_ref[3:4]
        for t in range(NT):
            res = res + nt(g_ref[t, s, :], w2[t])
        xhat, rstd = norm(res)
        xhat2_ref[s, :] = xhat
        rstd_ref[s, 1:2] = rstd
        y = xhat * row_ref[4:5] + row_ref[5:6]
        out_ref[s, :] = y.astype(bf16)
        here = i * ROWS + lax.broadcasted_iota(jnp.int32, (ROWS, 1), 0) < length
        pool[0:1] += jnp.sum(jnp.where(here, y, 0.0), axis=0, keepdims=True)
        gain_ref[...] += jnp.sum(jnp.where(here, xhat, 0.0), axis=0, keepdims=True)
        return 0

    lax.fori_loop(0, CHUNKS, second, 0)
    size = jnp.full((1, 1), length).astype(f32)
    mean = pool[0:1] / size
    if comm:
        block = [mean[:, i * 128 : i * 128 + 128] for i in range(D // 128)] + [jnp.zeros((8 - D // 128, 128), f32)]
        every[p.c, pl.ds(pl.multiple_of(((p.z * 2 + p.x) * 2 + p.y) * 8, 8), 8), :] = jnp.concatenate(block, axis=0)
        pools.start()
    save(0).start()
    save(4).start()
    if comm:
        pools.finish()
        for i in range(dp):
            for t in range(NT):
                at = (i * 2 + t // 2) * 8
                for k in range(D // 128):
                    pooled[i * NT + t : i * NT + t + 1, k * 128 : k * 128 + 128] = every[t % 2, at + k : at + k + 1, :]
        for g in parts:
            g.finish()
    else:
        pooled[...] = mean
    for h in range(H):
        for i, (src, dst) in enumerate(kept):
            pltpu.make_async_copy(src.at[h], dst.at[h], q_sem.at[i, h]).wait()
    for i in range(len(saved)):
        save(i).wait()


def forward(length, x, weights, n, cb, comm):
    s = jax.ShapeDtypeStruct
    dp = 2 * n
    r = D // dp
    dma = pltpu.SemaphoreType.DMA
    shapes = [s((LEN, 2), f32), s((1, D), f32), s((16, D), f32), s((NT, 1, D), f32), s((dp * NT if comm else 1, D), f32)]
    big = [s((LEN, D), bf16), s((LEN, D), bf16), s((LEN, D), f32), s((NT, LEN, D), bf16), s((LEN, D), f32), s((D, LEN), bf16), s((D, LEN), bf16)]
    kept = [
        s((NT, LEN, D), f32), s((H, AUG, LEN), bf16), s((H, AUG, LEN), bf16), s((H, HD, LEN), bf16),
        s((NJ, NT, D, 4 * HD), bf16), s((NT, D, D), bf16), s((NT, D, D), bf16),
    ]
    scratch = [pltpu.VMEM(v.shape, v.dtype) for v in big] + [
        pltpu.VMEM((NJ, NT, D, 4 * HD), bf16), pltpu.VMEM((NT, D, D), bf16), pltpu.VMEM((NT, D, D), bf16),
        pltpu.VMEM((NT, dp * 32, 128), bf16), pltpu.VMEM((NT, 2 * HC, 1), f32), pltpu.VMEM((NT, 8, dp * cb), f32),
        pltpu.VMEM((H, AUG, LEN), bf16), pltpu.VMEM((H, AUG, LEN), bf16), pltpu.VMEM((H, HD, LEN), bf16),
        pltpu.VMEM((2, LEN, AUG), bf16), pltpu.VMEM((2, LEN, LEN // 2), f32),
        pltpu.VMEM((D, D), bf16), pltpu.VMEM((8, D), f32), pltpu.VMEM((2, ROWS, D), f32),
        pltpu.VMEM((2, dp * 16, 128), f32),
        dma((PARTS,)), dma((3, H)), dma((2,)), dma((len(big) + 3,)),
    ]
    if comm:
        scratch += gather_sems(PARTS, n) + exchange_sems(n)
        params = pltpu.CompilerParams(collective_id=0, has_side_effects=True, vmem_limit_bytes=VMEM_CAP)
    else:
        params = pltpu.CompilerParams(vmem_limit_bytes=VMEM_CAP)
    return pl.pallas_call(
        functools.partial(forward_kernel, n, cb, comm),
        out_shape=shapes + big + kept,
        in_specs=[pl.BlockSpec(memory_space=pltpu.SMEM)] + vmem_spec(1) + (vmem_spec(6) if comm else any_spec(4)),
        out_specs=vmem_spec(len(shapes)) + any_spec(len(big) + len(kept)),
        scratch_shapes=scratch,
        compiler_params=params,
    )(length, x, *weights)


def backward_kernel(n, cb, comm, *refs):
    dp = 2 * n
    r = D // dp
    (len_ref, pooled_ref, groups_ref, gain_ref, rstd_ref, row_ref,
     xhat2_in, xhat1_in, w1_in, w2_in, wa_in, g_in, gp_in, h1_in, ct_in, xt_in, q_in, k_in, v_in, *refs) = refs
    dx_out, *refs = refs
    outs, refs = refs[: NJ + 3], refs[NJ + 3 :]
    landing, refs = (refs[: NJ + 3], refs[NJ + 3 :]) if comm else ([], refs)
    (wa, w1, w2, t2, dqkv, xt, df, dz, dh, sd, pp, turned, qkv, wcat, grow, ghb, gcol, gbias,
     load, s_load, q_sem, x_sem, *refs) = refs
    length = len_ref[lax.axis_index("tensor")]
    hooks, after, ends = {}, {}, [[]] * 6
    grads = [wa.at[j] for j in range(NJ)]
    h1t = dat = dqkv.at[1]
    ct = dqkv.at[2]
    dft = dct = t2
    folded = [df.at[0:D, :], dz.at[0:D, :], wcat]

    loads = [
        pltpu.make_async_copy(src, dst, load.at[i])
        for i, (src, dst) in enumerate(
            ((xhat2_in, sd.at[1, :, 0:D]), (w2_in, w2), (h1_in, dz), (w1_in, w1), (wa_in, wa), (ct_in, ct), (xt_in, xt))
        )
    ]

    def fetch(step):
        t = part_of(step)
        return [
            pltpu.make_async_copy(src.at[t], dst.at[step % 2, :, 0:D], s_load.at[step % 2, i])
            for i, (src, dst) in enumerate(((g_in, pp), (gp_in, sd)))
        ]

    if comm:
        p = Place(n)

        def part_of(step):
            y = jnp.where(step < 2, 1 - p.y, p.y)
            return y * 2 + jnp.where(step % 2 == 0, 1 - p.c, p.c)
    else:

        def part_of(step):
            return step

    for cp in loads[:2]:
        cp.start()
    for cp in fetch(0):
        cp.start()
    for cp in loads[2:]:
        cp.start()
    if comm:
        temp, *refs = refs
        bufs, sems = refs[:-8], refs[-8:]
        count = greet(p)
        where = [(lambda t: w1.at[t]), (lambda t: w2.at[t])] + [(lambda t, g=g: g.at[t]) for g in grads] + [lambda t: gbias.at[t]]
        parts = []
        for i, source in enumerate(where):
            rows, width = outs[i].shape
            parts.append(
                Scatter(p, i, rows, source, outs[i], [landing[i]] + list(bufs[3 * i : 3 * i + 3]),
                        temp.at[0 : 2 * n * rows, 0:width], x_sem.at[0], sems)
            )
        flows = [part.flow(i < 2) for i, part in enumerate(parts)]

        def steps(pairs):
            return [flows[g][k] for g, k in pairs]

        if n == 4:
            plan = {slot: steps(pairs) for slot, pairs in BACK.items()}
        else:
            plan = {1: steps([(g, k) for g in range(2) for k in range(4)]), 3: steps([(g, k) for g in range(2) for k in range(4, 7)])}
            plan[6] = [step for flow in flows[:2] for step in flow[7:]]
            for j in range(NJ):
                plan[7 + j * NT + NT - 1] = flows[2 + j]
            plan[7 + H] = flows[-1]
        after = {k: plan.get(k, []) for k in range(NT)}
        hooks = {h: plan.get(7 + h, []) for h in range(H)}
        ends = [plan.get(k, []) for k in (5, 6, 7 + H, 8 + H, 9 + H, 10 + H)]

    size = jnp.full((1, 1), length).astype(f32)
    u = loss_pull(pooled_ref[...], groups_ref[...], lax.axis_index("dp") * NT + lax.axis_index("tensor")) / size
    du = u * row_ref[4:5]
    mean_du = jnp.mean(du, axis=1, keepdims=True)
    grow[...] = jnp.zeros_like(grow)
    loads[0].wait()

    def outer(i, _):
        s = pl.ds(pl.multiple_of(i * ROWS, ROWS), ROWS)
        here = i * ROWS + lax.broadcasted_iota(jnp.int32, (ROWS, 1), 0) < length
        hat = sd[1, s, 0:D]
        dot = jnp.mean(hat * du, axis=1, keepdims=True)
        dr = jnp.where(here, rstd_ref[s, 1:2] * (du - mean_du - hat * dot), 0.0)
        dh[s, :] = dr
        low = dr.astype(bf16)
        df[s, :] = low
        grow[3:4] += jnp.sum(low.astype(f32), axis=0, keepdims=True)
        return 0

    lax.fori_loop(0, CHUNKS, outer, 0)
    if comm:
        enter(count)
    grow[4:5] = u * gain_ref[...]
    grow[5:6] = u * size
    dft[...] = df[...].T
    loads[2].wait()
    h1t[...] = dz[...].T
    last_hat = pltpu.make_async_copy(xhat1_in, sd.at[0, :, 0:D], load.at[0])
    loads[1].wait()
    loads[3].wait()

    def hidden(step, _):
        t = part_of(step)
        slot = step % 2
        for cp in fetch(step):
            cp.wait()

        @pl.when(step + 1 < NT)
        def _():
            for cp in fetch(step + 1):
                cp.start()

        hb = jnp.zeros((1, D), f32)
        for i in range(CHUNKS):
            s = pl.ds(i * ROWS, ROWS)
            low = (nn(df[s, :], w2[t]) * sd[slot, s, 0:D]).astype(bf16)
            dz[s, :] = low
            hb = hb + jnp.sum(low.astype(f32), axis=0, keepdims=True)
            dh[s, :] += nt(low, w1[t])
        ghb[t] = hb
        for i in range(D // ROWS):
            s = slice(i * ROWS, (i + 1) * ROWS)
            w1[t, s, :] = nn(h1t[s, :], dz[...]).astype(bf16)
            w2[t, s, :] = nn(dft[s, :], pp[slot, :, 0:D]).astype(bf16)
        pl.when(step == NT - 2)(last_hat.start)
        at_step(step, after)
        return 0

    lax.fori_loop(0, NT, hidden, 0)

    def fetch_head(h, slot):
        return [
            pltpu.make_async_copy(src.at[h], qkv.at[slot, i, 0 : src.shape[1], :], q_sem.at[slot, i])
            for i, src in enumerate((q_in, k_in, v_in))
        ]

    for cp in fetch_head(0, 0):
        cp.start()
    last_hat.wait()

    def inner_norm(i, _):
        s = pl.ds(pl.multiple_of(i * ROWS, ROWS), ROWS)
        d = dh[s, :]
        hat = sd[0, s, 0:D]
        grow[1:2] += jnp.sum(d * hat, axis=0, keepdims=True)
        grow[2:3] += jnp.sum(d, axis=0, keepdims=True)
        dn = d * row_ref[1:2]
        dr = rstd_ref[s, 0:1] * (dn - jnp.mean(dn, axis=1, keepdims=True) - hat * jnp.mean(dn * hat, axis=1, keepdims=True))
        dh[s, :] = dr
        low = dr.astype(bf16)
        grow[0:1] += jnp.sum(low.astype(f32), axis=0, keepdims=True)
        df[s, :] = low
        return 0

    lax.fori_loop(0, CHUNKS, inner_norm, 0)
    dat[...] = df[...].T
    run(ends[0])
    loads[4].wait()
    loads[5].wait()
    for j in range(NJ):
        for t in range(NT):
            h = j * NT + t
            wcat[:, h * HD : h * HD + HD] = wa[j, t, :, 3 * HD : 4 * HD]
    for i in range(D // ROWS):
        s = slice(i * ROWS, (i + 1) * ROWS)
        dct[s, :] = tn(wcat[:, s], dat[...]).astype(bf16)
        gwo = nt(dat[s, :], ct[...]).astype(bf16)
        for j in range(NJ):
            for t in range(NT):
                h = j * NT + t
                wa[j, t, s, 3 * HD : 4 * HD] = gwo[:, h * HD : h * HD + HD]
    loads[6].wait()
    run(ends[1])

    def head(h, _):
        j, t = h // NT, h % NT
        slot = h % 2
        for cp in fetch_head(h, slot):
            cp.wait()

        @pl.when(h + 1 < H)
        def _():
            for cp in fetch_head(h + 1, 1 - slot):
                cp.start()

        own = pl.ds(pl.multiple_of(h * HD, HD), HD)
        prob = jnp.exp(tn(qkv[slot, 0], qkv[slot, 1]))
        sd[0] = prob
        sd[1] = tn(dct[own, :], qkv[slot, 2, 0:HD, :])
        pp[0] = prob.astype(bf16)
        inner = jnp.sum(sd[0] * sd[1], axis=1, keepdims=True)
        pp[1] = (sd[0] * (sd[1] - inner)).astype(bf16)
        turned[...] = pp[1].T
        at = pl.multiple_of(t * 3 * HD, HD)
        dqkv[j, pl.ds(at + HD, HD), :] = nn(qkv[slot, 0, 0:HD, :], pp[1]).astype(bf16)
        dqkv[j, pl.ds(at + 2 * HD, HD), :] = nn(dct[own, :], pp[0]).astype(bf16)
        dqkv[j, pl.ds(at, HD), :] = (nn(qkv[slot, 1, 0:HD, :], turned[...]) * HD**-0.5).astype(bf16)

        @pl.when(t == NT - 1)
        def _():
            for i in range(NJ):

                @pl.when(j == i)
                def _(i=i):
                    for k in range(NT):
                        folded[i][:, k * 3 * HD : (k + 1) * 3 * HD] = wa[i, k, :, 0 : 3 * HD]

            sums = nt(jnp.ones((16, LEN), bf16), dqkv[j])
            for k in range(NT):
                gcol[j, k] = sums[0:8, k * 3 * HD : (k + 1) * 3 * HD]
            for i in range(D // ROWS):
                s = slice(i * ROWS, (i + 1) * ROWS)
                g = nt(xt[s, :], dqkv[j]).astype(bf16)
                for k in range(NT):
                    wa[j, k, s, 0 : 3 * HD] = g[:, k * 3 * HD : (k + 1) * 3 * HD]

        at_step(h, hooks)
        return 0

    lax.fori_loop(0, H, head, 0)

    col_rows = -(-cb // r)
    cols = []
    for t in range(NT):
        pieces = [gcol[j, t, 0:1, 0:HD] for j in range(NJ)] + [gcol[j, t, 0:1, 2 * HD : 3 * HD] for j in range(NJ)]
        cols.append(jnp.concatenate(pieces + [ghb[t]], axis=1))
    at = lax.broadcasted_iota(jnp.int32, (32, 128), 0)
    for i in range(dp):
        rows = jnp.pad(grow[0:8, i * r : i * r + r], ((0, 24), (0, 128 - r)))
        for t in range(NT):
            block = jnp.where(at < 6, rows, 0.0)
            for k in range(col_rows):
                wide = min(r, cb - k * r)
                piece = cols[t][:, i * cb + k * r : i * cb + k * r + wide]
                block = jnp.where(at == 6 + k, jnp.pad(piece, ((0, 0), (0, 128 - wide))), block)
            gbias[t, i * 32 : i * 32 + 32, :] = block.astype(bf16)
    run(ends[2])
    for j in range(NJ):
        for i in range(CHUNKS):
            s = slice(i * ROWS, (i + 1) * ROWS)
            dh[s, :] += lax.dot_general(dqkv[j, :, s], folded[j][...], (((0,), (1,)), ((), ())), preferred_element_type=f32)
        if j == NJ - 1:
            dx = pltpu.make_async_copy(dh, dx_out, load.at[0])
            dx.start()
        run(ends[3 + j])
    if comm:
        for part in parts:
            part.finish()
    else:
        copies = [pltpu.make_async_copy(src, dst, load.at[1 + i]) for i, (src, dst) in enumerate(zip([w1, w2] + grads + [gbias], outs))]
        for cp in copies:
            cp.start()
        for cp in copies:
            cp.wait()
    dx.wait()


def backward(length, pooled, groups, gain, rstd, row, big, n, cb, comm):
    s = jax.ShapeDtypeStruct
    dp = 2 * n
    r = D // dp
    dma = pltpu.SemaphoreType.DMA
    widths = [(r, D), (r, D)] + [(r, 4 * HD)] * NJ + [(32, 128)]
    if comm:
        sums = [s(shape, f32) for shape in widths]
        landing = [s((2, dp * rows, wide), bf16) for rows, wide in widths]
        specs = vmem_spec(len(sums)) + any_spec(len(landing))
    else:
        sums = [s((NT, dp * rows, wide), bf16) for rows, wide in widths]
        landing = []
        specs = any_spec(len(sums))
    turned = pltpu.VMEM((D, LEN), bf16)
    rows_low = pltpu.VMEM((LEN, D), bf16)
    rows_full = pltpu.VMEM((LEN, D), f32)
    scratch = [
        pltpu.VMEM((NJ, NT, D, 4 * HD), bf16), pltpu.VMEM((NT, D, D), bf16), pltpu.VMEM((NT, D, D), bf16),
        turned, pltpu.VMEM((NJ, D, LEN), bf16), turned, rows_low, rows_low, rows_full,
        pltpu.VMEM((2, LEN, LEN), f32), pltpu.VMEM((2, LEN, LEN), bf16), pltpu.VMEM((LEN, LEN), bf16), pltpu.VMEM((2, 3, AUG, LEN), bf16), pltpu.VMEM((D, D), bf16),
        pltpu.VMEM((16, D), f32), pltpu.VMEM((NT, 1, D), f32), pltpu.VMEM((NJ, NT, 8, 3 * HD), f32), pltpu.VMEM((NT, dp * 32, 128), bf16),
        dma((8,)), dma((2, 2)), dma((2, 3)), dma((1,)),
    ]
    if comm:
        scratch += [pltpu.VMEM((D, D), bf16)]
        for rows, wide in widths:
            scratch += scatter_bufs(n, rows, wide)
        scratch += scatter_sems(len(widths), n)
        params = pltpu.CompilerParams(collective_id=1, has_side_effects=True, vmem_limit_bytes=VMEM_CAP)
    else:
        params = pltpu.CompilerParams(vmem_limit_bytes=VMEM_CAP)
    return pl.pallas_call(
        functools.partial(backward_kernel, n, cb, comm),
        out_shape=[s((LEN, D), f32)] + sums + landing,
        in_specs=[pl.BlockSpec(memory_space=pltpu.SMEM)] + vmem_spec(5) + any_spec(len(big)),
        out_specs=any_spec(1) + specs,
        scratch_shapes=scratch,
        compiler_params=params,
    )(length, pooled, groups, gain, rstd, row, *big)


def adam_kernel(cb, *refs):
    ins, outs, refs = refs[:32], refs[32:58], refs[58:]
    held, new, sem_in, sem_out = refs[:32], refs[32:56], refs[56], refs[57]
    inward = [pltpu.make_async_copy(src, dst, sem_in.at[i]) for i, (src, dst) in enumerate(zip(ins, held))]
    outward = [pltpu.make_async_copy(src, dst, sem_out.at[i]) for i, (src, dst) in enumerate(zip((*held[:2], *new), outs))]
    for cp in inward:
        cp.start()
    moved, sums, old = held[:2], held[2:8], held[8:]
    gw1, gw2, ga, gbias = sums[0], sums[1], sums[2:5], sums[5]
    r = gw1.shape[0]

    def wide(k):
        return jnp.concatenate([ga[j][:, k * HD : k * HD + HD] for j in range(NJ)], axis=1)

    def group(i):
        for k in range(4):
            inward[8 + 4 * i + k].wait()

    def update(i, grad, rate, at=()):
        where = at + (Ellipsis,)
        out = adam_update(*[old[4 * i + k][where] for k in range(4)], grad, rate)
        for k, v in enumerate(out):
            new[4 * i + k][where] = v

    def leave(*at):
        for i in at:
            outward[i].start()

    for i in range(2):
        inward[i].wait()
    leave(0, 1)
    for i in range(2, 8):
        inward[i].wait()
    group(0)
    for k in range(3):
        update(0, wide(k), D ** (-0.5), (k,))
    leave(2, 3, 4, 5)
    group(2)
    update(2, gw1[...], D ** (-0.5))
    leave(10, 11, 12, 13)
    group(3)
    update(3, gw2[...], FF ** (-0.5))
    leave(14, 15, 16, 17)
    high = -(-r // 128) * 128
    turned = jnp.concatenate([wide(3), jnp.zeros((r, 256 - HC), f32)], axis=1)
    if high > r:
        turned = jnp.concatenate([turned, jnp.zeros((high - r, 256), f32)], axis=0)
    group(1)
    update(1, turned.T[0:HC, 0:r], D ** (-0.5))
    leave(6, 7, 8, 9)
    group(4)
    rows = gbias[...]
    pieces = [rows[6 + k : 7 + k, 0 : min(r, cb - k * r)] for k in range(-(-cb // r))]
    update(4, jnp.concatenate(pieces, axis=1), 0.1)
    group(5)
    update(5, rows[0:6, 0:r], 0.15)
    leave(*range(18, 26))
    for cp in outward:
        cp.wait()


def adam(moved, sums, olds, cb):
    flat = [v for group in olds for v in group]
    s = jax.ShapeDtypeStruct
    shapes = [s(group[0].shape, f32) for group in olds for _ in range(4)]
    ins = [*moved, *sums, *flat]
    return pl.pallas_call(
        functools.partial(adam_kernel, cb),
        out_shape=[s(v.shape, v.dtype) for v in moved] + shapes,
        in_specs=any_spec(32),
        out_specs=any_spec(26),
        scratch_shapes=[pltpu.VMEM(v.shape, v.dtype) for v in ins + shapes] + [pltpu.SemaphoreType.DMA((32,)), pltpu.SemaphoreType.DMA((26,))],
        compiler_params=pltpu.CompilerParams(vmem_limit_bytes=VMEM_CAP),
    )(*ins)


def gather_plain(own):
    return lax.all_gather(lax.all_gather(own, "dp", axis=0, tiled=True), "tensor", axis=0)


def scatter_plain(full):
    own = lax.psum_scatter(full.astype(f32), "tensor", scatter_dimension=0, tiled=False)
    return lax.psum_scatter(own, "dp", scatter_dimension=0, tiled=True)


def by_head(wide):
    return jnp.moveaxis(wide.reshape(*wide.shape[:-1], NJ, HD), -2, 0)


def packed(qkv_weight, out_weight, up_weight, down_weight, col_bias, row_params, r, cb):
    own_a = jnp.concatenate([by_head(qkv_weight[i]) for i in range(3)] + [by_head(out_weight.T)], axis=-1).astype(bf16)
    col_rows = -(-cb // r)
    col_pad = jnp.pad(col_bias[0], (0, col_rows * r - cb)).reshape(col_rows, r)
    own_b = jnp.pad(jnp.concatenate([row_params, col_pad], axis=0), ((0, 26 - col_rows), (0, 128 - r))).astype(bf16)
    return own_a, own_b, up_weight.astype(bf16), down_weight.T.astype(bf16)


def on_device(
    inputs, lengths, groups, qkv_weight, out_weight, up_weight, down_weight, col_bias, row_params,
    qkv_first, out_first, up_first, down_first, col_first, row_first,
    qkv_second, out_second, up_second, down_second, col_second, row_second,
    qkv_ema, out_ema, up_ema, down_ema, col_ema, row_ema,
):
    dp = lax.axis_size("dp")
    n = dp // 2
    r = D // dp
    cb = col_bias.shape[1]
    comm = r % 32 == 0
    if comm:
        weights = (qkv_weight, out_weight, up_weight, down_weight.T, col_bias, row_params)
    else:
        own_a, *others = packed(qkv_weight, out_weight, up_weight, down_weight, col_bias, row_params, r, cb)
        own_b, own_1, own_2 = [gather_plain(v) for v in others]
        weights = (jnp.stack([gather_plain(own_a[j]) for j in range(NJ)]), own_b, own_1, own_2)
    (rstd, gain, row, hb, pooled, outputs, h1, xhat1, g, xhat2, ct, xt, gp, qt, kt, vt, wa, w1, w2) = forward(
        lengths, inputs, weights, n, cb, comm
    )
    if not comm:
        pooled = lax.all_gather(pooled, ("dp", "tensor"), axis=0, tiled=True)
    big = (xhat2, xhat1, w1, w2, wa, g, gp, h1, ct, xt, qt, kt, vt)
    input_grad, *sums = backward(lengths, pooled, groups, gain, rstd, row, big, n, cb, comm)
    sums = sums[: NJ + 3] if comm else [scatter_plain(v) for v in sums]
    olds = (
        (qkv_weight, qkv_first, qkv_second, qkv_ema),
        (out_weight, out_first, out_second, out_ema),
        (up_weight, up_first, up_second, up_ema),
        (down_weight.T, down_first.T, down_second.T, down_ema.T),
        (col_bias, col_first, col_second, col_ema),
        (row_params, row_first, row_second, row_ema),
    )
    outputs, input_grad, *new = adam((outputs, input_grad), sums, olds, cb)
    new[12:16] = [v.T for v in new[12:16]]
    return (outputs, input_grad, *new)


def solution(mesh):
    tokens = P(("dp", "tensor"), None)
    placed = (P(None, "dp", "tensor"), P("tensor", "dp"), P("dp", "tensor"), P("tensor", "dp"), P("tensor", "dp"), P(None, "dp"))
    new = tuple(spec for spec in placed for _ in range(4))
    return jax.shard_map(
        on_device,
        mesh=mesh,
        in_specs=(tokens, P("dp"), P()) + placed * 4,
        out_specs=(tokens, tokens) + new,
        check_vma=False,
    )
```
